32 devices in a mesh: seq: 8 (over z, core), dp: 4 (over y, x).
Axes of the slice: x: 2, y: 2, z: 4, core: 2. Of those that a mesh axis runs over, the one named last changes fastest.
Arguments:
- tokens: bfloat16 [2, 4, 1024, 2048], P(None, 'dp', 'seq'), may hold values from -6 to 6
- doc_ends: int32 [2, 4, 18], P(None, 'dp'), may hold values from 60 to 1024, as said below
- input_gain: bfloat16 [2048], P(('seq', 'dp')), may hold values from 0.5 to 1.5
- mixer_in: bfloat16 [2048, 6704], P(('seq', 'dp')), may hold values from -0.125 to 0.125
- conv_weight: bfloat16 [4, 3584], P(None, ('seq', 'dp')), may hold values from -3 to 3
- conv_bias: bfloat16 [3584], P(('seq', 'dp')), may hold values from -2 to 2
- head_params: float32 [3, 48], replicated, may hold values from -8.2 to 1.5, as said below
- mixer_gain: bfloat16 [3072], P(('seq', 'dp')), may hold values from 0.5 to 1.5
- mixer_out: bfloat16 [3072, 2048], P(('seq', 'dp')), may hold values from -0.109375 to 0.109375
- attn_qkv: bfloat16 [2048, 1536], P(('seq', 'dp')), may hold values from -0.125 to 0.125
- attn_out: bfloat16 [1024, 2048], P(('seq', 'dp')), may hold values from -1 to 1
- ffn_gain: bfloat16 [2048], P(('seq', 'dp')), may hold values from 0.5 to 1.5
- gate_up: bfloat16 [2048, 8192], P(('seq', 'dp')), may hold values from -0.125 to 0.125
- down_proj: bfloat16 [4096, 2048], P(('seq', 'dp')), may hold values from -0.09375 to 0.09375
- out_grad: bfloat16 [2, 4, 1024, 2048], P(None, 'dp', 'seq'), may hold values from -6 to 6
Outputs:
- layer_out: bfloat16 [2, 4, 1024, 2048], P(None, 'dp', 'seq')
- token_grad: float32 [2, 4, 1024, 2048], P(None, 'dp', 'seq')
- input_gain_grad: float32 [2048], P(('seq', 'dp'))
- mixer_in_grad: float32 [2048, 6704], P(('seq', 'dp'))
- conv_weight_grad: float32 [4, 3584], P(None, ('seq', 'dp'))
- conv_bias_grad: float32 [3584], P(('seq', 'dp'))
- head_params_grad: float32 [3, 48], replicated
- mixer_gain_grad: float32 [3072], P(('seq', 'dp'))
- mixer_out_grad: float32 [3072, 2048], P(('seq', 'dp'))
- attn_qkv_grad: float32 [2048, 1536], P(('seq', 'dp'))
- attn_out_grad: float32 [1024, 2048], P(('seq', 'dp'))
- ffn_gain_grad: float32 [2048], P(('seq', 'dp'))
- gate_up_grad: float32 [2048, 8192], P(('seq', 'dp'))
- down_proj_grad: float32 [4096, 2048], P(('seq', 'dp'))
The draws below stay inside these ranges and needn't reach their ends.
Inputs may be any that keep to these rules, and one draw needn't show every extreme that they name: `doc_ends`: Non-decreasing along the last dimension; the last entry is 1024. For each index of dp, one of its 2 sequences, chosen at random, is one document of 1024 tokens; in the others documents have 60 to 800 tokens, the last one of a sequence possibly fewer, and unused slots hold 1024. `head_params`: row 0 holds logarithms of positive decay rates, row 1 time-step biases, row 2 skip weights.
All inputs are finite; a program needn't handle non-finite values.
Results may differ from the reference program's by a relative error of at most 0.015.
Values may be sent and summed in bfloat16 or wider, within the bound.
No kernel may reach another device: no remote copies, remote signals or barrier semaphores. Data moves between devices by JAX's collectives and lax.ppermute only.
A program may use at most 512 MiB of HBM per device.

```python
from functools import partial
import jax
import jax.numpy as jnp
from jax import lax

D = 2048
FF = 4096
HEADS = 48
HEAD_DIM = 64
STATE = 256
CONV = 4
ATT_HEADS = 8
KV_HEADS = 2
ATT_DIM = 128
SEQ_DEV = 128
MICRO = 2
DOC_MIN = 60
DOC_MAX = 800
INNER = 3072
CONVCH = 3584
PROJ = 6704
ATT_INNER = 1024
QKV = 1536
LENGTH = 1024
SEQS = 4
DOCS = 18


def draw_doc_ends(key, part):
    key = jax.random.fold_in(key, 7)
    length_key, pick_key = jax.random.split(key)
    lengths = jax.random.randint(length_key, (MICRO, SEQS, DOCS), DOC_MIN, DOC_MAX + 1, dtype=jnp.int32)
    end_points = jnp.minimum(jnp.cumsum(lengths, axis=-1), LENGTH)
    chosen = jax.random.randint(pick_key, (SEQS,), 0, MICRO, dtype=jnp.int32)
    single = jnp.arange(MICRO, dtype=jnp.int32)[:, None] == chosen[None, :]
    return jnp.where(single[:, :, None], LENGTH, end_points).astype(jnp.int32)


def draw_head_params(key, part):
    key = jax.random.fold_in(key, 11)
    rate_key, bias_key, skip_key = jax.random.split(key, 3)
    log_rate = jax.random.uniform(rate_key, (HEADS,), jnp.float32, jnp.log(0.001), jnp.log(0.08))
    step_bias = jax.random.uniform(bias_key, (HEADS,), jnp.float32, -1.5, 0.5)
    skip_weight = jax.random.uniform(skip_key, (HEADS,), jnp.float32, 0.5, 1.5)
    return jnp.stack([log_rate, step_bias, skip_weight], axis=0)


def steps_of(own_key, dims, cuts, smallest, top_value):
    factor_of, own = 1.0, jax.random.fold_in(own_key, 6)
    for dim, blocks in cuts:
        heights = jnp.exp(jax.random.uniform(jax.random.fold_in(own, dim), (blocks,), jnp.float32, smallest / len(cuts), top_value / len(cuts)))
        factor_of = factor_of * jnp.repeat(heights, dims[dim] // blocks).reshape([-1 if axis == dim else 1 for axis in range(len(dims))])
    return factor_of


def gaussian(stream_key, shape, deviation, bound, cuts=(), kind=jnp.bfloat16):
    array = deviation * jax.random.normal(stream_key, shape, jnp.float32)
    if cuts:
        array = array * steps_of(stream_key, shape, cuts, -0.22, 0.18)
    return jnp.clip(array, -bound, bound).astype(kind)


def setup_inputs(seed: int = 0) -> dict:
    seeds = jax.random.split(jax.random.key(seed), 16)
    return {
        "tokens": gaussian(seeds[0], (MICRO, SEQS, LENGTH, D), 1.0, 6.0, ((1, 4), (2, 8))),
        "doc_ends": draw_doc_ends(jax.random.fold_in(seeds[15], 71), 0),
        "input_gain": jnp.clip(1.0 + 0.1 * jax.random.normal(seeds[2], (D,), jnp.float32), 0.5, 1.5).astype(jnp.bfloat16),
        "mixer_in": gaussian(seeds[3], (D, PROJ), D ** -0.5, 0.125, ((0, 32),)),
        "conv_weight": gaussian(seeds[4], (CONV, CONVCH), CONV ** -0.5, 3.0, ((1, 32),)),
        "conv_bias": gaussian(seeds[5], (CONVCH,), 0.3, 2.0, ((0, 32),)),
        "head_params": draw_head_params(jax.random.fold_in(seeds[15], 71), 0),
        "mixer_gain": jnp.clip(1.0 + 0.1 * jax.random.normal(seeds[7], (INNER,), jnp.float32), 0.5, 1.5).astype(jnp.bfloat16),
        "mixer_out": gaussian(seeds[8], (INNER, D), INNER ** -0.5, 0.109375, ((0, 32),)),
        "attn_qkv": gaussian(seeds[9], (D, QKV), D ** -0.5, 0.125, ((0, 32),)),
        "attn_out": gaussian(seeds[10], (ATT_INNER, D), (ATT_INNER // 32) ** -0.5, 1.0, ((0, 32),)),
        "ffn_gain": jnp.clip(1.0 + 0.1 * jax.random.normal(seeds[11], (D,), jnp.float32), 0.5, 1.5).astype(jnp.bfloat16),
        "gate_up": gaussian(seeds[12], (D, 2 * FF), D ** -0.5, 0.125, ((0, 32),)),
        "down_proj": gaussian(seeds[13], (FF, D), FF ** -0.5, 0.09375, ((0, 32),)),
        "out_grad": gaussian(seeds[14], (MICRO, SEQS, LENGTH, D), 1.0, 6.0, ((1, 4), (2, 8))),
    }


epsilon = 1e-05
rope_base = 10000.0
highest = lax.Precision.HIGHEST

@jax.custom_vjp
def low(v):
    return lax.optimization_barrier(v.astype(jnp.bfloat16)).astype(jnp.float32)

@jax.custom_vjp
def low_back(v):
    return v

def low_keep(v):
    return (low(v), None)

def low_pass(kept, grad):
    return (grad,)

def back_keep(v):
    return (v, None)

def back_low(kept, grad):
    return (low(grad),)
low.defvjp(low_keep, low_pass)
low_back.defvjp(back_keep, back_low)

def matmul(left, right):
    return jnp.dot(left, right, precision=highest, preferred_element_type=jnp.float32)

def rms_scale(values, gain):
    return values * lax.rsqrt(lax.optimization_barrier(jnp.mean(values * values, axis=-1, keepdims=True)) + epsilon) * gain

def segment_of(positions, end_points):
    counted = lax.optimization_barrier(jnp.sum((end_points[None, :] <= positions[:, None]).astype(jnp.int32), axis=1))
    return jnp.where(positions < 0, -1, counted).astype(jnp.int32)

def rope_tables(positions, head_width):
    half_width = head_width // 2
    freqs = jnp.power(rope_base, -jnp.arange(half_width, dtype=jnp.float32) * (2.0 / head_width))
    angles = positions.astype(jnp.float32)[:, None] * freqs[None, :]
    return (jnp.concatenate([jnp.cos(angles), jnp.cos(angles)], axis=1), jnp.concatenate([jnp.sin(angles), jnp.sin(angles)], axis=1))

def rotate_half(values, cosine, sine):
    half_width = values.shape[-1] // 2
    turned = jnp.concatenate([-values[..., half_width:], values[..., :half_width]], axis=-1)
    return values * cosine[:, None, :] + turned * sine[:, None, :]

def attention_prep(qkv_rows, cosine, sine):
    row_count = qkv_rows.shape[0]
    query_width = ATT_HEADS * ATT_DIM
    key_width = KV_HEADS * ATT_DIM
    queries = rotate_half(qkv_rows[:, :query_width].reshape(row_count, ATT_HEADS, ATT_DIM), cosine, sine)
    keys = rotate_half(qkv_rows[:, query_width:query_width + key_width].reshape(row_count, KV_HEADS, ATT_DIM), cosine, sine)
    values = qkv_rows[:, query_width + key_width:].reshape(row_count, KV_HEADS, ATT_DIM)
    return (queries, keys, values)

def tap_masks(seg_ext, row_count, kernel):
    own_segment = seg_ext[kernel - 1:]
    return jnp.stack([(seg_ext[offset:offset + row_count] == own_segment).astype(jnp.float32) for offset in range(kernel)], axis=1)

def conv_part(extended, dt_raw, conv_weight, conv_bias, head_params, taps):
    row_count = dt_raw.shape[0]
    total = conv_bias[None, :]
    for offset in range(conv_weight.shape[0]):
        total = total + extended[offset:offset + row_count] * conv_weight[offset][None, :] * taps[:, offset:offset + 1]
    conv_out = jax.nn.silu(total)
    step_size = jax.nn.softplus(dt_raw + head_params[1][None, :])
    log_decay = -jnp.exp(head_params[0])[None, :] * step_size
    return (conv_out, step_size, log_decay)

def block_masks(seg_here, seg_before):
    row_count = seg_here.shape[0]
    order = jnp.arange(row_count, dtype=jnp.int32)
    within = ((order[None, :] <= order[:, None]) & (seg_here[:, None] == seg_here[None, :])).astype(jnp.float32)
    entering = (seg_here == seg_before).astype(jnp.float32)
    trailing = (seg_here == seg_here[row_count - 1]).astype(jnp.float32)
    passing = (seg_here[row_count - 1] == seg_before).astype(jnp.float32)
    return (within, entering, trailing, passing)

def block_output(conv_out, step_size, log_cum, head_params, state_in, within, entering, inner):
    row_count, head_count = step_size.shape
    state_width = (conv_out.shape[1] - inner) // 2
    head_inputs = conv_out[:, :inner].reshape(row_count, head_count, inner // head_count)
    input_proj = conv_out[:, inner:inner + state_width]
    output_proj = conv_out[:, inner + state_width:]
    intersection = jnp.dot(output_proj, input_proj.T, precision=highest)
    gap_log = log_cum[:, None, :] - log_cum[None, :, :]
    mask_cube = within[:, :, None]
    mixing = intersection[:, :, None] * jnp.exp(jnp.where(mask_cube > 0, gap_log, 0.0)) * mask_cube * step_size[None, :, :]
    outputs = jnp.einsum('tsh,shp->thp', mixing, head_inputs, precision=highest)
    carried = jnp.einsum('tn,hpn->thp', output_proj, state_in, precision=highest)
    outputs = outputs + carried * (jnp.exp(log_cum) * entering[:, None])[:, :, None]
    outputs = outputs + head_params[2][None, :, None] * head_inputs
    return outputs.reshape(row_count, inner)

def block_state(conv_out, step_size, log_cum, trailing, passing, inner):
    row_count, head_count = step_size.shape
    state_width = (conv_out.shape[1] - inner) // 2
    head_inputs = conv_out[:, :inner].reshape(row_count, head_count, inner // head_count)
    input_proj = conv_out[:, inner:inner + state_width]
    last_log = log_cum[row_count - 1]
    keeping = jnp.exp(last_log[None, :] - log_cum) * trailing[:, None] * step_size
    scaled = head_inputs * keeping[:, :, None]
    states = jnp.einsum('shp,sn->hpn', scaled, input_proj, precision=highest)
    return (jnp.exp(last_log) * passing, states)

def ssd_block(state_in, pieces, head_params):
    conv_out, step_size, log_cum, seg_here, seg_before = pieces
    within, entering, trailing, passing = block_masks(seg_here, seg_before)
    outputs = block_output(conv_out, step_size, log_cum, head_params, state_in, within, entering, INNER)
    passed, states = block_state(conv_out, step_size, log_cum, trailing, passing, INNER)
    return (passed[:, None, None] * state_in + states, outputs)

def swiglu(gate_vals):
    half_width = gate_vals.shape[1] // 2
    return jax.nn.silu(gate_vals[:, :half_width]) * gate_vals[:, half_width:]

def sequence_layer(weights, token_rows, end_points):
    input_gain, mixer_in, conv_weight, conv_bias, head_params, mixer_gain, mixer_out, attn_qkv, attn_out, ffn_gain, gate_up, down_proj = weights
    kernel = conv_weight.shape[0]
    positions = jnp.arange(LENGTH, dtype=jnp.int32)
    segments = segment_of(positions, end_points)
    normed_in = low(rms_scale(token_rows, input_gain))
    mixed = low_back(matmul(normed_in, mixer_in))
    gate_z = mixed[:, :INNER]
    conv_in = low(mixed[:, INNER:2 * INNER + 2 * STATE])
    dt_raw = mixed[:, 2 * INNER + 2 * STATE:]
    seg_ext = segment_of(jnp.arange(1 - kernel, LENGTH, dtype=jnp.int32), end_points)
    extended = jnp.concatenate([jnp.zeros((kernel - 1, conv_in.shape[1]), jnp.float32), conv_in], axis=0)
    conv_out, step_size, log_decay = conv_part(extended, dt_raw, conv_weight, conv_bias, head_params, tap_masks(seg_ext, LENGTH, kernel))
    block_count = LENGTH // SEQ_DEV
    log_cum = jnp.cumsum(log_decay.reshape(block_count, SEQ_DEV, HEADS), axis=1)
    seg_blocks = segments.reshape(block_count, SEQ_DEV)
    seg_prior = jnp.concatenate([jnp.full((1,), -1, jnp.int32), seg_blocks[:-1, SEQ_DEV - 1]]).astype(jnp.int32)
    step_fn = jax.checkpoint(partial(ssd_block, head_params=head_params))
    zero_state = jnp.zeros((HEADS, HEAD_DIM, STATE), jnp.float32)
    pieces = (conv_out.reshape(block_count, SEQ_DEV, -1), step_size.reshape(block_count, SEQ_DEV, HEADS), log_cum, seg_blocks, seg_prior)
    final_state, outputs = lax.scan(step_fn, zero_state, pieces)
    gated = outputs.reshape(LENGTH, INNER) * jax.nn.silu(gate_z)
    mixer_normed = low(rms_scale(gated, mixer_gain))
    mixer_branch = low_back(matmul(mixer_normed, mixer_out))
    qkv_rows = low_back(matmul(normed_in, attn_qkv))
    cosine, sine = rope_tables(positions, ATT_DIM)
    queries, keys, values = attention_prep(qkv_rows, cosine, sine)
    queries = low(queries)
    keys = low(keys)
    values = low(values)
    repeat = ATT_HEADS // KV_HEADS
    grouped = queries.reshape(LENGTH, KV_HEADS, repeat, ATT_DIM).transpose(1, 2, 0, 3)
    key_heads = keys.transpose(1, 0, 2)
    value_heads = values.transpose(1, 0, 2)
    scores = jnp.einsum('grtd,gkd->grtk', grouped, key_heads, precision=highest) * ATT_DIM ** (-0.5)
    visible = (positions[None, :] <= positions[:, None]) & (segments[None, :] == segments[:, None])
    scores = low_back(jnp.where(visible[None, None], scores, -1e+30))
    probs = low(jax.nn.softmax(scores, axis=-1))
    attended = jnp.einsum('grtk,gkd->grtd', probs, value_heads, precision=highest)
    attended = low(attended.transpose(2, 0, 1, 3).reshape(LENGTH, ATT_HEADS * ATT_DIM))
    attn_branch = low_back(matmul(attended, attn_out))
    hidden = token_rows + mixer_branch + attn_branch
    ffn_in = low(rms_scale(hidden, ffn_gain))
    gate_vals = low_back(matmul(ffn_in, gate_up))
    activated = low(swiglu(gate_vals))
    return hidden + low_back(matmul(activated, down_proj))

def reference(tokens, doc_ends, input_gain, mixer_in, conv_weight, conv_bias, head_params, mixer_gain, mixer_out, attn_qkv, attn_out, ffn_gain, gate_up, down_proj, out_grad):
    weights = tuple((entry.astype(jnp.float32) for entry in (input_gain, mixer_in, conv_weight, conv_bias, head_params, mixer_gain, mixer_out, attn_qkv, attn_out, ffn_gain, gate_up, down_proj)))
    flat_tokens = tokens.astype(jnp.float32).reshape(MICRO * SEQS, LENGTH, D)
    flat_ends = doc_ends.reshape(MICRO * SEQS, DOCS)
    per_sequence = jax.checkpoint(sequence_layer)

    def whole_layer(weight_set, token_set):
        return lax.map(lambda paired: per_sequence(weight_set, paired[0], paired[1]), (token_set, flat_ends))
    layer_out, pullback = jax.vjp(whole_layer, weights, flat_tokens)
    weight_grads, token_grad = pullback(out_grad.astype(jnp.float32).reshape(MICRO * SEQS, LENGTH, D))
    full_shape = (MICRO, SEQS, LENGTH, D)
    return (layer_out.reshape(full_shape).astype(jnp.bfloat16), token_grad.reshape(full_shape), weight_grads[0], weight_grads[1], weight_grads[2], weight_grads[3], weight_grads[4], weight_grads[5], weight_grads[6], weight_grads[7], weight_grads[8], weight_grads[9], weight_grads[10], weight_grads[11])
```

```python
from functools import partial

import jax
import jax.numpy as jnp
from jax import lax
from jax.sharding import PartitionSpec as P

D = 2048
FF = 4096
HEADS = 48
HEAD_DIM = 64
STATE = 256
ATT_HEADS = 8
KV_HEADS = 2
ATT_DIM = 128
INNER = HEADS * HEAD_DIM
CONV = 4
DT_PAD = 128

epsilon = 1e-05
rope_base = 10000.0
f32 = jnp.float32
bf16 = jnp.bfloat16


def permuted(value, axis, by):
    pairs = [(i, i ^ by) for i in range(lax.axis_size(axis))]
    return lax.ppermute(value, axis, pairs)


def small_gather(value):
    rows = value[None]
    for axis in ("dp", "seq"):
        here = lax.axis_index(axis)
        by = 1
        while by < lax.axis_size(axis):
            other = permuted(rows, axis, by)
            upper = (here & by) != 0
            rows = jnp.where(
                upper, jnp.concatenate([other, rows]), jnp.concatenate([rows, other])
            )
            by *= 2
    return rows


def summed(value, axes):
    for axis in axes:
        by = 1
        while by < lax.axis_size(axis):
            value = value + permuted(value, axis, by)
            by *= 2
    return value


def turned_order(value, here, count):
    by = 1
    tail = value.shape[1:]
    while by < count:
        split = value.reshape(count // (2 * by), 2, by, *tail)
        flipped = jnp.concatenate([split[:, 1:], split[:, :1]], axis=1)
        value = jnp.where((here & by) != 0, flipped, split).reshape(count, *tail)
        by *= 2
    return value


def exchanged(blocks, axis):
    count, here = lax.axis_size(axis), lax.axis_index(axis)
    ready = turned_order(blocks, here, count)
    got = [ready[0]] + [permuted(ready[k], axis, k) for k in range(1, count)]
    return turned_order(jnp.stack(got), here, count)


def dp_gather(value):
    if lax.axis_size("dp") != 4:
        return lax.all_gather(value, "dp", axis=0)
    half = value.shape[0] // 2
    one = permuted(value, "dp", 1)
    two = permuted(value, "dp", 2)
    three = jnp.concatenate([permuted(one[:half], "dp", 2), permuted(two[half:], "dp", 1)])
    return jnp.stack([value, one, two, three])


def dp_scatter(total):
    if lax.axis_size("dp") != 4:
        return lax.psum_scatter(total, "dp", scatter_dimension=0).astype(f32)
    half = total.shape[1] // 2
    low, high = total[:, :half], total[:, half:]
    low_in = permuted(jnp.stack([low[1], low[3]]), "dp", 1).astype(f32)
    high_in = permuted(high[2:], "dp", 2).astype(f32)
    low_on = (low[2].astype(f32) + low_in[1]).astype(bf16)
    high_on = (high[1].astype(f32) + high_in[1]).astype(bf16)
    low_own = low[0].astype(f32) + low_in[0] + permuted(low_on, "dp", 2).astype(f32)
    high_own = high[0].astype(f32) + high_in[0] + permuted(high_on, "dp", 1).astype(f32)
    return jnp.concatenate([low_own, high_own])


def segment_of(positions, end_points):
    counted = jnp.sum((end_points[None, :] <= positions[:, None]).astype(jnp.int32), axis=1)
    return jnp.where(positions < 0, -1, counted)


def rope_tables(positions):
    half = ATT_DIM // 2
    freqs = jnp.power(rope_base, -jnp.arange(half, dtype=f32) * (2.0 / ATT_DIM))
    angles = positions.astype(f32)[:, None] * freqs[None, :]
    cosine, sine = jnp.cos(angles), jnp.sin(angles)
    return jnp.concatenate([cosine, cosine], axis=1), jnp.concatenate([sine, sine], axis=1)


def turned(values, cosine, sine):
    half = ATT_DIM // 2
    swapped = jnp.concatenate([-values[..., half:], values[..., :half]], axis=-1)
    return values * cosine + swapped * sine


def turned_back(values, cosine, sine):
    return turned(values, cosine, -sine)


def rms_row(values):
    return lax.rsqrt(jnp.mean(values * values, axis=-1, keepdims=True) + epsilon)


def rms_back(grad, values, gain):
    r = rms_row(values)
    scaled = grad * gain
    along = jnp.mean(scaled * values, axis=-1, keepdims=True)
    return scaled * r - values * (r * r * r) * along, jnp.sum(grad * values * r, axis=0)


def silu_back(value):
    sig = jax.nn.sigmoid(value)
    return sig * (1.0 + value * (1.0 - sig))


def dot(left, right):
    return jnp.dot(left, right, preferred_element_type=f32)


def dot_t(left, right):
    return lax.dot_general(left, right, (((1,), (1,)), ((), ())), preferred_element_type=f32)


def cross(left, right):
    return lax.dot_general(left, right, (((0,), (0,)), ((), ())), preferred_element_type=f32)


def mixer_core(x_in, bc_in, dt_raw, gate_z, w_x, b_x, w_bc, b_bc, head, seg, blocks):
    rows, inner = x_in.shape
    heads = head.shape[1]
    width = inner // heads
    per = rows // blocks
    conv_in = jnp.concatenate([x_in, bc_in], axis=1)
    weight = jnp.concatenate([w_x, w_bc], axis=1)
    total = jnp.concatenate([b_x, b_bc])[None, :]
    for tap in range(CONV):
        back = CONV - 1 - tap
        if back:
            moved = jnp.pad(conv_in[: rows - back], ((back, 0), (0, 0)))
            seg_moved = jnp.pad(seg[: rows - back], (back, 0), constant_values=-1)
        else:
            moved, seg_moved = conv_in, seg
        same = (seg_moved == seg).astype(f32)[:, None]
        total = total + moved * weight[tap][None, :] * same
    conv_out = jax.nn.silu(total)
    step = jax.nn.softplus(dt_raw + head[1][None, :])
    decay = -jnp.exp(head[0])[None, :] * step
    tril = jnp.tril(jnp.ones((per, per), f32))
    cum = jnp.einsum(
        "ts,bsh->bth", tril, decay.reshape(blocks, per, heads), precision=lax.Precision.HIGHEST
    )
    step = step.reshape(blocks, per, heads)
    x = conv_out[:, :inner].reshape(blocks, per, heads, width)
    b = conv_out[:, inner : inner + STATE].reshape(blocks, per, STATE)
    c = conv_out[:, inner + STATE :].reshape(blocks, per, STATE)
    seg_b = seg.reshape(blocks, per)
    prior = jnp.concatenate([jnp.full((1,), -1, jnp.int32), seg_b[:-1, per - 1]])
    order = jnp.arange(per)
    within = (order[None, :, None] >= order[None, None, :]) & (
        seg_b[:, :, None] == seg_b[:, None, :]
    )
    entering = (seg_b == prior[:, None]).astype(f32)
    last = seg_b[:, per - 1]
    trailing = (seg_b == last[:, None]).astype(f32)
    passing = (last == prior).astype(f32)
    both = jnp.einsum("btn,bsn->bts", c, b, preferred_element_type=f32)
    gap = cum[:, :, None, :] - cum[:, None, :, :]
    mask = within[..., None]
    mixing = both[..., None] * jnp.where(mask, jnp.exp(jnp.where(mask, gap, 0.0)), 0.0)
    mixing = mixing * step[:, None, :, :]
    y = jnp.einsum("btsh,bshp->bthp", mixing, x, preferred_element_type=f32)
    end = cum[:, per - 1]
    keeping = jnp.exp(end[:, None, :] - cum) * trailing[:, :, None] * step
    states = jnp.einsum("bshp,bsn->bhpn", x * keeping[..., None], b, preferred_element_type=f32)
    passed = jnp.exp(end) * passing[:, None]
    state = jnp.zeros(states.shape[1:], f32)
    entered = []
    for k in range(blocks):
        entered.append(state)
        state = passed[k][:, None, None] * state + states[k]
    entered = jnp.stack(entered)
    carried = jnp.einsum("btn,bhpn->bthp", c, entered, preferred_element_type=f32)
    y = y + carried * (jnp.exp(cum) * entering[..., None])[..., None]
    y = y + head[2][None, None, :, None] * x
    return y.reshape(rows, inner) * jax.nn.silu(gate_z)


def local(
    tokens,
    doc_ends,
    input_gain,
    mixer_in,
    conv_weight,
    conv_bias,
    head_params,
    mixer_gain,
    mixer_out,
    attn_qkv,
    attn_out,
    ffn_gain,
    gate_up,
    down_proj,
    out_grad,
):
    n = lax.axis_size("seq")
    nd = lax.axis_size("dp")
    s = lax.axis_index("seq")
    d = lax.axis_index("dp")
    micro, _, per, _ = tokens.shape
    own = micro * per
    length = n * per
    rows = n * own
    owner = mixer_in.shape[0]
    inner = INNER // n
    heads = HEADS // n
    ffl = FF // n
    parts = n // ATT_HEADS
    group = ATT_HEADS // KV_HEADS
    scale = ATT_DIM ** (-0.5)
    conv_ch = INNER + 2 * STATE

    def dp_order(value):
        return turned_order(value, d, nd) if nd == 4 else value

    def mixed_order(value):
        split = dp_order(value.reshape(own, n, nd, owner).transpose(2, 0, 1, 3))
        return split.transpose(1, 0, 2, 3).reshape(own, D)

    def plain_order(value):
        split = dp_order(value.reshape(own, nd, n, owner).transpose(1, 0, 2, 3))
        return split.transpose(1, 2, 0, 3).reshape(own, D)

    def row_weight(value):
        return dp_order(dp_gather(value)).reshape(-1, D)

    def row_grad(total):
        return dp_scatter(dp_order(total.reshape(nd, -1, D)))

    def to_seq(value):
        return value.reshape(n, micro, per, -1).transpose(1, 0, 2, 3).reshape(micro, length, -1)

    def from_seq(value):
        return value.reshape(micro, n, per, -1).transpose(1, 0, 2, 3).reshape(rows, -1)

    def gathered(value):
        return lax.all_gather(value, "seq", axis=0, tiled=True)

    def scattered(value):
        return lax.psum_scatter(
            value.astype(bf16), "seq", scatter_dimension=0, tiled=True
        ).astype(f32)

    token_rows = tokens.reshape(own, D).astype(f32)
    grad_rows = out_grad.reshape(own, D)

    cols = [
        mixer_in[:, :INNER].reshape(owner, n, inner).transpose(1, 0, 2),
        mixer_in[:, INNER : 2 * INNER].reshape(owner, n, inner).transpose(1, 0, 2),
        jnp.broadcast_to(
            mixer_in[:, 2 * INNER : 2 * INNER + 2 * STATE][None], (n, owner, 2 * STATE)
        ),
        jnp.pad(
            mixer_in[:, 2 * INNER + 2 * STATE :].reshape(owner, n, heads).transpose(1, 0, 2),
            ((0, 0), (0, 0), (0, DT_PAD - heads)),
        ),
    ]
    by_head = attn_qkv.reshape(owner, ATT_HEADS + 2 * KV_HEADS, ATT_DIM).transpose(1, 0, 2)
    q_of = [k // parts for k in range(n)]
    k_of = [ATT_HEADS + q // group for q in q_of]
    v_of = [ATT_HEADS + KV_HEADS + q // group for q in q_of]
    for of in (q_of, k_of, v_of):
        cols.append(jnp.stack([by_head[k] for k in of]))
    sizes = [inner, inner, 2 * STATE, DT_PAD, ATT_DIM, ATT_DIM, ATT_DIM]
    starts = [sum(sizes[:k]) for k in range(len(sizes) + 1)]
    sent_in = exchanged(jnp.concatenate(cols, axis=2), "seq")
    w_in = dp_gather(sent_in).reshape(D, starts[-1])
    sent_gu = exchanged(
        gate_up.reshape(owner, 2, n, ffl).transpose(2, 0, 1, 3).reshape(n, owner, 2 * ffl), "seq"
    )
    w_gu = dp_gather(sent_gu).reshape(D, 2 * ffl)
    w_mix = row_weight(mixer_out)
    w_att = row_weight(attn_out)
    if parts > 1:
        other = permuted(w_att, "seq", 1)
        w_att = jnp.where(
            (s & 1) != 0, jnp.concatenate([other, w_att]), jnp.concatenate([w_att, other])
        )
    w_down = row_weight(down_proj)

    tap_count = conv_weight.shape[1]
    small = small_gather(
        jnp.concatenate(
            [input_gain, conv_weight.reshape(-1), conv_bias, mixer_gain, ffn_gain]
        )
    )
    cuts = [owner, CONV * tap_count, tap_count, mixer_gain.shape[0], owner]
    at = [sum(cuts[:k]) for k in range(len(cuts) + 1)]
    small = small.astype(f32)
    gain_in = small[:, at[0] : at[1]].reshape(-1)
    taps = (
        small[:, at[1] : at[2]].reshape(-1, CONV, tap_count).transpose(1, 0, 2).reshape(CONV, -1)
    )
    shift = small[:, at[2] : at[3]].reshape(-1)
    gain_mix = lax.dynamic_slice_in_dim(
        small[:, at[3] : at[4]].reshape(-1), s * inner, inner
    )
    gain_ffn = small[:, at[4] : at[5]].reshape(-1)
    w_x = lax.dynamic_slice_in_dim(taps, s * inner, inner, axis=1)
    b_x = lax.dynamic_slice_in_dim(shift, s * inner, inner)
    w_bc, b_bc = taps[:, INNER:], shift[INNER:]
    head = lax.dynamic_slice_in_dim(head_params, s * heads, heads, axis=1)

    normed_own = (token_rows * rms_row(token_rows) * gain_in).astype(bf16)
    normed = gathered(mixed_order(normed_own))
    grads = gathered(lax.optimization_barrier((grad_rows, normed[:8, :128]))[0])
    mixed = dot(normed, w_in)
    gate_z, x_in, bc_in, dt_raw, q_raw, k_raw, v_raw = (
        mixed[:, starts[k] : starts[k + 1]] for k in range(7)
    )
    positions = jnp.arange(length, dtype=jnp.int32)
    seg = jnp.stack([segment_of(positions, doc_ends[m, 0]) for m in range(micro)])

    def core(gate_z, x_in, bc_in, dt_raw, w_x, b_x, w_bc, b_bc, head):
        def one(z, x, bc, dt, seg_m):
            return mixer_core(x, bc, dt, z, w_x, b_x, w_bc, b_bc, head, seg_m, n)

        return from_seq(
            jax.vmap(one)(to_seq(gate_z), to_seq(x_in), to_seq(bc_in), to_seq(dt_raw), seg)
        )

    gated, pull_core = jax.vjp(
        core,
        gate_z,
        x_in.astype(bf16).astype(f32),
        bc_in.astype(bf16).astype(f32),
        dt_raw[:, :heads],
        w_x,
        b_x,
        w_bc,
        b_bc,
        head,
    )
    squares = summed(jnp.sum(gated * gated, axis=1), ("seq",)) / INNER
    r_mix = lax.rsqrt(squares + epsilon)[:, None]
    mixer_b = (gated * r_mix * gain_mix).astype(bf16)

    cosine, sine = rope_tables(positions)
    queries = turned(to_seq(q_raw), cosine, sine).astype(bf16)
    keys = turned(to_seq(k_raw), cosine, sine).astype(bf16)
    values = to_seq(v_raw).astype(bf16)
    part = s % parts

    def taken(value):
        if parts == 1:
            return value
        split = value.reshape(micro, n // parts, parts, per, -1)
        split = lax.dynamic_index_in_dim(split, part, 2, False)
        return split.reshape(micro, length // parts, -1)

    def put_back(value):
        if parts == 1:
            return value
        split = value.reshape(micro, n // parts, 1, per, -1)
        here = (jnp.arange(parts) == part)[None, None, :, None, None]
        return jnp.where(here, split, 0).reshape(micro, length, -1)

    q_pos = taken(jnp.broadcast_to(positions[None, :, None], (micro, length, 1)))
    q_seg = taken(seg[:, :, None])
    queries = taken(queries)
    visible = (positions[None, None, :] <= q_pos) & (seg[:, None, :] == q_seg)
    scores = jnp.einsum("mtd,mkd->mtk", queries, keys, preferred_element_type=f32) * scale
    scores = jnp.where(visible, scores, -1e30)
    top = jnp.max(scores, axis=-1, keepdims=True)
    expd = jnp.exp(scores - top)
    probs_b = (expd / jnp.sum(expd, axis=-1, keepdims=True)).astype(bf16)
    attended = jnp.einsum("mtk,mkd->mtd", probs_b, values, preferred_element_type=f32)
    attended_b = from_seq(put_back(attended.astype(bf16)))
    branches = dot(mixer_b, w_mix) + dot(attended_b, w_att)
    branches, _ = lax.optimization_barrier((branches.astype(bf16), grads[:8, :128]))
    hidden = token_rows + scattered(branches)
    ffn_own = (hidden * rms_row(hidden) * gain_ffn).astype(bf16)
    ffn_in = gathered(mixed_order(ffn_own))
    gate_vals = dot(ffn_in, w_gu)
    gate, up = gate_vals[:, :ffl], gate_vals[:, ffl:]
    activated_b = (jax.nn.silu(gate) * up).astype(bf16)
    ffn_out = dot(activated_b, w_down)

    act_grad = dot_t(grads, w_down)
    gate_grad = jnp.concatenate(
        [act_grad * up * silu_back(gate), act_grad * jax.nn.silu(gate)], axis=1
    ).astype(bf16)
    ffn_in_grad = plain_order(scattered(dot_t(gate_grad, w_gu)))
    gu_total = cross(ffn_in, gate_grad).astype(bf16)
    down_total = cross(activated_b, grads).astype(bf16)
    hidden_part, ffn_gain_grad = rms_back(ffn_in_grad, hidden, gain_ffn)
    hidden_grad = hidden_part + grad_rows.astype(f32)
    hidden_b = gathered(hidden_grad.astype(bf16))

    ffn_out, _ = lax.optimization_barrier((ffn_out.astype(bf16), hidden_b[:8, :128]))
    layer_out = (hidden + scattered(ffn_out)).astype(bf16)

    att_grad = taken(to_seq(dot_t(hidden_b, w_att).astype(bf16)))
    probs = probs_b.astype(f32)
    probs_grad = jnp.einsum("mtd,mkd->mtk", att_grad, values, preferred_element_type=f32)
    scores_grad = (
        probs * (probs_grad - jnp.sum(probs * probs_grad, axis=-1, keepdims=True))
    ).astype(bf16)
    q_grad = jnp.einsum("mtk,mkd->mtd", scores_grad, keys, preferred_element_type=f32) * scale
    k_grad = jnp.einsum("mtk,mtd->mkd", scores_grad, queries, preferred_element_type=f32) * scale
    v_grad = jnp.einsum("mtk,mtd->mkd", probs_b, att_grad, preferred_element_type=f32)
    q_grad = from_seq(turned_back(put_back(q_grad), cosine, sine).astype(bf16))
    k_grad = from_seq(turned_back(k_grad, cosine, sine).astype(bf16))
    v_grad = from_seq(v_grad.astype(bf16))

    mix_grad = dot_t(hidden_b, w_mix)
    scaled = mix_grad * gain_mix
    along = summed(jnp.sum(scaled * gated, axis=1), ("seq",))[:, None] / INNER
    mix_gain_grad = jnp.sum(mix_grad * gated * r_mix, axis=0)
    gated_grad = scaled * r_mix - gated * (r_mix * r_mix * r_mix) * along
    z_g, x_g, bc_g, dt_g, w_x_g, b_x_g, w_bc_g, b_bc_g, head_g = pull_core(gated_grad)
    mixed_grad = jnp.concatenate(
        [
            z_g.astype(bf16),
            x_g.astype(bf16),
            bc_g.astype(bf16),
            jnp.pad(dt_g, ((0, 0), (0, DT_PAD - heads))).astype(bf16),
            q_grad,
            k_grad,
            v_grad,
        ],
        axis=1,
    )
    in_back, _ = lax.optimization_barrier(
        (dot_t(mixed_grad, w_in).astype(bf16), layer_out[:8, :128])
    )
    normed_grad = plain_order(scattered(in_back))
    in_total = cross(normed, mixed_grad).astype(bf16)
    mix_total = cross(mixer_b, hidden_b).astype(bf16)
    att_total = cross(attended_b, hidden_b).astype(bf16)
    token_part, in_gain_grad = rms_back(normed_grad, token_rows, gain_in)
    token_grad = token_part + hidden_grad

    def to_owners(total):
        part_sum = dp_scatter(total.reshape(nd, n * owner, -1)).astype(bf16)
        return exchanged(part_sum.reshape(n, owner, -1), "seq").astype(f32)

    gu_sum = to_owners(gu_total)
    gate_up_grad = (
        gu_sum.reshape(n, owner, 2, ffl).transpose(1, 2, 0, 3).reshape(owner, 2 * FF)
    )
    down_grad = row_grad(down_total)
    mixer_out_grad = row_grad(mix_total)
    if parts > 1:
        half = att_total.shape[0] // 2
        low, high = att_total[:half], att_total[half:]
        odd = (s & 1) != 0
        other = permuted(jnp.where(odd, low, high), "seq", 1)
        att_total = (jnp.where(odd, high, low).astype(f32) + other.astype(f32)).astype(bf16)
    attn_out_grad = row_grad(att_total)
    in_sum = to_owners(in_total)
    pieces = [in_sum[:, :, starts[k] : starts[k + 1]] for k in range(7)]
    mixer_in_grad = jnp.concatenate(
        [
            pieces[0].transpose(1, 0, 2).reshape(owner, INNER),
            pieces[1].transpose(1, 0, 2).reshape(owner, INNER),
            jnp.sum(pieces[2], axis=0),
            pieces[3][:, :, :heads].transpose(1, 0, 2).reshape(owner, HEADS),
        ],
        axis=1,
    )
    q_sum = pieces[4].reshape(ATT_HEADS, parts, owner, ATT_DIM).sum(axis=1)
    k_sum = pieces[5].reshape(KV_HEADS, n // KV_HEADS, owner, ATT_DIM).sum(axis=1)
    v_sum = pieces[6].reshape(KV_HEADS, n // KV_HEADS, owner, ATT_DIM).sum(axis=1)
    attn_qkv_grad = (
        jnp.concatenate([q_sum, k_sum, v_sum]).transpose(1, 0, 2).reshape(owner, -1)
    )

    def placed(value, width):
        full = jnp.zeros(value.shape[:-1] + (width,), f32)
        return lax.dynamic_update_slice_in_dim(
            full, value, s * value.shape[-1], axis=value.ndim - 1
        )

    conv_full = jnp.concatenate([placed(jnp.concatenate([w_x_g, b_x_g[None]]), INNER),
                                 jnp.concatenate([w_bc_g, b_bc_g[None]])], axis=1)
    flat = jnp.concatenate(
        [
            ffn_gain_grad,
            placed(mix_gain_grad, INNER),
            conv_full.reshape(-1),
            placed(head_g, HEADS).reshape(-1),
        ]
    )
    flat = jnp.concatenate(
        [summed(in_gain_grad, ("seq", "dp")), summed(flat, ("seq", "dp"))]
    )
    index = s * nd + d

    def mine(value):
        width = value.shape[-1] // (n * nd)
        return lax.dynamic_slice_in_dim(value, index * width, width, axis=value.ndim - 1)

    ends = [D, 2 * D, 2 * D + INNER, 2 * D + INNER + (CONV + 1) * conv_ch]
    conv_full = flat[ends[2] : ends[3]].reshape(CONV + 1, conv_ch)
    conv_own = mine(conv_full)
    return (
        layer_out.reshape(micro, 1, per, D),
        token_grad.reshape(micro, 1, per, D),
        mine(flat[: ends[0]]),
        mixer_in_grad,
        conv_own[:CONV],
        conv_own[CONV],
        flat[ends[3] :].reshape(3, HEADS),
        mine(flat[ends[1] : ends[2]]),
        mixer_out_grad,
        attn_qkv_grad,
        attn_out_grad,
        mine(flat[ends[0] : ends[1]]),
        gate_up_grad,
        down_grad,
    )


def solution(mesh):
    rows = P(("seq", "dp"), None)
    vector = P(("seq", "dp"))
    activations = P(None, "dp", "seq", None)
    return jax.shard_map(
        local,
        mesh=mesh,
        in_specs=(
            activations,
            P(None, "dp", None),
            vector,
            rows,
            P(None, ("seq", "dp")),
            vector,
            P(),
            vector,
            rows,
            rows,
            rows,
            vector,
            rows,
            rows,
            activations,
        ),
        out_specs=(
            activations,
            activations,
            vector,
            rows,
            P(None, ("seq", "dp")),
            vector,
            P(),
            vector,
            rows,
            rows,
            rows,
            vector,
            rows,
            rows,
        ),
        check_vma=False,
    )
```

```python
import jax
import jax.numpy as jnp
from jax import lax
from jax.experimental import pallas as pl
from jax.experimental.pallas import tpu as pltpu
from jax.sharding import PartitionSpec as P

D = 2048
FF = 4096
HEADS = 48
HEAD_DIM = 64
STATE = 256
ATT_HEADS = 8
KV_HEADS = 2
ATT_DIM = 128
INNER = HEADS * HEAD_DIM
CONV = 4
PROJ = 2 * INNER + 2 * STATE + HEADS
DT_PAD = 128

epsilon = 1e-05
rope_base = 10000.0
f32 = jnp.float32
bf16 = jnp.bfloat16


def after(value, *others):
    def nothing(*refs):
        pass

    return pl.pallas_call(
        nothing,
        out_shape=jax.ShapeDtypeStruct(value.shape, value.dtype),
        in_specs=[pl.BlockSpec(memory_space=pl.ANY)] * (1 + len(others)),
        out_specs=pl.BlockSpec(memory_space=pl.ANY),
        input_output_aliases={0: 0},
    )(value, *others)


def permuted(value, axis, by):
    pairs = [(i, i ^ by) for i in range(lax.axis_size(axis))]
    return lax.ppermute(value, axis, pairs)


def small_gather(value):
    rows = value[None]
    for axis in ("dp", "seq"):
        here = lax.axis_index(axis)
        by = 1
        while by < lax.axis_size(axis):
            other = permuted(rows, axis, by)
            upper = (here & by) != 0
            rows = jnp.where(
                upper, jnp.concatenate([other, rows]), jnp.concatenate([rows, other])
            )
            by *= 2
    return rows


def summed(value, axes):
    for axis in axes:
        by = 1
        while by < lax.axis_size(axis):
            value = value + permuted(value, axis, by)
            by *= 2
    return value


def exchanged(blocks, axis):
    return lax.all_to_all(blocks, axis, 0, 0, tiled=True)


def assembled(shape, kind, moves, *inputs):
    def kernel(*refs):
        out = refs[-1]
        for which, source, target in moves:
            out[target] = refs[which][source].astype(out.dtype)

    return pl.pallas_call(
        kernel,
        out_shape=jax.ShapeDtypeStruct(shape, kind),
        compiler_params=pltpu.CompilerParams(vmem_limit_bytes=40 * 1024 * 1024),
        cost_estimate=about(4),
    )(*inputs)


def about(microseconds):
    return pl.CostEstimate(
        flops=0, bytes_accessed=int(microseconds * 3.6e6), transcendentals=0
    )


def regrouped(value, outer, inner, width):
    rows, total = value.shape
    if width != 64 or outer % 2:
        split = value.reshape(rows, outer, inner, width)
        return jnp.swapaxes(split, 1, 2).reshape(rows, total)

    def kernel(in_ref, out_ref):
        for i in range(inner):
            for o in range(0, outer, 2):
                left = in_ref[:, (o * inner + i) * width : (o * inner + i + 1) * width]
                right = in_ref[:, ((o + 1) * inner + i) * width : ((o + 1) * inner + i + 1) * width]
                at = (i * outer + o) * width
                out_ref[:, at : at + 2 * width] = jnp.concatenate([left, right], axis=1)

    return pl.pallas_call(
        kernel,
        out_shape=jax.ShapeDtypeStruct(value.shape, value.dtype),
        compiler_params=pltpu.CompilerParams(vmem_limit_bytes=40 * 1024 * 1024),
        cost_estimate=about(2),
    )(value)


def dp_gather(value, forward=True):
    if lax.axis_size("dp") != 4:
        return lax.all_gather(value, "dp", axis=0)
    here = lax.axis_index("dp")
    half = value.shape[0] // 2
    one = permuted(value, "dp", 1)
    two = permuted(value, "dp", 2)
    if forward:
        three = jnp.concatenate([permuted(one[:half], "dp", 2), permuted(two[half:], "dp", 1)])
    else:
        three = permuted(value, "dp", 3)
    whole = jnp.zeros((4,) + value.shape, value.dtype)
    for k, piece in enumerate((value, one, two, three)):
        whole = lax.dynamic_update_index_in_dim(whole, piece, here ^ k, 0)
    return whole


def placed_pieces(pieces, here, cuts):
    count, (rows, width) = len(pieces), pieces[0].shape
    spans = list(zip(cuts[:-1], cuts[1:]))

    def kernel(here_ref, *refs):
        for k in range(count):
            owner = here_ref[0] ^ k
            for (low, high), out in zip(spans, refs[count:]):
                out[pl.ds(pl.multiple_of(owner * (high - low), 16), high - low)] = refs[k][low:high]

    return pl.pallas_call(
        kernel,
        out_shape=[
            jax.ShapeDtypeStruct((count * (high - low), width), pieces[0].dtype)
            for low, high in spans
        ],
        in_specs=[pl.BlockSpec(memory_space=pltpu.SMEM)]
        + [pl.BlockSpec(memory_space=pltpu.VMEM)] * count,
        out_specs=[pl.BlockSpec(memory_space=pltpu.VMEM)] * len(spans),
        compiler_params=pltpu.CompilerParams(vmem_limit_bytes=40 * 1024 * 1024),
        cost_estimate=about(2),
    )(here[None], *pieces)


def dp_scatter(total, forward=True, meanwhile=()):
    if lax.axis_size("dp") != 4:
        return lax.psum_scatter(total, "dp", scatter_dimension=0).astype(f32)
    here = lax.axis_index("dp")
    blocks = [lax.dynamic_index_in_dim(total, here ^ k, 0, False) for k in range(4)]
    if not forward:
        own = blocks[0].astype(f32)
        for k in range(1, 4):
            own = own + permuted(blocks[k], "dp", k).astype(f32)
        return own
    half = total.shape[1] // 2
    low, high = [b[:half] for b in blocks], [b[half:] for b in blocks]
    low_in = permuted(jnp.stack([low[1], low[3]]), "dp", 1)
    high_in = permuted(jnp.stack(high[2:]), "dp", 2)
    if meanwhile:
        low_in, high_in = after(low_in, *meanwhile), after(high_in, *meanwhile)
    low_in, high_in = low_in.astype(f32), high_in.astype(f32)
    low_on = (low[2].astype(f32) + low_in[1]).astype(bf16)
    high_on = (high[1].astype(f32) + high_in[1]).astype(bf16)
    low_own = low[0].astype(f32) + low_in[0] + permuted(low_on, "dp", 2).astype(f32)
    high_own = high[0].astype(f32) + high_in[0] + permuted(high_on, "dp", 1).astype(f32)
    return jnp.concatenate([low_own, high_own])


def row_sums(value):
    return other_pairs(value + permuted(value, "seq", 1))


def other_pairs(value):
    total = value
    for by in range(2, lax.axis_size("seq"), 2):
        total = total + permuted(value, "seq", by)
    return total


def segment_of(positions, end_points):
    counted = jnp.sum((end_points[None, :] <= positions[:, None]).astype(jnp.int32), axis=1)
    return jnp.where(positions < 0, -1, counted)


def rope_tables(positions):
    half = ATT_DIM // 2
    freqs = jnp.power(rope_base, -jnp.arange(half, dtype=f32) * (2.0 / ATT_DIM))
    angles = positions.astype(f32)[:, None] * freqs[None, :]
    cosine, sine = jnp.cos(angles), jnp.sin(angles)
    return jnp.concatenate([cosine, cosine], axis=1), jnp.concatenate([sine, sine], axis=1)


def rms_row(values):
    return lax.rsqrt(jnp.mean(values * values, axis=-1, keepdims=True) + epsilon)


def rms_back(grad, values, gain):
    r = rms_row(values)
    scaled = grad * gain
    along = jnp.mean(scaled * values, axis=-1, keepdims=True)
    return scaled * r - values * (r * r * r) * along, jnp.sum(grad * values * r, axis=0)


def dot(left, right):
    return jnp.dot(left, right, preferred_element_type=f32)


def dot_t(left, right):
    return lax.dot_general(left, right, (((1,), (1,)), ((), ())), preferred_element_type=f32)


def cross(left, right):
    return lax.dot_general(left, right, (((0,), (0,)), ((), ())), preferred_element_type=f32)


def halves(columns, pair, lanes):
    left, right = columns[:, 2 * pair : 2 * pair + 1], columns[:, 2 * pair + 1 : 2 * pair + 2]
    return jnp.where(lanes < HEAD_DIM, left, right)


def spread(columns, pairs, lanes):
    return jnp.concatenate([halves(columns, k, lanes) for k in range(pairs)], axis=1)


def counted(pattern, value, dims=(((1,), (0,)), ((), ())), terms=2, first=True):
    pattern = pattern.astype(bf16)
    total, rest = None, value
    for k in range(terms):
        term = rest.astype(bf16)
        pair = (pattern, term) if first else (term, pattern)
        part = lax.dot_general(*pair, dims, preferred_element_type=f32)
        total = part if total is None else total + part
        if k + 1 < terms:
            rest = rest - term.astype(f32)
    return total


def rough(left, right, dims=(((1,), (0,)), ((), ()))):
    return lax.dot_general(
        left.astype(bf16), right.astype(bf16), dims, preferred_element_type=f32
    )


ROWS = (((0,), (0,)), ((), ()))
LAST = (((1,), (1,)), ((), ()))


def block_start(mixed_ref, before_ref, aux_ref, conv_ref, head_ref, ext_ref, width):
    per = mixed_ref.shape[0]
    channels = width + 2 * STATE
    ext_ref[0:8] = before_ref[:, width : width + channels].astype(bf16).astype(f32)
    ext_ref[8 : 8 + per] = mixed_ref[:, width : width + channels].astype(bf16).astype(f32)
    aux = aux_ref[...]
    total = conv_ref[4:5] + ext_ref[8 : 8 + per] * conv_ref[3:4]
    for back in range(1, CONV):
        total = total + ext_ref[8 - back : 8 - back + per] * (
            aux[:, back : back + 1] * conv_ref[3 - back : 4 - back]
        )
    sig = jax.nn.sigmoid(total)
    shifted = mixed_ref[:, width + channels : width + channels + DT_PAD] + head_ref[1:2]
    step = jnp.maximum(shifted, 0.0) + jnp.log1p(jnp.exp(-jnp.abs(shifted)))
    rate = -jnp.exp(head_ref[0:1])
    rows_at = lax.broadcasted_iota(jnp.int32, (per, per), 0)
    cols_at = lax.broadcasted_iota(jnp.int32, (per, per), 1)
    tril = (rows_at >= cols_at).astype(f32)
    cum = counted(tril, step * rate, terms=3)
    return aux, total, sig, shifted, step, rate, tril, cum


def ssd_forward_kernel(
    mixed_ref,
    before_ref,
    aux_ref,
    seg_ref,
    conv_ref,
    head_ref,
    skip_ref,
    y_ref,
    gated_ref,
    enter_ref,
    ext_ref,
    state_ref,
):
    per, width = y_ref.shape
    pairs = width // 128

    @pl.when(pl.program_id(1) == 0)
    def _():
        state_ref[...] = jnp.zeros_like(state_ref)

    aux, total, sig, _, step, _, tril, cum = block_start(
        mixed_ref, before_ref, aux_ref, conv_ref, head_ref, ext_ref, width
    )
    conv = total * sig
    x = conv[:, :width]
    b = conv[:, width : width + STATE].astype(bf16)
    c = conv[:, width + STATE :].astype(bf16)
    lanes = lax.broadcasted_iota(jnp.int32, (per, 128), 1)
    mask = (tril > 0) & (aux[:, 0:1] == seg_ref[0])
    both = rough(c, b, LAST)
    cum_t, step_t = cum.T, step.T
    state = state_ref[...]
    enter_ref[0] = state.astype(bf16)
    carried = rough(c, state)
    grown = jnp.exp(cum) * aux[:, 4:5]
    last = cum[per - 1 : per]
    keep = jnp.exp(last - cum) * aux[:, 5:6] * step
    gate = mixed_ref[:, :width]
    silu_gate = gate * jax.nn.sigmoid(gate)
    scaled = []
    for k in range(pairs):
        at = slice(128 * k, 128 * k + 128)
        x_pair = x[:, at]
        x_low = x_pair.astype(bf16)
        sides = []
        for h in (2 * k, 2 * k + 1):
            gap = jnp.where(mask, cum[:, h : h + 1] - cum_t[h : h + 1], -1e30)
            mixing = both * jnp.exp(gap) * step_t[h : h + 1]
            sides.append(rough(mixing, x_low))
        y = jnp.where(lanes < HEAD_DIM, sides[0], sides[1])
        y = y + carried[:, at] * halves(grown, k, lanes) + skip_ref[:, at] * x_pair
        y_ref[:, at] = y
        gated_ref[:, at] = y * silu_gate[:, at]
        scaled.append(x_pair * halves(keep, k, lanes))
    passed = spread(jnp.exp(last) * aux[0:1, 6:7], pairs, lanes[0:1])
    state_ref[...] = state * passed + rough(b, jnp.concatenate(scaled, axis=1), ROWS)


def ssd_backward_kernel(
    mixed_ref,
    before_ref,
    aux_ref,
    seg_ref,
    conv_ref,
    head_ref,
    skip_ref,
    y_ref,
    enter_ref,
    grad_ref,
    qkv_ref,
    out_ref,
    conv_grad_ref,
    head_grad_ref,
    skip_grad_ref,
    ext_ref,
    next_ref,
    col_ref,
    state_ref,
):
    per, width = y_ref.shape
    pairs = width // 128
    channels = width + 2 * STATE

    @pl.when(pl.program_id(1) == 0)
    def _():
        state_ref[...] = jnp.zeros_like(state_ref)
        next_ref[...] = jnp.zeros_like(next_ref)

    @pl.when((pl.program_id(0) == 0) & (pl.program_id(1) == 0))
    def _():
        conv_grad_ref[...] = jnp.zeros_like(conv_grad_ref)
        head_grad_ref[...] = jnp.zeros_like(head_grad_ref)
        skip_grad_ref[...] = jnp.zeros_like(skip_grad_ref)
        col_ref[...] = jnp.zeros_like(col_ref)

    aux, total, sig, shifted, step, rate, tril, cum = block_start(
        mixed_ref, before_ref, aux_ref, conv_ref, head_ref, ext_ref, width
    )
    conv = total * sig
    x = conv[:, :width]
    b = conv[:, width : width + STATE].astype(bf16)
    c = conv[:, width + STATE :].astype(bf16)
    lanes = lax.broadcasted_iota(jnp.int32, (per, 128), 1)
    mask = (tril > 0) & (aux[:, 0:1] == seg_ref[0])
    both = rough(c, b, LAST)
    cum_t, step_t = cum.T, step.T
    enter = enter_ref[0]
    growth = jnp.exp(cum) * aux[:, 4:5]
    last = cum[per - 1 : per]
    fade = jnp.exp(last - cum) * aux[:, 5:6]
    keep = fade * step
    passed_row = jnp.exp(last) * aux[0:1, 6:7]

    gate = mixed_ref[:, :width]
    gate_sig = jax.nn.sigmoid(gate)
    grad = grad_ref[...]
    dy = grad * gate * gate_sig
    out_ref[:, :width] = (
        grad * y_ref[...] * (gate_sig * (1.0 + gate * (1.0 - gate_sig)))
    ).astype(bf16)

    d_out = state_ref[...]
    wide_growth = spread(growth, pairs, lanes)
    wide_keep = spread(keep, pairs, lanes)
    carried = rough(c, enter)
    dq = dy * wide_growth
    d_c = rough(dq, enter, LAST)
    xk = x * wide_keep
    d_b = rough(xk, d_out, LAST)
    dxk = rough(b, d_out)
    of_head = (
        lax.broadcasted_iota(jnp.int32, (width, 128), 0) // HEAD_DIM
        == lax.broadcasted_iota(jnp.int32, (width, 128), 1)
    ).astype(f32)
    d_growth = counted(of_head, dq * carried, first=False)
    d_keep = counted(of_head, dxk * x, first=False)
    d_passed = jnp.sum(d_out * enter.astype(f32), axis=0, keepdims=True)
    d_passed = counted(of_head, jnp.broadcast_to(d_passed, (16, width)), first=False)[0:1]
    d_x = dxk * wide_keep + dy * skip_ref[...]
    skip_grad_ref[0:1] += jnp.sum(dy * x, axis=0, keepdims=True)
    state_ref[...] = d_out * spread(passed_row, pairs, lanes[0:1]) + rough(c, dq, ROWS)

    d_both = jnp.zeros((per, per), f32)
    row_sums = jnp.zeros((per, 128), f32)
    within = []
    for k in range(pairs):
        at = slice(128 * k, 128 * k + 128)
        x_low = x[:, at].astype(bf16)
        dy_pair = dy[:, at]
        dy_low = dy_pair.astype(bf16)
        sides = []
        for h in (2 * k, 2 * k + 1):
            mine = (lanes >= HEAD_DIM) if h % 2 else (lanes < HEAD_DIM)
            gap = jnp.where(mask, cum[:, h : h + 1] - cum_t[h : h + 1], -1e30)
            level = jnp.exp(gap)
            step_row = step_t[h : h + 1]
            weighted = level * step_row
            sides.append(rough(both * weighted, dy_low, ROWS))
            d_mix = rough(jnp.where(mine, dy_pair, 0.0), x_low, LAST)
            d_both = d_both + d_mix * weighted
            flow = d_mix * both * level
            col_ref[h : h + 1] = jnp.sum(flow, axis=0, keepdims=True)
            row_sum = jnp.sum(flow * step_row, axis=1, keepdims=True)
            row_sums = jnp.where(lanes == h, row_sum, row_sums)
        within.append(jnp.where(lanes < HEAD_DIM, sides[0], sides[1]))
    d_x = d_x + jnp.concatenate(within, axis=1)
    d_c = d_c + rough(d_both, b)
    d_b = d_b + rough(d_both, c, ROWS)
    col_sums = col_ref[...].T
    d_step = col_sums + d_keep * fade
    kept = d_keep * keep
    d_cum = row_sums - col_sums * step + d_growth - kept
    d_last = jnp.sum(kept, axis=0, keepdims=True) + d_passed * passed_row
    at_end = lax.broadcasted_iota(jnp.int32, (per, 128), 0) == per - 1
    d_cum = d_cum + jnp.where(at_end, d_last, 0.0)
    d_decay = counted(tril, d_cum, ROWS)
    d_step = d_step + d_decay * rate
    d_shifted = d_step * jax.nn.sigmoid(shifted)
    head_grad_ref[0:1] += jnp.sum(d_decay * step, axis=0, keepdims=True) * rate
    head_grad_ref[1:2] += jnp.sum(d_shifted, axis=0, keepdims=True)
    out_ref[:, width + channels : width + channels + DT_PAD] = d_shifted.astype(bf16)
    out_ref[:, width + channels + DT_PAD :] = qkv_ref[...]

    d_conv = jnp.concatenate([d_x, d_b, d_c], axis=1)
    d_total = d_conv * (sig * (1.0 + total * (1.0 - sig)))
    conv_grad_ref[4:5] += jnp.sum(d_total, axis=0, keepdims=True)
    conv_grad_ref[3:4] += jnp.sum(d_total * ext_ref[8 : 8 + per], axis=0, keepdims=True)
    for back in range(1, CONV):
        conv_grad_ref[3 - back : 4 - back] += jnp.sum(
            d_total * aux[:, back : back + 1] * ext_ref[8 - back : 8 - back + per],
            axis=0,
            keepdims=True,
        )
    d_in = d_total * conv_ref[3:4]
    for back in range(1, CONV):
        masked = d_total * aux[:, back : back + 1]
        ext_ref[0:per] = masked
        ext_ref[per : per + 8] = next_ref[back - 1]
        d_in = d_in + ext_ref[back : back + per] * conv_ref[3 - back : 4 - back]
        next_ref[back - 1] = masked[0:8]
    out_ref[:, width : width + channels] = d_in.astype(bf16)


def ssd_specs(n, micro, per, width, used, order):
    eighths = per // 8
    return [
        pl.BlockSpec((per, used), lambda m, k: (order(k) * micro + m, 0)),
        pl.BlockSpec(
            (8, used),
            lambda m, k: (
                (jnp.maximum(order(k) - 1, 0) * micro + m) * eighths + eighths - 1,
                0,
            ),
        ),
        pl.BlockSpec((per, 8), lambda m, k: (order(k) * micro + m, 0)),
        pl.BlockSpec((1, 1, per), lambda m, k: (order(k) * micro + m, 0, 0)),
        pl.BlockSpec((8, width + 2 * STATE), lambda m, k: (0, 0)),
        pl.BlockSpec((8, DT_PAD), lambda m, k: (0, 0)),
        pl.BlockSpec((1, width), lambda m, k: (0, 0)),
    ]


def ssd_forward(mixed, aux, seg_rows, conv_rows, head_rows, skip_row, n, micro):
    rows = mixed.shape[0]
    per = rows // (n * micro)
    width = skip_row.shape[1]
    channels = width + 2 * STATE
    used = width + channels + DT_PAD
    specs = ssd_specs(n, micro, per, width, used, lambda k: k)
    by_block = pl.BlockSpec((per, width), lambda m, k: (k * micro + m, 0))
    return pl.pallas_call(
        ssd_forward_kernel,
        grid=(micro, n),
        out_shape=(
            jax.ShapeDtypeStruct((rows, width), f32),
            jax.ShapeDtypeStruct((rows, width), f32),
            jax.ShapeDtypeStruct((n * micro, STATE, width), bf16),
        ),
        in_specs=specs,
        out_specs=(
            by_block,
            by_block,
            pl.BlockSpec((1, STATE, width), lambda m, k: (k * micro + m, 0, 0)),
        ),
        scratch_shapes=[
            pltpu.VMEM((per + 8, channels), f32),
            pltpu.VMEM((STATE, width), f32),
        ],
        compiler_params=pltpu.CompilerParams(vmem_limit_bytes=40 * 1024 * 1024),
        cost_estimate=about(20),
    )(mixed, mixed, aux, seg_rows, conv_rows, head_rows, skip_row)


def ssd_backward(
    mixed, aux, seg_rows, conv_rows, head_rows, skip_row, y, enter, grad, qkv, n, micro
):
    rows = mixed.shape[0]
    per = rows // (n * micro)
    width = skip_row.shape[1]
    channels = width + 2 * STATE
    used = width + channels + DT_PAD

    def order(k):
        return n - 1 - k

    specs = ssd_specs(n, micro, per, width, used, order)
    by_block = pl.BlockSpec((per, width), lambda m, k: (order(k) * micro + m, 0))
    return pl.pallas_call(
        ssd_backward_kernel,
        grid=(micro, n),
        out_shape=(
            jax.ShapeDtypeStruct(mixed.shape, bf16),
            jax.ShapeDtypeStruct((8, channels), f32),
            jax.ShapeDtypeStruct((8, DT_PAD), f32),
            jax.ShapeDtypeStruct((8, width), f32),
        ),
        in_specs=specs
        + [
            by_block,
            pl.BlockSpec((1, STATE, width), lambda m, k: (order(k) * micro + m, 0, 0)),
            by_block,
            pl.BlockSpec((per, qkv.shape[1]), lambda m, k: (order(k) * micro + m, 0)),
        ],
        out_specs=(
            pl.BlockSpec((per, mixed.shape[1]), lambda m, k: (order(k) * micro + m, 0)),
            pl.BlockSpec((8, channels), lambda m, k: (0, 0)),
            pl.BlockSpec((8, DT_PAD), lambda m, k: (0, 0)),
            pl.BlockSpec((8, width), lambda m, k: (0, 0)),
        ),
        scratch_shapes=[
            pltpu.VMEM((per + 8, channels), f32),
            pltpu.VMEM((CONV - 1, 8, channels), f32),
            pltpu.VMEM((128, per), f32),
            pltpu.VMEM((STATE, width), f32),
        ],
        compiler_params=pltpu.CompilerParams(vmem_limit_bytes=40 * 1024 * 1024),
        cost_estimate=about(43),
    )(mixed, mixed, aux, seg_rows, conv_rows, head_rows, skip_row, y, enter, grad, qkv)


def turn(values, cosine, sine):
    half = ATT_DIM // 2
    swapped = jnp.concatenate([-values[:, half:], values[:, :half]], axis=1)
    return values * cosine + swapped * sine


def attention_start(k_ref, v_ref, table_ref, keys_ref, values_ref):
    blocks, per, _ = k_ref.shape
    for b in range(blocks):
        at = slice(b * per, b * per + per)
        keys_ref[at] = turn(k_ref[b], table_ref[b, :, :ATT_DIM], table_ref[b, :, ATT_DIM:]).astype(
            bf16
        )
        values_ref[at] = v_ref[b].astype(bf16)


def attention_probs(q_ref, q_table_ref, q_aux_ref, seg_ref, keys_ref):
    scale = ATT_DIM ** (-0.5)
    table = q_table_ref[0]
    queries = turn(q_ref[0], table[:, :ATT_DIM], table[:, ATT_DIM:]).astype(bf16)
    scores = rough(queries, keys_ref[...], LAST) * scale
    q_aux = q_aux_ref[0]
    positions = lax.broadcasted_iota(jnp.int32, scores.shape, 1)
    seen = (positions <= q_aux[:, 1:2].astype(jnp.int32)) & (q_aux[:, 0:1] == seg_ref[0])
    scores = jnp.where(seen, scores, -1e30)
    raised = jnp.exp(scores - jnp.max(scores, axis=1, keepdims=True))
    return queries, raised / jnp.sum(raised, axis=1, keepdims=True)


def attention_forward_kernel(
    q_ref, k_ref, v_ref, table_ref, q_table_ref, q_aux_ref, seg_ref, out_ref, keys_ref, values_ref
):
    @pl.when(pl.program_id(1) == 0)
    def _():
        attention_start(k_ref, v_ref, table_ref, keys_ref, values_ref)

    _, probs = attention_probs(q_ref, q_table_ref, q_aux_ref, seg_ref, keys_ref)
    out_ref[0] = rough(probs, values_ref[...]).astype(bf16)


def attention_backward_kernel(
    q_ref,
    k_ref,
    v_ref,
    table_ref,
    q_table_ref,
    q_aux_ref,
    seg_ref,
    grad_ref,
    q_grad_ref,
    k_grad_ref,
    v_grad_ref,
    keys_ref,
    values_ref,
    k_sum_ref,
    v_sum_ref,
):
    blocks, per, _ = k_ref.shape

    @pl.when(pl.program_id(1) == 0)
    def _():
        attention_start(k_ref, v_ref, table_ref, keys_ref, values_ref)
        k_sum_ref[...] = jnp.zeros_like(k_sum_ref)
        v_sum_ref[...] = jnp.zeros_like(v_sum_ref)

    scale = ATT_DIM ** (-0.5)
    queries, probs = attention_probs(q_ref, q_table_ref, q_aux_ref, seg_ref, keys_ref)
    grad = grad_ref[0]
    probs_grad = rough(grad, values_ref[...], LAST)
    along = jnp.sum(probs * probs_grad, axis=1, keepdims=True)
    scores_grad = (probs * (probs_grad - along)).astype(bf16)
    table = q_table_ref[0]
    q_grad = rough(scores_grad, keys_ref[...]) * scale
    q_grad_ref[0] = turn(q_grad, table[:, :ATT_DIM], -table[:, ATT_DIM:]).astype(bf16)
    k_sum_ref[...] += rough(scores_grad, queries, ROWS)
    v_sum_ref[...] += rough(probs, grad, ROWS)

    @pl.when(pl.program_id(1) == pl.num_programs(1) - 1)
    def _():
        for b in range(blocks):
            at = slice(b * per, b * per + per)
            k_grad_ref[b] = turn(
                k_sum_ref[at] * scale, table_ref[b, :, :ATT_DIM], -table_ref[b, :, ATT_DIM:]
            ).astype(bf16)
            v_grad_ref[b] = v_sum_ref[at].astype(bf16)


def attention_specs(n, micro, per, q_at, k_at, v_at):
    return [
        pl.BlockSpec((1, per, ATT_DIM), lambda m, k: (k, m, q_at)),
        pl.BlockSpec((n, per, ATT_DIM), lambda m, k: (0, m, k_at)),
        pl.BlockSpec((n, per, ATT_DIM), lambda m, k: (0, m, v_at)),
        pl.BlockSpec((n, per, 2 * ATT_DIM), lambda m, k: (0, 0, 0)),
        pl.BlockSpec((1, per, 2 * ATT_DIM), lambda m, k: (k, 0, 0)),
        pl.BlockSpec((1, per, 8), lambda m, k: (k, m, 0)),
        pl.BlockSpec((1, 1, n * per), lambda m, k: (m, 0, 0)),
    ]


def attention_forward(q, mixed, table, q_table, q_aux, seg, q_at, k_at):
    n, both, _ = mixed.shape
    micro = seg.shape[0]
    per = both // micro
    block = pl.BlockSpec((1, per, ATT_DIM), lambda m, k: (k, m, 0))
    return pl.pallas_call(
        attention_forward_kernel,
        grid=(micro, q_table.shape[0]),
        out_shape=jax.ShapeDtypeStruct((q_table.shape[0], both, ATT_DIM), bf16),
        in_specs=attention_specs(n, micro, per, q_at, k_at, k_at + 1),
        out_specs=block,
        scratch_shapes=[pltpu.VMEM((n * per, ATT_DIM), bf16)] * 2,
        compiler_params=pltpu.CompilerParams(vmem_limit_bytes=40 * 1024 * 1024),
        cost_estimate=about(14),
    )(q, mixed, mixed, table, q_table, q_aux, seg)


def attention_backward(q, mixed, table, q_table, q_aux, seg, grad, q_at, k_at):
    n, both, _ = mixed.shape
    micro = seg.shape[0]
    per = both // micro
    block = pl.BlockSpec((1, per, ATT_DIM), lambda m, k: (k, m, 0))
    whole = pl.BlockSpec((n, per, ATT_DIM), lambda m, k: (0, m, 0))
    return pl.pallas_call(
        attention_backward_kernel,
        grid=(micro, q_table.shape[0]),
        out_shape=(
            jax.ShapeDtypeStruct((q_table.shape[0], both, ATT_DIM), bf16),
            jax.ShapeDtypeStruct((n, both, ATT_DIM), bf16),
            jax.ShapeDtypeStruct((n, both, ATT_DIM), bf16),
        ),
        in_specs=attention_specs(n, micro, per, q_at, k_at, k_at + 1) + [block],
        out_specs=(block, whole, whole),
        scratch_shapes=[pltpu.VMEM((n * per, ATT_DIM), bf16)] * 2
        + [pltpu.VMEM((n * per, ATT_DIM), f32)] * 2,
        compiler_params=pltpu.CompilerParams(vmem_limit_bytes=40 * 1024 * 1024),
        cost_estimate=about(19),
    )(q, mixed, mixed, table, q_table, q_aux, seg, grad)


def ffn_kernel(rows_ref, weight_ref, turned_ref, grad_ref, act_ref, gate_grad_ref, back_ref):
    half = grad_ref.shape[1]
    values = rough(rows_ref[...], weight_ref[...])
    gate, up = values[:, :half], values[:, half:]
    grad = grad_ref[...]
    sig = jax.nn.sigmoid(gate)
    silu = gate * sig
    act_ref[...] = (silu * up).astype(bf16)
    gate_grad_ref[:, :half] = (grad * up * (sig * (1.0 + gate * (1.0 - sig)))).astype(bf16)
    gate_grad_ref[:, half:] = (grad * silu).astype(bf16)
    back_ref[...] = rough(gate_grad_ref[...], turned_ref[...]).astype(bf16)


def ffn_both(rows, weight, turned_weight, act_grad):
    count, depth = rows.shape
    block, wide = 256, weight.shape[1]

    def by_block(columns):
        return pl.BlockSpec((block, columns), lambda k: (k, 0))

    def whole(array):
        return pl.BlockSpec(array.shape, lambda k: (0, 0))

    return pl.pallas_call(
        ffn_kernel,
        grid=(count // block,),
        out_shape=(
            jax.ShapeDtypeStruct((count, wide // 2), bf16),
            jax.ShapeDtypeStruct((count, wide), bf16),
            jax.ShapeDtypeStruct((count, depth), bf16),
        ),
        in_specs=[by_block(depth), whole(weight), whole(turned_weight), by_block(wide // 2)],
        out_specs=(by_block(wide // 2), by_block(wide), by_block(depth)),
        compiler_params=pltpu.CompilerParams(vmem_limit_bytes=48 * 1024 * 1024),
        cost_estimate=about(22),
    )(rows, weight, turned_weight, act_grad)


def local(
    tokens,
    doc_ends,
    input_gain,
    mixer_in,
    conv_weight,
    conv_bias,
    head_params,
    mixer_gain,
    mixer_out,
    attn_qkv,
    attn_out,
    ffn_gain,
    gate_up,
    down_proj,
    out_grad,
):
    n = lax.axis_size("seq")
    nd = lax.axis_size("dp")
    s = lax.axis_index("seq")
    d = lax.axis_index("dp")
    micro, _, per, _ = tokens.shape
    own = micro * per
    length = n * per
    rows = n * own
    owner = mixer_in.shape[0]
    inner = INNER // n
    width = -(-inner // 128) * 128
    heads = HEADS // n
    ffl = FF // n
    parts = n // ATT_HEADS
    group = ATT_HEADS // KV_HEADS
    conv_ch = INNER + 2 * STATE

    def mixed_order(value):
        if value.ndim == 1:
            return jnp.swapaxes(value.reshape(n, nd, owner), 0, 1).reshape(D)
        return regrouped(value, n, nd, owner)

    def plain_order(value):
        if value.ndim == 1:
            return jnp.swapaxes(value.reshape(nd, n, owner), 0, 1).reshape(D)
        return regrouped(value, nd, n, owner)

    def widened(value):
        return jnp.pad(value, [(0, 0)] * (value.ndim - 1) + [(0, width - inner)])

    def from_seq(value):
        return value.reshape(micro, n, per, -1).transpose(1, 0, 2, 3).reshape(rows, -1)

    def gathered(value):
        return lax.all_gather(value, "seq", axis=0, tiled=True)

    def scattered(value, *others):
        total = lax.psum_scatter(value.astype(bf16), "seq", scatter_dimension=0, tiled=True)
        return (after(total, *others) if others else total).astype(f32)

    token_b = mixed_order(tokens.reshape(own, D))
    token_rows = token_b.astype(f32)
    grad_rows = mixed_order(out_grad.reshape(own, D))

    tap_count = conv_weight.shape[1]
    small_own = jnp.concatenate(
        [input_gain, conv_weight.reshape(-1), conv_bias, mixer_gain, ffn_gain]
    )
    small_count = small_own.shape[0]
    small_cols = -(-small_count // owner)
    small_own = jnp.pad(small_own, (0, small_cols * owner - small_count)).reshape(owner, small_cols)

    steps_own = jnp.pad(
        jnp.concatenate(
            [
                mixer_in[:, 2 * INNER + 2 * STATE :].reshape(owner, n, heads).transpose(1, 0, 2),
                jnp.broadcast_to(small_own[None], (n,) + small_own.shape),
            ],
            axis=2,
        ),
        ((0, 0), (0, 0), (0, DT_PAD - heads - small_cols)),
    )
    q_of = [k // parts for k in range(n)]
    kv_of = [ATT_HEADS + q // group for q in q_of]
    sizes = [width, width, 2 * STATE, DT_PAD, ATT_DIM, ATT_DIM, ATT_DIM]
    starts = [sum(sizes[:k]) for k in range(len(sizes) + 1)]
    every = slice(None)
    moves = []
    for k in range(n):
        for which, source, target, wide in (
            (0, k * inner, starts[0], inner),
            (0, INNER + k * inner, starts[1], inner),
            (0, 2 * INNER, starts[2], 2 * STATE),
            (1, q_of[k] * ATT_DIM, starts[4], ATT_DIM),
            (1, kv_of[k] * ATT_DIM, starts[5], ATT_DIM),
            (1, (kv_of[k] + KV_HEADS) * ATT_DIM, starts[6], ATT_DIM),
        ):
            moves.append(
                (which, (every, slice(source, source + wide)), (k, every, slice(target, target + wide)))
            )
        moves.append((2, (k,), (k, every, slice(starts[3], starts[4]))))
        if width != inner:
            gap = slice(0, width - inner)
            for target in (starts[1], starts[2]):
                hole = slice(target - width + inner, target)
                moves.append((3, (every, gap), (k, every, hole)))
    blank = jnp.zeros((owner, 128), bf16)
    packed = assembled(
        (n, owner, starts[-1]), bf16, moves, mixer_in, attn_qkv, steps_own, blank
    )
    sent_in = exchanged(packed, "seq")
    positions = jnp.arange(length, dtype=jnp.int32)
    seg = jnp.stack([segment_of(positions, doc_ends[m, 0]) for m in range(micro)])

    blocks = seg.reshape(micro, n, per)
    columns = [seg.astype(f32)]
    for back in range(1, CONV):
        moved = jnp.pad(seg[:, : length - back], ((0, 0), (back, 0)), constant_values=-1)
        columns.append((moved == seg).astype(f32))
    prior = jnp.concatenate(
        [jnp.full((micro, 1), -1, jnp.int32), blocks[:, :-1, per - 1]], axis=1
    )
    last = blocks[:, :, per - 1]
    for flag in (
        blocks == prior[:, :, None],
        blocks == last[:, :, None],
        jnp.broadcast_to((last == prior)[:, :, None], blocks.shape),
        jnp.zeros_like(blocks),
    ):
        columns.append(flag.astype(f32).reshape(micro, length))
    aux = from_seq(jnp.stack(columns, axis=-1))
    seg_blocks = blocks.transpose(1, 0, 2).reshape(n * micro, 1, per).astype(f32)
    cosine, sine = rope_tables(positions)
    table = jnp.concatenate([cosine, sine], axis=1).reshape(n, per, 2 * ATT_DIM)
    part = s % parts

    def taken(value):
        if parts == 1:
            return value
        split = value.reshape(n // parts, parts, *value.shape[1:])
        return lax.dynamic_index_in_dim(split, part, 1, False)

    def put_back(value):
        if parts == 1:
            return value
        here = (jnp.arange(parts) == part).reshape(1, parts, 1, 1)
        return jnp.where(here, value[:, None], 0).reshape(n, *value.shape[1:])

    q_aux = jnp.stack(
        [seg.astype(f32), jnp.broadcast_to(positions.astype(f32), seg.shape)], axis=-1
    )
    q_aux = jnp.pad(from_seq(q_aux), ((0, 0), (0, 6))).reshape(n, own, 8)
    q_aux, q_table = taken(q_aux), taken(table)
    w_in = after(dp_gather(sent_in), aux, seg_blocks, table, q_aux)
    small = w_in[:, :, :, starts[3] + heads : starts[3] + heads + small_cols]
    small = jnp.swapaxes(small, 0, 1).reshape(n * nd, -1)[:, :small_count]
    w_in = w_in.reshape(D, starts[-1])
    gu_moves = []
    for k in range(n):
        for half in range(2):
            gu_moves.append(
                (
                    (every, slice(half * FF + k * ffl, half * FF + (k + 1) * ffl)),
                    (k, every, slice(half * ffl, (half + 1) * ffl)),
                )
            )
    gu_own = assembled(
        (n, owner, 2 * ffl), bf16, [(0, flat, cube) for flat, cube in gu_moves], gate_up
    )
    sent_gu = exchanged(after(gu_own, w_in), "seq")
    cuts = [owner, CONV * tap_count, tap_count, mixer_gain.shape[0], owner]
    at = [sum(cuts[:k]) for k in range(len(cuts) + 1)]
    small = small.astype(f32)
    gain_in = mixed_order(small[:, at[0] : at[1]].reshape(-1))
    taps = (
        small[:, at[1] : at[2]].reshape(-1, CONV, tap_count).transpose(1, 0, 2).reshape(CONV, -1)
    )
    shift = small[:, at[2] : at[3]].reshape(-1)
    gain_mix = widened(
        lax.dynamic_slice_in_dim(small[:, at[3] : at[4]].reshape(-1), s * inner, inner)
    )
    gain_ffn = mixed_order(small[:, at[4] : at[5]].reshape(-1))
    conv_rows = jnp.concatenate([taps, shift[None], jnp.zeros((3, conv_ch), f32)])
    conv_rows = jnp.concatenate(
        [
            widened(lax.dynamic_slice_in_dim(conv_rows, s * inner, inner, axis=1)),
            conv_rows[:, INNER:],
        ],
        axis=1,
    )
    head = lax.dynamic_slice_in_dim(head_params, s * heads, heads, axis=1)
    head_rows = jnp.pad(head, ((0, 5), (0, DT_PAD - heads)))
    skip_row = widened(jnp.repeat(head[2], HEAD_DIM)[None])

    token_all = gathered(after(token_b, sent_in))
    token_f32 = token_all.astype(f32)
    normed = (token_f32 * rms_row(token_f32) * gain_in).astype(bf16)
    grads = gathered(after(grad_rows, token_all, w_in))
    mixed = dot(normed, w_in)
    out_own = after(mixed_order(jnp.concatenate([mixer_out, attn_out])), w_in)
    out_cut = mixer_out.shape[0]
    if nd == 4 and out_cut % 16 == 0:
        pieces = [after(permuted(out_own, "dp", k), mixed) for k in range(1, nd)]
        w_mix, w_att = placed_pieces([out_own, *pieces], d, [0, out_cut, out_own.shape[0]])
    else:
        out_parts = dp_gather(out_own, forward=False)
        w_mix = out_parts[:, :out_cut].reshape(-1, D)
        w_att = out_parts[:, out_cut:].reshape(-1, D)
    w_mix = jnp.pad(w_mix, ((0, width - inner), (0, 0)))
    if parts > 1:
        other = permuted(w_att, "seq", 1)
        w_att = jnp.where(
            (s & 1) != 0, jnp.concatenate([other, w_att]), jnp.concatenate([w_att, other])
        )
    w_gu = dp_gather(after(sent_gu, mixed), forward=False).reshape(D, 2 * ffl)
    w_down = dp_gather(after(mixed_order(down_proj), mixed), forward=False).reshape(ffl, D)
    ssd_args = (mixed, aux, seg_blocks, conv_rows, head_rows, skip_row)
    y, gated, enter = ssd_forward(*ssd_args, n, micro)
    squares = row_sums(jnp.sum(gated * gated, axis=1)) / INNER
    r_mix = lax.rsqrt(squares + epsilon)[:, None]
    mixer_b = (gated * r_mix * gain_mix).astype(bf16)

    q_at = starts[4] // ATT_DIM
    mixed_blocks = mixed.reshape(n, own, starts[-1])
    queries, own_q_at = mixed_blocks, q_at
    if parts > 1:
        queries, own_q_at = taken(mixed_blocks[:, :, starts[4] : starts[5]]), 0
    q_aux = after(q_aux, sent_gu, gated)
    att_args = (queries, mixed_blocks, table, q_table, q_aux)
    att_args = att_args + (seg.astype(f32)[:, None],)
    attended_b = put_back(attention_forward(*att_args, own_q_at, q_at + 1)).reshape(rows, ATT_DIM)
    branch_b = jnp.concatenate([mixer_b, attended_b], axis=1)
    w_out = jnp.concatenate([w_mix, w_att])
    branches = dot(branch_b, w_out)
    branches = after(branches.astype(bf16), grads)
    hidden = token_rows + scattered(branches, w_gu, w_down)
    ffn_own = (hidden * rms_row(hidden) * gain_ffn).astype(bf16)
    ffn_in = gathered(ffn_own)

    act_grad = after(dot_t(grads, w_down), branches)
    turned_gu = after(w_gu.T, branches)
    activated_b, gate_grad, ffn_back = ffn_both(ffn_in, w_gu, turned_gu, act_grad)
    gu_total = cross(ffn_in, gate_grad).astype(bf16)
    down_total = cross(activated_b, grads).astype(bf16)
    ffn_in_grad = scattered(ffn_back, gu_total, down_total)

    def over_dp(total, forward, meanwhile=()):
        return dp_scatter(total.reshape(nd, n * owner, -1), forward, meanwhile).astype(bf16)

    def to_owners(part_sum):
        return exchanged(part_sum.reshape(n, owner, -1), "seq")

    gu_part = over_dp(gu_total, False)
    down_grad = dp_scatter(down_total.reshape(nd, -1, D), False)
    hidden_part, ffn_gain_grad = rms_back(ffn_in_grad, hidden, gain_ffn)
    hidden_grad = hidden_part + grad_rows.astype(f32)
    hidden_b = after(gathered(hidden_grad.astype(bf16)), gu_part, down_grad)
    gu_sum = to_owners(gu_part)

    ffn_out = after(dot(activated_b, w_down).astype(bf16), hidden_b)
    ffn_sum = scattered(ffn_out)
    layer_out = plain_order((hidden + ffn_sum).astype(bf16))

    branch_total = cross(branch_b, hidden_b).astype(bf16)
    mix_total, att_total = branch_total[:width], branch_total[width:]
    if parts > 1:
        half = att_total.shape[0] // 2
        low, high = att_total[:half], att_total[half:]
        odd = (s & 1) != 0
        other = permuted(jnp.where(odd, low, high), "seq", 1)
        att_total = (jnp.where(odd, high, low).astype(f32) + other.astype(f32)).astype(bf16)
    out_total = jnp.concatenate(
        [mix_total[:inner].reshape(nd, -1, D), att_total.reshape(nd, -1, D)], axis=1
    )
    out_sum = dp_scatter(out_total, False)

    branch_grad = dot_t(hidden_b, w_out)
    mix_grad = branch_grad[:, :width]
    scaled = mix_grad * gain_mix
    along = jnp.sum(scaled * gated, axis=1)
    along = along + permuted(along, "seq", 1)
    att_grad = taken(branch_grad[:, width:].astype(bf16).reshape(n, own, ATT_DIM))
    att_grad = after(att_grad, along)
    q_grad, k_grad, v_grad = attention_backward(*att_args, att_grad, own_q_at, q_at + 1)
    qkv_grad = jnp.concatenate([put_back(q_grad), k_grad, v_grad], axis=2).reshape(rows, -1)

    along = other_pairs(along)[:, None] / INNER
    mix_gain_grad = jnp.sum(mix_grad * gated * r_mix, axis=0)
    gated_grad = scaled * r_mix - gated * (r_mix * r_mix * r_mix) * along
    mixed_grad, conv_g, head_g, skip_g = ssd_backward(
        *ssd_args, y, enter, gated_grad, qkv_grad, n, micro
    )
    mixed_grad = after(mixed_grad, out_sum, gu_sum)

    def placed(value, full):
        whole = jnp.zeros(value.shape[:-1] + (full,), f32)
        return lax.dynamic_update_slice_in_dim(
            whole, value, s * value.shape[-1], axis=value.ndim - 1
        )

    def by_owner(value):
        return value.reshape(-1, n * nd, value.shape[-1] // (n * nd)).transpose(1, 0, 2)

    conv_full = jnp.concatenate(
        [placed(conv_g[: CONV + 1, :inner], INNER), conv_g[: CONV + 1, width:]], axis=1
    )
    vectors = [
        by_owner(conv_full),
        by_owner(placed(mix_gain_grad[:inner], INNER)[None]),
        by_owner(plain_order(ffn_gain_grad)[None]),
    ]
    vectors = jnp.concatenate([v.reshape(n * nd, -1) for v in vectors], axis=1)
    vector_count = vectors.shape[1]
    vector_cols = -(-vector_count // owner)
    vectors = jnp.pad(vectors, ((0, 0), (0, vector_cols * owner - vector_count)))
    vectors = vectors.reshape(n, nd, owner, vector_cols).transpose(1, 0, 2, 3)
    vectors = vectors.reshape(D, vector_cols)

    in_back = after(dot_t(mixed_grad, w_in).astype(bf16), ffn_sum)
    mixed_grad = after(mixed_grad, in_back)
    zx_total = cross(normed, mixed_grad[:, : starts[2]]).astype(bf16)
    at_steps, at_heads = starts[3] - starts[2], starts[4] - starts[2]
    spare = starts[-1] - starts[2] - at_steps - heads - vector_cols
    rest_total = cross(normed, mixed_grad[:, starts[2] :])
    rest_total = (
        rest_total + jnp.pad(vectors, ((0, 0), (at_steps + heads, spare)))
    ).astype(bf16)
    zx_part = over_dp(zx_total, True, (rest_total,))
    zx_sum = to_owners(zx_part)
    rest_sum = to_owners(over_dp(rest_total, True, (zx_total,)))
    gate_up_grad = assembled(
        (owner, 2 * FF), f32, [(0, cube, flat) for flat, cube in gu_moves], gu_sum
    )
    out_plain = plain_order(out_sum)
    mixer_out_grad = out_plain[: mixer_out.shape[0]]
    attn_out_grad = out_plain[mixer_out.shape[0] :]
    down_grad = plain_order(down_grad)
    normed_grad = scattered(
        in_back, gate_up_grad, mixer_out_grad, attn_out_grad, down_grad, layer_out
    )
    head_g = jnp.concatenate(
        [head_g[:2, :heads], skip_g[:1, :inner].reshape(1, heads, HEAD_DIM).sum(axis=2)]
    )
    head_g = after(placed(head_g, HEADS).reshape(-1), normed_grad)
    head_g = summed(head_g, ("dp",))
    head_g = head_g + permuted(head_g, "seq", 1)
    others = [head_g] + [permuted(head_g, "seq", by) for by in range(2, n, 2)]
    head_g = jnp.sum(jnp.stack(others)[jnp.arange(n // 2) ^ (s // 2)], axis=0)
    token_part, _ = rms_back(normed_grad, token_rows, gain_in)
    token_grad = plain_order(token_part + hidden_grad)
    zx_sum = after(zx_sum, token_grad, head_g)

    bc_sum = jnp.sum(rest_sum[:, :, :at_steps].astype(f32), axis=0)
    step_sum = (
        rest_sum[:, :, at_steps : at_steps + heads]
        .transpose(1, 0, 2)
        .reshape(owner, HEADS)
    )
    moves = []
    for k in range(n):
        for half in range(2):
            source = slice(half * width, half * width + inner)
            target = slice(half * INNER + k * inner, half * INNER + (k + 1) * inner)
            moves.append((0, (k, every, source), (every, target)))
    moves.append((1, (every, every), (every, slice(2 * INNER, 2 * INNER + 2 * STATE))))
    moves.append((2, (every, every), (every, slice(2 * INNER + 2 * STATE, PROJ))))
    mixer_in_grad = assembled((owner, PROJ), f32, moves, zx_sum, bc_sum, step_sum)
    head_sum = rest_sum[:, :, at_heads:].astype(f32)
    head_sum = [head_sum[:, :, k * ATT_DIM : (k + 1) * ATT_DIM] for k in range(3)]
    q_sum = head_sum[0].reshape(ATT_HEADS, parts, owner, ATT_DIM).sum(axis=1)
    k_sum = head_sum[1].reshape(KV_HEADS, n // KV_HEADS, owner, ATT_DIM).sum(axis=1)
    v_sum = head_sum[2].reshape(KV_HEADS, n // KV_HEADS, owner, ATT_DIM).sum(axis=1)
    attn_qkv_grad = (
        jnp.concatenate([q_sum, k_sum, v_sum]).transpose(1, 0, 2).reshape(owner, -1)
    )

    vectors = jnp.sum(
        rest_sum[:, :, at_steps + heads : at_steps + heads + vector_cols].astype(f32), axis=0
    ).reshape(-1)[:vector_count]
    ends = [(CONV + 1) * tap_count, (CONV + 1) * tap_count + mixer_gain.shape[0]]
    conv_own = vectors[: ends[0]].reshape(CONV + 1, tap_count)
    in_gain_grad = (
        jnp.sum(mixer_in.astype(f32) * mixer_in_grad, axis=1)
        + jnp.sum(attn_qkv.astype(f32) * attn_qkv_grad, axis=1)
    ) / input_gain.astype(f32)
    return (
        layer_out.reshape(micro, 1, per, D),
        token_grad.reshape(micro, 1, per, D),
        in_gain_grad,
        mixer_in_grad,
        conv_own[:CONV],
        conv_own[CONV],
        head_g.reshape(3, HEADS),
        vectors[ends[0] : ends[1]],
        mixer_out_grad,
        attn_qkv_grad,
        attn_out_grad,
        vectors[ends[1] :],
        gate_up_grad,
        down_grad,
    )


def solution(mesh):
    rows = P(("seq", "dp"), None)
    vector = P(("seq", "dp"))
    activations = P(None, "dp", "seq", None)
    return jax.shard_map(
        local,
        mesh=mesh,
        in_specs=(
            activations,
            P(None, "dp", None),
            vector,
            rows,
            P(None, ("seq", "dp")),
            vector,
            P(),
            vector,
            rows,
            rows,
            rows,
            vector,
            rows,
            rows,
            activations,
        ),
        out_specs=(
            activations,
            activations,
            vector,
            rows,
            P(None, ("seq", "dp")),
            vector,
            P(),
            vector,
            rows,
            rows,
            rows,
            vector,
            rows,
            rows,
        ),
        check_vma=False,
    )
```

```python
import jax
import jax.numpy as jnp
from jax import lax
from jax.experimental import pallas as pl
from jax.experimental.pallas import tpu as pltpu
from jax.sharding import PartitionSpec as P

D = 2048
FF = 4096
HEADS = 48
HEAD_DIM = 64
STATE = 256
ATT_HEADS = 8
KV_HEADS = 2
ATT_DIM = 128
INNER = HEADS * HEAD_DIM
CONV = 4
PROJ = 2 * INNER + 2 * STATE + HEADS
DT_PAD = 128

epsilon = 1e-05
rope_base = 10000.0
f32 = jnp.float32
bf16 = jnp.bfloat16


def after(value, *others):
    def nothing(*refs):
        pass

    return pl.pallas_call(
        nothing,
        out_shape=jax.ShapeDtypeStruct(value.shape, value.dtype),
        in_specs=[pl.BlockSpec(memory_space=pl.ANY)] * (1 + len(others)),
        out_specs=pl.BlockSpec(memory_space=pl.ANY),
        input_output_aliases={0: 0},
    )(value, *others)


def permuted(value, axis, by):
    pairs = [(i, i ^ by) for i in range(lax.axis_size(axis))]
    return lax.ppermute(value, axis, pairs)


def small_gather(value):
    rows = value[None]
    for axis in ("dp", "seq"):
        here = lax.axis_index(axis)
        by = 1
        while by < lax.axis_size(axis):
            other = permuted(rows, axis, by)
            upper = (here & by) != 0
            rows = jnp.where(
                upper, jnp.concatenate([other, rows]), jnp.concatenate([rows, other])
            )
            by *= 2
    return rows


def summed(value, axes):
    for axis in axes:
        by = 1
        while by < lax.axis_size(axis):
            value = value + permuted(value, axis, by)
            by *= 2
    return value


def exchanged(blocks, axis):
    return lax.all_to_all(blocks, axis, 0, 0, tiled=True)


def assembled(shape, kind, moves, *inputs):
    def kernel(*refs):
        out = refs[-1]
        for which, source, target in moves:
            out[target] = refs[which][source].astype(out.dtype)

    return pl.pallas_call(
        kernel,
        out_shape=jax.ShapeDtypeStruct(shape, kind),
        compiler_params=pltpu.CompilerParams(vmem_limit_bytes=40 * 1024 * 1024),
        cost_estimate=about(4),
    )(*inputs)


def about(microseconds):
    return pl.CostEstimate(
        flops=0, bytes_accessed=int(microseconds * 3.6e6), transcendentals=0
    )


def regrouped(value, outer, inner, width):
    rows, total = value.shape
    if width != 64 or outer % 2:
        split = value.reshape(rows, outer, inner, width)
        return jnp.swapaxes(split, 1, 2).reshape(rows, total)

    def kernel(in_ref, out_ref):
        for i in range(inner):
            for o in range(0, outer, 2):
                left = in_ref[:, (o * inner + i) * width : (o * inner + i + 1) * width]
                right = in_ref[:, ((o + 1) * inner + i) * width : ((o + 1) * inner + i + 1) * width]
                at = (i * outer + o) * width
                out_ref[:, at : at + 2 * width] = jnp.concatenate([left, right], axis=1)

    return pl.pallas_call(
        kernel,
        out_shape=jax.ShapeDtypeStruct(value.shape, value.dtype),
        compiler_params=pltpu.CompilerParams(vmem_limit_bytes=40 * 1024 * 1024),
        cost_estimate=about(2),
    )(value)


def dp_gather(value, forward=True):
    if lax.axis_size("dp") != 4:
        return lax.all_gather(value, "dp", axis=0)
    here = lax.axis_index("dp")
    half = value.shape[0] // 2
    one = permuted(value, "dp", 1)
    two = permuted(value, "dp", 2)
    if forward:
        three = jnp.concatenate([permuted(one[:half], "dp", 2), permuted(two[half:], "dp", 1)])
    else:
        three = permuted(value, "dp", 3)
    whole = jnp.zeros((4,) + value.shape, value.dtype)
    for k, piece in enumerate((value, one, two, three)):
        whole = lax.dynamic_update_index_in_dim(whole, piece, here ^ k, 0)
    return whole


def placed_pieces(pieces, here, cuts):
    count, (rows, width) = len(pieces), pieces[0].shape
    spans = list(zip(cuts[:-1], cuts[1:]))

    def kernel(here_ref, *refs):
        for k in range(count):
            owner = here_ref[0] ^ k
            for (low, high), out in zip(spans, refs[count:]):
                out[pl.ds(pl.multiple_of(owner * (high - low), 16), high - low)] = refs[k][low:high]

    return pl.pallas_call(
        kernel,
        out_shape=[
            jax.ShapeDtypeStruct((count * (high - low), width), pieces[0].dtype)
            for low, high in spans
        ],
        in_specs=[pl.BlockSpec(memory_space=pltpu.SMEM)]
        + [pl.BlockSpec(memory_space=pltpu.VMEM)] * count,
        out_specs=[pl.BlockSpec(memory_space=pltpu.VMEM)] * len(spans),
        compiler_params=pltpu.CompilerParams(vmem_limit_bytes=40 * 1024 * 1024),
        cost_estimate=about(2),
    )(here[None], *pieces)


def dp_scatter(total, forward=True, meanwhile=()):
    if lax.axis_size("dp") != 4:
        return lax.psum_scatter(total, "dp", scatter_dimension=0).astype(f32)
    here = lax.axis_index("dp")
    blocks = [lax.dynamic_index_in_dim(total, here ^ k, 0, False) for k in range(4)]
    if not forward:
        own = blocks[0].astype(f32)
        for k in range(1, 4):
            own = own + permuted(blocks[k], "dp", k).astype(f32)
        return own
    half = total.shape[1] // 2
    low, high = [b[:half] for b in blocks], [b[half:] for b in blocks]
    low_in = permuted(jnp.stack([low[1], low[3]]), "dp", 1)
    high_in = permuted(jnp.stack(high[2:]), "dp", 2)
    if meanwhile:
        low_in, high_in = after(low_in, *meanwhile), after(high_in, *meanwhile)
    low_in, high_in = low_in.astype(f32), high_in.astype(f32)
    low_on = (low[2].astype(f32) + low_in[1]).astype(bf16)
    high_on = (high[1].astype(f32) + high_in[1]).astype(bf16)
    low_own = low[0].astype(f32) + low_in[0] + permuted(low_on, "dp", 2).astype(f32)
    high_own = high[0].astype(f32) + high_in[0] + permuted(high_on, "dp", 1).astype(f32)
    return jnp.concatenate([low_own, high_own])


def row_sums(value):
    return other_pairs(value + permuted(value, "seq", 1))


def other_pairs(value):
    total = value
    for by in range(2, lax.axis_size("seq"), 2):
        total = total + permuted(value, "seq", by)
    return total


def segment_of(positions, end_points):
    counted = jnp.sum((end_points[None, :] <= positions[:, None]).astype(jnp.int32), axis=1)
    return jnp.where(positions < 0, -1, counted)


def rope_tables(positions):
    half = ATT_DIM // 2
    freqs = jnp.power(rope_base, -jnp.arange(half, dtype=f32) * (2.0 / ATT_DIM))
    angles = positions.astype(f32)[:, None] * freqs[None, :]
    cosine, sine = jnp.cos(angles), jnp.sin(angles)
    return jnp.concatenate([cosine, cosine], axis=1), jnp.concatenate([sine, sine], axis=1)


def rms_row(values):
    return lax.rsqrt(jnp.mean(values * values, axis=-1, keepdims=True) + epsilon)


def rms_back(grad, values, gain):
    r = rms_row(values)
    scaled = grad * gain
    along = jnp.mean(scaled * values, axis=-1, keepdims=True)
    return scaled * r - values * (r * r * r) * along, jnp.sum(grad * values * r, axis=0)


def dot(left, right):
    return jnp.dot(left, right, preferred_element_type=f32)


def dot_t(left, right):
    return lax.dot_general(left, right, (((1,), (1,)), ((), ())), preferred_element_type=f32)


def cross(left, right):
    return lax.dot_general(left, right, (((0,), (0,)), ((), ())), preferred_element_type=f32)


def halves(columns, pair, lanes):
    left, right = columns[:, 2 * pair : 2 * pair + 1], columns[:, 2 * pair + 1 : 2 * pair + 2]
    return jnp.where(lanes < HEAD_DIM, left, right)


def spread(columns, pairs, lanes):
    return jnp.concatenate([halves(columns, k, lanes) for k in range(pairs)], axis=1)


def counted(pattern, value, dims=(((1,), (0,)), ((), ())), terms=2, first=True):
    pattern = pattern.astype(bf16)
    total, rest = None, value
    for k in range(terms):
        term = rest.astype(bf16)
        pair = (pattern, term) if first else (term, pattern)
        part = lax.dot_general(*pair, dims, preferred_element_type=f32)
        total = part if total is None else total + part
        if k + 1 < terms:
            rest = rest - term.astype(f32)
    return total


def rough(left, right, dims=(((1,), (0,)), ((), ()))):
    return lax.dot_general(
        left.astype(bf16), right.astype(bf16), dims, preferred_element_type=f32
    )


ROWS = (((0,), (0,)), ((), ()))
LAST = (((1,), (1,)), ((), ()))


def block_start(mixed_ref, before_ref, aux_ref, conv_ref, head_ref, ext_ref, width):
    per = mixed_ref.shape[0]
    channels = width + 2 * STATE
    ext_ref[0:8] = before_ref[:, width : width + channels].astype(bf16).astype(f32)
    ext_ref[8 : 8 + per] = mixed_ref[:, width : width + channels].astype(bf16).astype(f32)
    aux = aux_ref[...]
    total = conv_ref[4:5] + ext_ref[8 : 8 + per] * conv_ref[3:4]
    for back in range(1, CONV):
        total = total + ext_ref[8 - back : 8 - back + per] * (
            aux[:, back : back + 1] * conv_ref[3 - back : 4 - back]
        )
    sig = jax.nn.sigmoid(total)
    shifted = mixed_ref[:, width + channels : width + channels + DT_PAD] + head_ref[1:2]
    step = jnp.maximum(shifted, 0.0) + jnp.log1p(jnp.exp(-jnp.abs(shifted)))
    rate = -jnp.exp(head_ref[0:1])
    rows_at = lax.broadcasted_iota(jnp.int32, (per, per), 0)
    cols_at = lax.broadcasted_iota(jnp.int32, (per, per), 1)
    tril = (rows_at >= cols_at).astype(f32)
    cum = counted(tril, step * rate, terms=3)
    return aux, total, sig, shifted, step, rate, tril, cum


def ssd_forward_kernel(
    mixed_ref,
    before_ref,
    aux_ref,
    seg_ref,
    conv_ref,
    head_ref,
    skip_ref,
    y_ref,
    gated_ref,
    enter_ref,
    ext_ref,
    state_ref,
):
    per, width = y_ref.shape
    pairs = width // 128

    @pl.when(pl.program_id(1) == 0)
    def _():
        state_ref[...] = jnp.zeros_like(state_ref)

    aux, total, sig, _, step, _, tril, cum = block_start(
        mixed_ref, before_ref, aux_ref, conv_ref, head_ref, ext_ref, width
    )
    conv = total * sig
    x = conv[:, :width]
    b = conv[:, width : width + STATE].astype(bf16)
    c = conv[:, width + STATE :].astype(bf16)
    lanes = lax.broadcasted_iota(jnp.int32, (per, 128), 1)
    mask = (tril > 0) & (aux[:, 0:1] == seg_ref[0])
    both = rough(c, b, LAST)
    cum_t, step_t = cum.T, step.T
    state = state_ref[...]
    enter_ref[0] = state.astype(bf16)
    carried = rough(c, state)
    grown = jnp.exp(cum) * aux[:, 4:5]
    last = cum[per - 1 : per]
    keep = jnp.exp(last - cum) * aux[:, 5:6] * step
    gate = mixed_ref[:, :width]
    silu_gate = gate * jax.nn.sigmoid(gate)
    scaled = []
    for k in range(pairs):
        at = slice(128 * k, 128 * k + 128)
        x_pair = x[:, at]
        x_low = x_pair.astype(bf16)
        sides = []
        for h in (2 * k, 2 * k + 1):
            gap = jnp.where(mask, cum[:, h : h + 1] - cum_t[h : h + 1], -1e30)
            mixing = both * jnp.exp(gap) * step_t[h : h + 1]
            sides.append(rough(mixing, x_low))
        y = jnp.where(lanes < HEAD_DIM, sides[0], sides[1])
        y = y + carried[:, at] * halves(grown, k, lanes) + skip_ref[:, at] * x_pair
        y_ref[:, at] = y
        gated_ref[:, at] = y * silu_gate[:, at]
        scaled.append(x_pair * halves(keep, k, lanes))
    passed = spread(jnp.exp(last) * aux[0:1, 6:7], pairs, lanes[0:1])
    state_ref[...] = state * passed + rough(b, jnp.concatenate(scaled, axis=1), ROWS)


def ssd_backward_kernel(
    mixed_ref,
    before_ref,
    aux_ref,
    seg_ref,
    conv_ref,
    head_ref,
    skip_ref,
    y_ref,
    enter_ref,
    grad_ref,
    qkv_ref,
    out_ref,
    conv_grad_ref,
    head_grad_ref,
    skip_grad_ref,
    ext_ref,
    next_ref,
    col_ref,
    state_ref,
):
    per, width = y_ref.shape
    pairs = width // 128
    channels = width + 2 * STATE

    @pl.when(pl.program_id(1) == 0)
    def _():
        state_ref[...] = jnp.zeros_like(state_ref)
        next_ref[...] = jnp.zeros_like(next_ref)

    @pl.when((pl.program_id(0) == 0) & (pl.program_id(1) == 0))
    def _():
        conv_grad_ref[...] = jnp.zeros_like(conv_grad_ref)
        head_grad_ref[...] = jnp.zeros_like(head_grad_ref)
        skip_grad_ref[...] = jnp.zeros_like(skip_grad_ref)
        col_ref[...] = jnp.zeros_like(col_ref)

    aux, total, sig, shifted, step, rate, tril, cum = block_start(
        mixed_ref, before_ref, aux_ref, conv_ref, head_ref, ext_ref, width
    )
    conv = total * sig
    x = conv[:, :width]
    b = conv[:, width : width + STATE].astype(bf16)
    c = conv[:, width + STATE :].astype(bf16)
    lanes = lax.broadcasted_iota(jnp.int32, (per, 128), 1)
    mask = (tril > 0) & (aux[:, 0:1] == seg_ref[0])
    both = rough(c, b, LAST)
    cum_t, step_t = cum.T, step.T
    enter = enter_ref[0]
    growth = jnp.exp(cum) * aux[:, 4:5]
    last = cum[per - 1 : per]
    fade = jnp.exp(last - cum) * aux[:, 5:6]
    keep = fade * step
    passed_row = jnp.exp(last) * aux[0:1, 6:7]

    gate = mixed_ref[:, :width]
    gate_sig = jax.nn.sigmoid(gate)
    grad = grad_ref[...]
    dy = grad * gate * gate_sig
    out_ref[:, :width] = (
        grad * y_ref[...] * (gate_sig * (1.0 + gate * (1.0 - gate_sig)))
    ).astype(bf16)

    d_out = state_ref[...]
    wide_growth = spread(growth, pairs, lanes)
    wide_keep = spread(keep, pairs, lanes)
    carried = rough(c, enter)
    dq = dy * wide_growth
    d_c = rough(dq, enter, LAST)
    xk = x * wide_keep
    d_b = rough(xk, d_out, LAST)
    dxk = rough(b, d_out)
    of_head = (
        lax.broadcasted_iota(jnp.int32, (width, 128), 0) // HEAD_DIM
        == lax.broadcasted_iota(jnp.int32, (width, 128), 1)
    ).astype(f32)
    d_growth = counted(of_head, dq * carried, first=False)
    d_keep = counted(of_head, dxk * x, first=False)
    d_passed = jnp.sum(d_out * enter.astype(f32), axis=0, keepdims=True)
    d_passed = counted(of_head, jnp.broadcast_to(d_passed, (16, width)), first=False)[0:1]
    d_x = dxk * wide_keep + dy * skip_ref[...]
    skip_grad_ref[0:1] += jnp.sum(dy * x, axis=0, keepdims=True)
    state_ref[...] = d_out * spread(passed_row, pairs, lanes[0:1]) + rough(c, dq, ROWS)

    d_both = jnp.zeros((per, per), f32)
    row_sums = jnp.zeros((per, 128), f32)
    within = []
    for k in range(pairs):
        at = slice(128 * k, 128 * k + 128)
        x_low = x[:, at].astype(bf16)
        dy_pair = dy[:, at]
        dy_low = dy_pair.astype(bf16)
        sides = []
        for h in (2 * k, 2 * k + 1):
            mine = (lanes >= HEAD_DIM) if h % 2 else (lanes < HEAD_DIM)
            gap = jnp.where(mask, cum[:, h : h + 1] - cum_t[h : h + 1], -1e30)
            level = jnp.exp(gap)
            step_row = step_t[h : h + 1]
            weighted = level * step_row
            sides.append(rough(both * weighted, dy_low, ROWS))
            d_mix = rough(jnp.where(mine, dy_pair, 0.0), x_low, LAST)
            d_both = d_both + d_mix * weighted
            flow = d_mix * both * level
            col_ref[h : h + 1] = jnp.sum(flow, axis=0, keepdims=True)
            row_sum = jnp.sum(flow * step_row, axis=1, keepdims=True)
            row_sums = jnp.where(lanes == h, row_sum, row_sums)
        within.append(jnp.where(lanes < HEAD_DIM, sides[0], sides[1]))
    d_x = d_x + jnp.concatenate(within, axis=1)
    d_c = d_c + rough(d_both, b)
    d_b = d_b + rough(d_both, c, ROWS)
    col_sums = col_ref[...].T
    d_step = col_sums + d_keep * fade
    kept = d_keep * keep
    d_cum = row_sums - col_sums * step + d_growth - kept
    d_last = jnp.sum(kept, axis=0, keepdims=True) + d_passed * passed_row
    at_end = lax.broadcasted_iota(jnp.int32, (per, 128), 0) == per - 1
    d_cum = d_cum + jnp.where(at_end, d_last, 0.0)
    d_decay = counted(tril, d_cum, ROWS)
    d_step = d_step + d_decay * rate
    d_shifted = d_step * jax.nn.sigmoid(shifted)
    head_grad_ref[0:1] += jnp.sum(d_decay * step, axis=0, keepdims=True) * rate
    head_grad_ref[1:2] += jnp.sum(d_shifted, axis=0, keepdims=True)
    out_ref[:, width + channels : width + channels + DT_PAD] = d_shifted.astype(bf16)
    out_ref[:, width + channels + DT_PAD :] = qkv_ref[...]

    d_conv = jnp.concatenate([d_x, d_b, d_c], axis=1)
    d_total = d_conv * (sig * (1.0 + total * (1.0 - sig)))
    conv_grad_ref[4:5] += jnp.sum(d_total, axis=0, keepdims=True)
    conv_grad_ref[3:4] += jnp.sum(d_total * ext_ref[8 : 8 + per], axis=0, keepdims=True)
    for back in range(1, CONV):
        conv_grad_ref[3 - back : 4 - back] += jnp.sum(
            d_total * aux[:, back : back + 1] * ext_ref[8 - back : 8 - back + per],
            axis=0,
            keepdims=True,
        )
    d_in = d_total * conv_ref[3:4]
    for back in range(1, CONV):
        masked = d_total * aux[:, back : back + 1]
        ext_ref[0:per] = masked
        ext_ref[per : per + 8] = next_ref[back - 1]
        d_in = d_in + ext_ref[back : back + per] * conv_ref[3 - back : 4 - back]
        next_ref[back - 1] = masked[0:8]
    out_ref[:, width : width + channels] = d_in.astype(bf16)


def ssd_specs(n, micro, per, width, used, order):
    eighths = per // 8
    return [
        pl.BlockSpec((per, used), lambda m, k: (order(k) * micro + m, 0)),
        pl.BlockSpec(
            (8, used),
            lambda m, k: (
                (jnp.maximum(order(k) - 1, 0) * micro + m) * eighths + eighths - 1,
                0,
            ),
        ),
        pl.BlockSpec((per, 8), lambda m, k: (order(k) * micro + m, 0)),
        pl.BlockSpec((1, 1, per), lambda m, k: (order(k) * micro + m, 0, 0)),
        pl.BlockSpec((8, width + 2 * STATE), lambda m, k: (0, 0)),
        pl.BlockSpec((8, DT_PAD), lambda m, k: (0, 0)),
        pl.BlockSpec((1, width), lambda m, k: (0, 0)),
    ]


def ssd_forward(mixed, aux, seg_rows, conv_rows, head_rows, skip_row, n, micro):
    rows = mixed.shape[0]
    per = rows // (n * micro)
    width = skip_row.shape[1]
    channels = width + 2 * STATE
    used = width + channels + DT_PAD
    specs = ssd_specs(n, micro, per, width, used, lambda k: k)
    by_block = pl.BlockSpec((per, width), lambda m, k: (k * micro + m, 0))
    return pl.pallas_call(
        ssd_forward_kernel,
        grid=(micro, n),
        out_shape=(
            jax.ShapeDtypeStruct((rows, width), f32),
            jax.ShapeDtypeStruct((rows, width), f32),
            jax.ShapeDtypeStruct((n * micro, STATE, width), bf16),
        ),
        in_specs=specs,
        out_specs=(
            by_block,
            by_block,
            pl.BlockSpec((1, STATE, width), lambda m, k: (k * micro + m, 0, 0)),
        ),
        scratch_shapes=[
            pltpu.VMEM((per + 8, channels), f32),
            pltpu.VMEM((STATE, width), f32),
        ],
        compiler_params=pltpu.CompilerParams(vmem_limit_bytes=40 * 1024 * 1024),
        cost_estimate=about(20),
    )(mixed, mixed, aux, seg_rows, conv_rows, head_rows, skip_row)


def ssd_backward(
    mixed, aux, seg_rows, conv_rows, head_rows, skip_row, y, enter, grad, qkv, n, micro
):
    rows = mixed.shape[0]
    per = rows // (n * micro)
    width = skip_row.shape[1]
    channels = width + 2 * STATE
    used = width + channels + DT_PAD

    def order(k):
        return n - 1 - k

    specs = ssd_specs(n, micro, per, width, used, order)
    by_block = pl.BlockSpec((per, width), lambda m, k: (order(k) * micro + m, 0))
    return pl.pallas_call(
        ssd_backward_kernel,
        grid=(micro, n),
        out_shape=(
            jax.ShapeDtypeStruct(mixed.shape, bf16),
            jax.ShapeDtypeStruct((8, channels), f32),
            jax.ShapeDtypeStruct((8, DT_PAD), f32),
            jax.ShapeDtypeStruct((8, width), f32),
        ),
        in_specs=specs
        + [
            by_block,
            pl.BlockSpec((1, STATE, width), lambda m, k: (order(k) * micro + m, 0, 0)),
            by_block,
            pl.BlockSpec((per, qkv.shape[1]), lambda m, k: (order(k) * micro + m, 0)),
        ],
        out_specs=(
            pl.BlockSpec((per, mixed.shape[1]), lambda m, k: (order(k) * micro + m, 0)),
            pl.BlockSpec((8, channels), lambda m, k: (0, 0)),
            pl.BlockSpec((8, DT_PAD), lambda m, k: (0, 0)),
            pl.BlockSpec((8, width), lambda m, k: (0, 0)),
        ),
        scratch_shapes=[
            pltpu.VMEM((per + 8, channels), f32),
            pltpu.VMEM((CONV - 1, 8, channels), f32),
            pltpu.VMEM((128, per), f32),
            pltpu.VMEM((STATE, width), f32),
        ],
        compiler_params=pltpu.CompilerParams(vmem_limit_bytes=40 * 1024 * 1024),
        cost_estimate=about(43),
    )(mixed, mixed, aux, seg_rows, conv_rows, head_rows, skip_row, y, enter, grad, qkv)


def turn(values, cosine, sine):
    half = ATT_DIM // 2
    swapped = jnp.concatenate([-values[:, half:], values[:, :half]], axis=1)
    return values * cosine + swapped * sine


def attention_start(k_ref, v_ref, table_ref, keys_ref, values_ref):
    blocks, per, _ = k_ref.shape
    for b in range(blocks):
        at = slice(b * per, b * per + per)
        keys_ref[at] = turn(k_ref[b], table_ref[b, :, :ATT_DIM], table_ref[b, :, ATT_DIM:]).astype(
            bf16
        )
        values_ref[at] = v_ref[b].astype(bf16)


def attention_probs(q_ref, q_table_ref, q_aux_ref, seg_ref, keys_ref):
    scale = ATT_DIM ** (-0.5)
    table = q_table_ref[0]
    queries = turn(q_ref[0], table[:, :ATT_DIM], table[:, ATT_DIM:]).astype(bf16)
    scores = rough(queries, keys_ref[...], LAST) * scale
    q_aux = q_aux_ref[0]
    positions = lax.broadcasted_iota(jnp.int32, scores.shape, 1)
    seen = (positions <= q_aux[:, 1:2].astype(jnp.int32)) & (q_aux[:, 0:1] == seg_ref[0])
    scores = jnp.where(seen, scores, -1e30)
    raised = jnp.exp(scores - jnp.max(scores, axis=1, keepdims=True))
    return queries, raised / jnp.sum(raised, axis=1, keepdims=True)


def attention_forward_kernel(
    q_ref, k_ref, v_ref, table_ref, q_table_ref, q_aux_ref, seg_ref, out_ref, keys_ref, values_ref
):
    @pl.when(pl.program_id(1) == 0)
    def _():
        attention_start(k_ref, v_ref, table_ref, keys_ref, values_ref)

    _, probs = attention_probs(q_ref, q_table_ref, q_aux_ref, seg_ref, keys_ref)
    out_ref[0] = rough(probs, values_ref[...]).astype(bf16)


def attention_backward_kernel(
    q_ref,
    k_ref,
    v_ref,
    table_ref,
    q_table_ref,
    q_aux_ref,
    seg_ref,
    grad_ref,
    q_grad_ref,
    k_grad_ref,
    v_grad_ref,
    keys_ref,
    values_ref,
    k_sum_ref,
    v_sum_ref,
):
    blocks, per, _ = k_ref.shape

    @pl.when(pl.program_id(1) == 0)
    def _():
        attention_start(k_ref, v_ref, table_ref, keys_ref, values_ref)
        k_sum_ref[...] = jnp.zeros_like(k_sum_ref)
        v_sum_ref[...] = jnp.zeros_like(v_sum_ref)

    scale = ATT_DIM ** (-0.5)
    queries, probs = attention_probs(q_ref, q_table_ref, q_aux_ref, seg_ref, keys_ref)
    grad = grad_ref[0]
    probs_grad = rough(grad, values_ref[...], LAST)
    along = jnp.sum(probs * probs_grad, axis=1, keepdims=True)
    scores_grad = (probs * (probs_grad - along)).astype(bf16)
    table = q_table_ref[0]
    q_grad = rough(scores_grad, keys_ref[...]) * scale
    q_grad_ref[0] = turn(q_grad, table[:, :ATT_DIM], -table[:, ATT_DIM:]).astype(bf16)
    k_sum_ref[...] += rough(scores_grad, queries, ROWS)
    v_sum_ref[...] += rough(probs, grad, ROWS)

    @pl.when(pl.program_id(1) == pl.num_programs(1) - 1)
    def _():
        for b in range(blocks):
            at = slice(b * per, b * per + per)
            k_grad_ref[b] = turn(
                k_sum_ref[at] * scale, table_ref[b, :, :ATT_DIM], -table_ref[b, :, ATT_DIM:]
            ).astype(bf16)
            v_grad_ref[b] = v_sum_ref[at].astype(bf16)


def attention_specs(n, micro, per, q_at, k_at, v_at):
    return [
        pl.BlockSpec((1, per, ATT_DIM), lambda m, k: (k, m, q_at)),
        pl.BlockSpec((n, per, ATT_DIM), lambda m, k: (0, m, k_at)),
        pl.BlockSpec((n, per, ATT_DIM), lambda m, k: (0, m, v_at)),
        pl.BlockSpec((n, per, 2 * ATT_DIM), lambda m, k: (0, 0, 0)),
        pl.BlockSpec((1, per, 2 * ATT_DIM), lambda m, k: (k, 0, 0)),
        pl.BlockSpec((1, per, 8), lambda m, k: (k, m, 0)),
        pl.BlockSpec((1, 1, n * per), lambda m, k: (m, 0, 0)),
    ]


def attention_forward(q, mixed, table, q_table, q_aux, seg, q_at, k_at):
    n, both, _ = mixed.shape
    micro = seg.shape[0]
    per = both // micro
    block = pl.BlockSpec((1, per, ATT_DIM), lambda m, k: (k, m, 0))
    return pl.pallas_call(
        attention_forward_kernel,
        grid=(micro, q_table.shape[0]),
        out_shape=jax.ShapeDtypeStruct((q_table.shape[0], both, ATT_DIM), bf16),
        in_specs=attention_specs(n, micro, per, q_at, k_at, k_at + 1),
        out_specs=block,
        scratch_shapes=[pltpu.VMEM((n * per, ATT_DIM), bf16)] * 2,
        compiler_params=pltpu.CompilerParams(vmem_limit_bytes=40 * 1024 * 1024),
        cost_estimate=about(14),
    )(q, mixed, mixed, table, q_table, q_aux, seg)


def attention_backward(q, mixed, table, q_table, q_aux, seg, grad, q_at, k_at):
    n, both, _ = mixed.shape
    micro = seg.shape[0]
    per = both // micro
    block = pl.BlockSpec((1, per, ATT_DIM), lambda m, k: (k, m, 0))
    whole = pl.BlockSpec((n, per, ATT_DIM), lambda m, k: (0, m, 0))
    return pl.pallas_call(
        attention_backward_kernel,
        grid=(micro, q_table.shape[0]),
        out_shape=(
            jax.ShapeDtypeStruct((q_table.shape[0], both, ATT_DIM), bf16),
            jax.ShapeDtypeStruct((n, both, ATT_DIM), bf16),
            jax.ShapeDtypeStruct((n, both, ATT_DIM), bf16),
        ),
        in_specs=attention_specs(n, micro, per, q_at, k_at, k_at + 1) + [block],
        out_specs=(block, whole, whole),
        scratch_shapes=[pltpu.VMEM((n * per, ATT_DIM), bf16)] * 2
        + [pltpu.VMEM((n * per, ATT_DIM), f32)] * 2,
        compiler_params=pltpu.CompilerParams(vmem_limit_bytes=40 * 1024 * 1024),
        cost_estimate=about(19),
    )(q, mixed, mixed, table, q_table, q_aux, seg, grad)


def ffn_kernel(rows_ref, weight_ref, turned_ref, grad_ref, act_ref, gate_grad_ref, back_ref):
    half = grad_ref.shape[1]
    values = rough(rows_ref[...], weight_ref[...])
    gate, up = values[:, :half], values[:, half:]
    grad = grad_ref[...]
    sig = jax.nn.sigmoid(gate)
    silu = gate * sig
    act_ref[...] = (silu * up).astype(bf16)
    gate_grad_ref[:, :half] = (grad * up * (sig * (1.0 + gate * (1.0 - sig)))).astype(bf16)
    gate_grad_ref[:, half:] = (grad * silu).astype(bf16)
    back_ref[...] = rough(gate_grad_ref[...], turned_ref[...]).astype(bf16)


def ffn_both(rows, weight, turned_weight, act_grad):
    count, depth = rows.shape
    block, wide = 256, weight.shape[1]

    def by_block(columns):
        return pl.BlockSpec((block, columns), lambda k: (k, 0))

    def whole(array):
        return pl.BlockSpec(array.shape, lambda k: (0, 0))

    return pl.pallas_call(
        ffn_kernel,
        grid=(count // block,),
        out_shape=(
            jax.ShapeDtypeStruct((count, wide // 2), bf16),
            jax.ShapeDtypeStruct((count, wide), bf16),
            jax.ShapeDtypeStruct((count, depth), bf16),
        ),
        in_specs=[by_block(depth), whole(weight), whole(turned_weight), by_block(wide // 2)],
        out_specs=(by_block(wide // 2), by_block(wide), by_block(depth)),
        compiler_params=pltpu.CompilerParams(vmem_limit_bytes=48 * 1024 * 1024),
        cost_estimate=about(22),
    )(rows, weight, turned_weight, act_grad)


def local(
    tokens,
    doc_ends,
    input_gain,
    mixer_in,
    conv_weight,
    conv_bias,
    head_params,
    mixer_gain,
    mixer_out,
    attn_qkv,
    attn_out,
    ffn_gain,
    gate_up,
    down_proj,
    out_grad,
):
    n = lax.axis_size("seq")
    nd = lax.axis_size("dp")
    s = lax.axis_index("seq")
    d = lax.axis_index("dp")
    micro, _, per, _ = tokens.shape
    own = micro * per
    length = n * per
    rows = n * own
    owner = mixer_in.shape[0]
    inner = INNER // n
    width = -(-inner // 128) * 128
    heads = HEADS // n
    ffl = FF // n
    parts = n // ATT_HEADS
    group = ATT_HEADS // KV_HEADS
    conv_ch = INNER + 2 * STATE

    def mixed_order(value):
        if value.ndim == 1:
            return jnp.swapaxes(value.reshape(n, nd, owner), 0, 1).reshape(D)
        return regrouped(value, n, nd, owner)

    def plain_order(value):
        if value.ndim == 1:
            return jnp.swapaxes(value.reshape(nd, n, owner), 0, 1).reshape(D)
        return regrouped(value, nd, n, owner)

    def widened(value):
        return jnp.pad(value, [(0, 0)] * (value.ndim - 1) + [(0, width - inner)])

    def from_seq(value):
        return value.reshape(micro, n, per, -1).transpose(1, 0, 2, 3).reshape(rows, -1)

    def gathered(value):
        return lax.all_gather(value, "seq", axis=0, tiled=True)

    def scattered(value, *others):
        total = lax.psum_scatter(value.astype(bf16), "seq", scatter_dimension=0, tiled=True)
        return (after(total, *others) if others else total).astype(f32)

    token_b = mixed_order(tokens.reshape(own, D))
    token_rows = token_b.astype(f32)
    grad_rows = mixed_order(out_grad.reshape(own, D))

    tap_count = conv_weight.shape[1]
    small_own = jnp.concatenate(
        [input_gain, conv_weight.reshape(-1), conv_bias, mixer_gain, ffn_gain]
    )
    small_count = small_own.shape[0]
    small_cols = -(-small_count // owner)
    small_own = jnp.pad(small_own, (0, small_cols * owner - small_count)).reshape(owner, small_cols)

    steps_own = jnp.pad(
        jnp.concatenate(
            [
                mixer_in[:, 2 * INNER + 2 * STATE :].reshape(owner, n, heads).transpose(1, 0, 2),
                jnp.broadcast_to(small_own[None], (n,) + small_own.shape),
            ],
            axis=2,
        ),
        ((0, 0), (0, 0), (0, DT_PAD - heads - small_cols)),
    )
    q_of = [k // parts for k in range(n)]
    kv_of = [ATT_HEADS + q // group for q in q_of]
    sizes = [width, width, 2 * STATE, DT_PAD, ATT_DIM, ATT_DIM, ATT_DIM]
    starts = [sum(sizes[:k]) for k in range(len(sizes) + 1)]
    every = slice(None)
    sent_sizes = [width, width, STATE, DT_PAD, ATT_DIM, ATT_DIM]
    sent_at = [sum(sent_sizes[:k]) for k in range(len(sent_sizes) + 1)]
    moves = []
    for k in range(n):
        odd = k % 2
        for which, source, target, wide in (
            (0, k * inner, sent_at[0], inner),
            (0, INNER + k * inner, sent_at[1], inner),
            (0, 2 * INNER + odd * STATE, sent_at[2], STATE),
            (1, q_of[k] * ATT_DIM, sent_at[4], ATT_DIM),
            (1, (kv_of[k] + odd * KV_HEADS) * ATT_DIM, sent_at[5], ATT_DIM),
        ):
            moves.append(
                (which, (every, slice(source, source + wide)), (k, every, slice(target, target + wide)))
            )
        moves.append((2, (k,), (k, every, slice(sent_at[3], sent_at[4]))))
        if width != inner:
            gap = slice(0, width - inner)
            for target in (sent_at[1], sent_at[2]):
                hole = slice(target - width + inner, target)
                moves.append((3, (every, gap), (k, every, hole)))
    blank = jnp.zeros((owner, 128), bf16)
    packed = assembled(
        (n, owner, sent_at[-1]), bf16, moves, mixer_in, attn_qkv, steps_own, blank
    )
    sent_in = exchanged(packed, "seq")
    positions = jnp.arange(length, dtype=jnp.int32)
    seg = jnp.stack([segment_of(positions, doc_ends[m, 0]) for m in range(micro)])

    blocks = seg.reshape(micro, n, per)
    columns = [seg.astype(f32)]
    for back in range(1, CONV):
        moved = jnp.pad(seg[:, : length - back], ((0, 0), (back, 0)), constant_values=-1)
        columns.append((moved == seg).astype(f32))
    prior = jnp.concatenate(
        [jnp.full((micro, 1), -1, jnp.int32), blocks[:, :-1, per - 1]], axis=1
    )
    last = blocks[:, :, per - 1]
    for flag in (
        blocks == prior[:, :, None],
        blocks == last[:, :, None],
        jnp.broadcast_to((last == prior)[:, :, None], blocks.shape),
        jnp.zeros_like(blocks),
    ):
        columns.append(flag.astype(f32).reshape(micro, length))
    aux = from_seq(jnp.stack(columns, axis=-1))
    seg_blocks = blocks.transpose(1, 0, 2).reshape(n * micro, 1, per).astype(f32)
    cosine, sine = rope_tables(positions)
    table = jnp.concatenate([cosine, sine], axis=1).reshape(n, per, 2 * ATT_DIM)
    part = s % parts

    def taken(value):
        if parts == 1:
            return value
        split = value.reshape(n // parts, parts, *value.shape[1:])
        return lax.dynamic_index_in_dim(split, part, 1, False)

    def put_back(value):
        if parts == 1:
            return value
        here = (jnp.arange(parts) == part).reshape(1, parts, 1, 1)
        return jnp.where(here, value[:, None], 0).reshape(n, *value.shape[1:])

    q_aux = jnp.stack(
        [seg.astype(f32), jnp.broadcast_to(positions.astype(f32), seg.shape)], axis=-1
    )
    q_aux = jnp.pad(from_seq(q_aux), ((0, 0), (0, 6))).reshape(n, own, 8)
    q_aux, q_table = taken(q_aux), taken(table)
    w_half = dp_gather(sent_in)
    small = w_half[:, :, :, sent_at[3] + heads : sent_at[3] + heads + small_cols]
    small = jnp.swapaxes(small, 0, 1).reshape(n * nd, -1)[:, :small_count]
    w_half = w_half.reshape(D, sent_at[-1])
    w_cut = [w_half[:, sent_at[k] : sent_at[k + 1]] for k in range(6)]
    own_side = jnp.concatenate([w_cut[2], w_cut[5]], axis=1)
    other_side = permuted(own_side, "seq", 1)
    odd_place = (s & 1) != 0
    first_side = jnp.where(odd_place, other_side, own_side)
    second_side = jnp.where(odd_place, own_side, other_side)
    w_in = jnp.concatenate(
        [
            w_cut[0],
            w_cut[1],
            first_side[:, :STATE],
            second_side[:, :STATE],
            w_cut[3],
            w_cut[4],
            first_side[:, STATE:],
            second_side[:, STATE:],
        ],
        axis=1,
    )
    w_in = after(w_in, aux, seg_blocks, table, q_aux)
    gu_moves = []
    for k in range(n):
        for half in range(2):
            gu_moves.append(
                (
                    (every, slice(half * FF + k * ffl, half * FF + (k + 1) * ffl)),
                    (k, every, slice(half * ffl, (half + 1) * ffl)),
                )
            )
    gu_own = assembled(
        (n, owner, 2 * ffl), bf16, [(0, flat, cube) for flat, cube in gu_moves], gate_up
    )
    sent_gu = exchanged(after(gu_own, w_in), "seq")
    cuts = [owner, CONV * tap_count, tap_count, mixer_gain.shape[0], owner]
    at = [sum(cuts[:k]) for k in range(len(cuts) + 1)]
    small = small.astype(f32)
    gain_in = mixed_order(small[:, at[0] : at[1]].reshape(-1))
    taps = (
        small[:, at[1] : at[2]].reshape(-1, CONV, tap_count).transpose(1, 0, 2).reshape(CONV, -1)
    )
    shift = small[:, at[2] : at[3]].reshape(-1)
    gain_mix = widened(
        lax.dynamic_slice_in_dim(small[:, at[3] : at[4]].reshape(-1), s * inner, inner)
    )
    gain_ffn = mixed_order(small[:, at[4] : at[5]].reshape(-1))
    conv_rows = jnp.concatenate([taps, shift[None], jnp.zeros((3, conv_ch), f32)])
    conv_rows = jnp.concatenate(
        [
            widened(lax.dynamic_slice_in_dim(conv_rows, s * inner, inner, axis=1)),
            conv_rows[:, INNER:],
        ],
        axis=1,
    )
    head = lax.dynamic_slice_in_dim(head_params, s * heads, heads, axis=1)
    head_rows = jnp.pad(head, ((0, 5), (0, DT_PAD - heads)))
    skip_row = widened(jnp.repeat(head[2], HEAD_DIM)[None])

    token_all = gathered(after(token_b, sent_in))
    token_f32 = token_all.astype(f32)
    normed = (token_f32 * rms_row(token_f32) * gain_in).astype(bf16)
    grads = gathered(after(grad_rows, token_all, w_in))
    mixed = dot(normed, w_in)
    out_own = after(mixed_order(jnp.concatenate([mixer_out, attn_out])), w_in)
    out_cut = mixer_out.shape[0]
    if nd == 4 and out_cut % 16 == 0:
        pieces = [after(permuted(out_own, "dp", k), mixed) for k in range(1, nd)]
        w_mix, w_att = placed_pieces([out_own, *pieces], d, [0, out_cut, out_own.shape[0]])
    else:
        out_parts = dp_gather(out_own, forward=False)
        w_mix = out_parts[:, :out_cut].reshape(-1, D)
        w_att = out_parts[:, out_cut:].reshape(-1, D)
    w_mix = jnp.pad(w_mix, ((0, width - inner), (0, 0)))
    if parts > 1:
        other = permuted(w_att, "seq", 1)
        w_att = jnp.where(
            (s & 1) != 0, jnp.concatenate([other, w_att]), jnp.concatenate([w_att, other])
        )
    w_gu = dp_gather(after(sent_gu, mixed), forward=False).reshape(D, 2 * ffl)
    w_down = dp_gather(after(mixed_order(down_proj), mixed), forward=False).reshape(ffl, D)
    ssd_args = (mixed, aux, seg_blocks, conv_rows, head_rows, skip_row)
    y, gated, enter = ssd_forward(*ssd_args, n, micro)
    squares = row_sums(jnp.sum(gated * gated, axis=1)) / INNER
    r_mix = lax.rsqrt(squares + epsilon)[:, None]
    mixer_b = (gated * r_mix * gain_mix).astype(bf16)

    q_at = starts[4] // ATT_DIM
    mixed_blocks = mixed.reshape(n, own, starts[-1])
    queries, own_q_at = mixed_blocks, q_at
    if parts > 1:
        queries, own_q_at = taken(mixed_blocks[:, :, starts[4] : starts[5]]), 0
    q_aux = after(q_aux, sent_gu, gated)
    att_args = (queries, mixed_blocks, table, q_table, q_aux)
    att_args = att_args + (seg.astype(f32)[:, None],)
    attended_b = put_back(attention_forward(*att_args, own_q_at, q_at + 1)).reshape(rows, ATT_DIM)
    branch_b = jnp.concatenate([mixer_b, attended_b], axis=1)
    w_out = jnp.concatenate([w_mix, w_att])
    branches = dot(branch_b, w_out)
    branches = after(branches.astype(bf16), grads)
    hidden = token_rows + scattered(branches, w_gu, w_down)
    ffn_own = (hidden * rms_row(hidden) * gain_ffn).astype(bf16)
    ffn_in = gathered(ffn_own)

    act_grad = after(dot_t(grads, w_down), branches)
    turned_gu = after(w_gu.T, branches)
    activated_b, gate_grad, ffn_back = ffn_both(ffn_in, w_gu, turned_gu, act_grad)
    gu_total = cross(ffn_in, gate_grad).astype(bf16)
    down_total = cross(activated_b, grads).astype(bf16)
    ffn_in_grad = scattered(ffn_back, gu_total, down_total)

    def over_dp(total, forward, meanwhile=()):
        return dp_scatter(total.reshape(nd, n * owner, -1), forward, meanwhile).astype(bf16)

    def to_owners(part_sum):
        return exchanged(part_sum.reshape(n, owner, -1), "seq")

    gu_part = over_dp(gu_total, False)
    down_grad = dp_scatter(down_total.reshape(nd, -1, D), False)
    hidden_part, ffn_gain_grad = rms_back(ffn_in_grad, hidden, gain_ffn)
    hidden_grad = hidden_part + grad_rows.astype(f32)
    hidden_b = after(gathered(hidden_grad.astype(bf16)), gu_part, down_grad)
    gu_sum = to_owners(gu_part)

    ffn_out = after(dot(activated_b, w_down).astype(bf16), hidden_b)
    ffn_sum = lax.psum_scatter(ffn_out, "seq", scatter_dimension=0, tiled=True)
    layer_out = plain_order((hidden + ffn_sum.astype(f32)).astype(bf16))

    branch_total = cross(branch_b, hidden_b).astype(bf16)
    mix_total, att_total = branch_total[:width], branch_total[width:]
    if parts > 1:
        half = att_total.shape[0] // 2
        low, high = att_total[:half], att_total[half:]
        odd = (s & 1) != 0
        other = permuted(jnp.where(odd, low, high), "seq", 1)
        att_total = (jnp.where(odd, high, low).astype(f32) + other.astype(f32)).astype(bf16)
    out_total = jnp.concatenate(
        [mix_total[:inner].reshape(nd, -1, D), att_total.reshape(nd, -1, D)], axis=1
    )
    if nd == 4:
        out_blocks = [lax.dynamic_index_in_dim(out_total, d ^ k, 0, False) for k in range(nd)]
        out_pieces = [permuted(out_blocks[k], "dp", k) for k in range(1, nd)]
        out_sum = out_blocks[0].astype(f32)
        for piece in out_pieces:
            out_sum = out_sum + piece.astype(f32)
    else:
        out_sum = dp_scatter(out_total, False)
        out_pieces = [out_sum]

    branch_grad = dot_t(hidden_b, w_out)
    mix_grad = branch_grad[:, :width]
    scaled = mix_grad * gain_mix
    along = jnp.sum(scaled * gated, axis=1)
    along = along + permuted(along, "seq", 1)
    att_grad = taken(branch_grad[:, width:].astype(bf16).reshape(n, own, ATT_DIM))
    att_grad = after(att_grad, along)
    q_grad, k_grad, v_grad = attention_backward(*att_args, att_grad, own_q_at, q_at + 1)
    qkv_grad = jnp.concatenate([put_back(q_grad), k_grad, v_grad], axis=2).reshape(rows, -1)

    along = other_pairs(along)[:, None] / INNER
    mix_gain_grad = jnp.sum(mix_grad * gated * r_mix, axis=0)
    gated_grad = scaled * r_mix - gated * (r_mix * r_mix * r_mix) * along
    mixed_grad, conv_g, head_g, skip_g = ssd_backward(
        *ssd_args, y, enter, gated_grad, qkv_grad, n, micro
    )
    mixed_grad = after(mixed_grad, gu_sum, *out_pieces)

    def placed(value, full):
        whole = jnp.zeros(value.shape[:-1] + (full,), f32)
        return lax.dynamic_update_slice_in_dim(
            whole, value, s * value.shape[-1], axis=value.ndim - 1
        )

    def by_owner(value):
        return value.reshape(-1, n * nd, value.shape[-1] // (n * nd)).transpose(1, 0, 2)

    conv_full = jnp.concatenate(
        [placed(conv_g[: CONV + 1, :inner], INNER), conv_g[: CONV + 1, width:]], axis=1
    )
    vectors = [
        by_owner(conv_full),
        by_owner(placed(mix_gain_grad[:inner], INNER)[None]),
        by_owner(plain_order(ffn_gain_grad)[None]),
    ]
    vectors = jnp.concatenate([v.reshape(n * nd, -1) for v in vectors], axis=1)
    vector_count = vectors.shape[1]
    vector_cols = -(-vector_count // owner)
    vectors = jnp.pad(vectors, ((0, 0), (0, vector_cols * owner - vector_count)))
    vectors = vectors.reshape(n, nd, owner, vector_cols).transpose(1, 0, 2, 3)
    vectors = vectors.reshape(D, vector_cols)

    in_back = after(dot_t(mixed_grad, w_in).astype(bf16), ffn_sum)
    mixed_grad = after(mixed_grad, in_back)
    zx_total = cross(normed, mixed_grad[:, : starts[2]]).astype(bf16)
    at_steps, at_heads = starts[3] - starts[2], starts[4] - starts[2]
    spare = starts[-1] - starts[2] - at_steps - heads - vector_cols
    rest_total = cross(normed, mixed_grad[:, starts[2] :])
    rest_total = (
        rest_total + jnp.pad(vectors, ((0, 0), (at_steps + heads, spare)))
    ).astype(bf16)
    zx_part = over_dp(zx_total, True, (rest_total,))
    zx_sum = to_owners(zx_part)
    rest_sum = to_owners(over_dp(rest_total, True, (zx_total,)))
    gate_up_grad = assembled(
        (owner, 2 * FF), f32, [(0, cube, flat) for flat, cube in gu_moves], gu_sum
    )
    out_plain = plain_order(out_sum)
    mixer_out_grad = out_plain[: mixer_out.shape[0]]
    attn_out_grad = out_plain[mixer_out.shape[0] :]
    down_grad = plain_order(down_grad)
    normed_sum = lax.psum_scatter(in_back, "seq", scatter_dimension=0, tiled=True)
    normed_sum = after(
        normed_sum, gate_up_grad, mixer_out_grad, attn_out_grad, down_grad, layer_out
    )
    normed_grad = normed_sum.astype(f32)
    head_g = jnp.concatenate(
        [head_g[:2, :heads], skip_g[:1, :inner].reshape(1, heads, HEAD_DIM).sum(axis=2)]
    )
    head_g = after(placed(head_g, HEADS).reshape(-1), normed_sum)
    head_g = summed(head_g, ("dp",))
    head_g = head_g + permuted(head_g, "seq", 1)
    others = [head_g] + [permuted(head_g, "seq", by) for by in range(2, n, 2)]
    head_g = jnp.sum(jnp.stack(others)[jnp.arange(n // 2) ^ (s // 2)], axis=0)
    token_part, _ = rms_back(normed_grad, token_rows, gain_in)
    token_grad = plain_order(token_part + hidden_grad)
    zx_sum = after(zx_sum, token_grad, head_g)

    bc_sum = jnp.sum(rest_sum[:, :, :at_steps].astype(f32), axis=0)
    step_sum = (
        rest_sum[:, :, at_steps : at_steps + heads]
        .transpose(1, 0, 2)
        .reshape(owner, HEADS)
    )
    moves = []
    for k in range(n):
        for half in range(2):
            source = slice(half * width, half * width + inner)
            target = slice(half * INNER + k * inner, half * INNER + (k + 1) * inner)
            moves.append((0, (k, every, source), (every, target)))
    moves.append((1, (every, every), (every, slice(2 * INNER, 2 * INNER + 2 * STATE))))
    moves.append((2, (every, every), (every, slice(2 * INNER + 2 * STATE, PROJ))))
    mixer_in_grad = assembled((owner, PROJ), f32, moves, zx_sum, bc_sum, step_sum)
    head_sum = rest_sum[:, :, at_heads:].astype(f32)
    head_sum = [head_sum[:, :, k * ATT_DIM : (k + 1) * ATT_DIM] for k in range(3)]
    q_sum = head_sum[0].reshape(ATT_HEADS, parts, owner, ATT_DIM).sum(axis=1)
    k_sum = head_sum[1].reshape(KV_HEADS, n // KV_HEADS, owner, ATT_DIM).sum(axis=1)
    v_sum = head_sum[2].reshape(KV_HEADS, n // KV_HEADS, owner, ATT_DIM).sum(axis=1)
    attn_qkv_grad = (
        jnp.concatenate([q_sum, k_sum, v_sum]).transpose(1, 0, 2).reshape(owner, -1)
    )

    vectors = jnp.sum(
        rest_sum[:, :, at_steps + heads : at_steps + heads + vector_cols].astype(f32), axis=0
    ).reshape(-1)[:vector_count]
    ends = [(CONV + 1) * tap_count, (CONV + 1) * tap_count + mixer_gain.shape[0]]
    conv_own = vectors[: ends[0]].reshape(CONV + 1, tap_count)
    in_gain_grad = (
        jnp.sum(mixer_in.astype(f32) * mixer_in_grad, axis=1)
        + jnp.sum(attn_qkv.astype(f32) * attn_qkv_grad, axis=1)
    ) / input_gain.astype(f32)
    return (
        layer_out.reshape(micro, 1, per, D),
        token_grad.reshape(micro, 1, per, D),
        in_gain_grad,
        mixer_in_grad,
        conv_own[:CONV],
        conv_own[CONV],
        head_g.reshape(3, HEADS),
        vectors[ends[0] : ends[1]],
        mixer_out_grad,
        attn_qkv_grad,
        attn_out_grad,
        vectors[ends[1] :],
        gate_up_grad,
        down_grad,
    )


def solution(mesh):
    rows = P(("seq", "dp"), None)
    vector = P(("seq", "dp"))
    activations = P(None, "dp", "seq", None)
    return jax.shard_map(
        local,
        mesh=mesh,
        in_specs=(
            activations,
            P(None, "dp", None),
            vector,
            rows,
            P(None, ("seq", "dp")),
            vector,
            P(),
            vector,
            rows,
            rows,
            rows,
            vector,
            rows,
            rows,
            activations,
        ),
        out_specs=(
            activations,
            activations,
            vector,
            rows,
            P(None, ("seq", "dp")),
            vector,
            P(),
            vector,
            rows,
            rows,
            rows,
            vector,
            rows,
            rows,
        ),
        check_vma=False,
    )
```

```python
import jax
import jax.numpy as jnp
from jax import lax
from jax.experimental import pallas as pl
from jax.experimental.pallas import tpu as pltpu
from jax.sharding import PartitionSpec as P

D = 2048
FF = 4096
HEADS = 48
HEAD_DIM = 64
STATE = 256
ATT_HEADS = 8
KV_HEADS = 2
ATT_DIM = 128
INNER = HEADS * HEAD_DIM
CONV = 4
PROJ = 2 * INNER + 2 * STATE + HEADS
DT_PAD = 128

epsilon = 1e-05
rope_base = 10000.0
f32 = jnp.float32
bf16 = jnp.bfloat16


def after(value, *others):
    def nothing(*refs):
        pass

    return pl.pallas_call(
        nothing,
        out_shape=jax.ShapeDtypeStruct(value.shape, value.dtype),
        in_specs=[pl.BlockSpec(memory_space=pl.ANY)] * (1 + len(others)),
        out_specs=pl.BlockSpec(memory_space=pl.ANY),
        input_output_aliases={0: 0},
    )(value, *others)


def permuted(value, axis, by):
    pairs = [(i, i ^ by) for i in range(lax.axis_size(axis))]
    return lax.ppermute(value, axis, pairs)


def small_gather(value):
    rows = value[None]
    for axis in ("dp", "seq"):
        here = lax.axis_index(axis)
        by = 1
        while by < lax.axis_size(axis):
            other = permuted(rows, axis, by)
            upper = (here & by) != 0
            rows = jnp.where(
                upper, jnp.concatenate([other, rows]), jnp.concatenate([rows, other])
            )
            by *= 2
    return rows


def summed(value, axes):
    for axis in axes:
        by = 1
        while by < lax.axis_size(axis):
            value = value + permuted(value, axis, by)
            by *= 2
    return value


def exchanged(blocks, axis):
    return lax.all_to_all(blocks, axis, 0, 0, tiled=True)


def assembled(shape, kind, moves, *inputs):
    def kernel(*refs):
        out = refs[-1]
        for which, source, target in moves:
            out[target] = refs[which][source].astype(out.dtype)

    return pl.pallas_call(
        kernel,
        out_shape=jax.ShapeDtypeStruct(shape, kind),
        compiler_params=pltpu.CompilerParams(vmem_limit_bytes=40 * 1024 * 1024),
        cost_estimate=about(4),
    )(*inputs)


def about(microseconds):
    return pl.CostEstimate(
        flops=0, bytes_accessed=int(microseconds * 3.6e6), transcendentals=0
    )


def regrouped(value, outer, inner, width):
    rows, total = value.shape
    if width != 64 or outer % 2:
        split = value.reshape(rows, outer, inner, width)
        return jnp.swapaxes(split, 1, 2).reshape(rows, total)

    def kernel(in_ref, out_ref):
        for i in range(inner):
            for o in range(0, outer, 2):
                left = in_ref[:, (o * inner + i) * width : (o * inner + i + 1) * width]
                right = in_ref[:, ((o + 1) * inner + i) * width : ((o + 1) * inner + i + 1) * width]
                at = (i * outer + o) * width
                out_ref[:, at : at + 2 * width] = jnp.concatenate([left, right], axis=1)

    return pl.pallas_call(
        kernel,
        out_shape=jax.ShapeDtypeStruct(value.shape, value.dtype),
        compiler_params=pltpu.CompilerParams(vmem_limit_bytes=40 * 1024 * 1024),
        cost_estimate=about(2),
    )(value)


def dp_gather(value, forward=True):
    if lax.axis_size("dp") != 4:
        return lax.all_gather(value, "dp", axis=0)
    here = lax.axis_index("dp")
    half = value.shape[0] // 2
    one = permuted(value, "dp", 1)
    two = permuted(value, "dp", 2)
    if forward:
        three = jnp.concatenate([permuted(one[:half], "dp", 2), permuted(two[half:], "dp", 1)])
    else:
        three = permuted(value, "dp", 3)
    whole = jnp.zeros((4,) + value.shape, value.dtype)
    for k, piece in enumerate((value, one, two, three)):
        whole = lax.dynamic_update_index_in_dim(whole, piece, here ^ k, 0)
    return whole


def placed_pieces(pieces, here, cuts):
    count, (rows, width) = len(pieces), pieces[0].shape
    spans = list(zip(cuts[:-1], cuts[1:]))

    def kernel(here_ref, *refs):
        for k in range(count):
            owner = here_ref[0] ^ k
            for (low, high), out in zip(spans, refs[count:]):
                out[pl.ds(pl.multiple_of(owner * (high - low), 16), high - low)] = refs[k][low:high]

    return pl.pallas_call(
        kernel,
        out_shape=[
            jax.ShapeDtypeStruct((count * (high - low), width), pieces[0].dtype)
            for low, high in spans
        ],
        in_specs=[pl.BlockSpec(memory_space=pltpu.SMEM)]
        + [pl.BlockSpec(memory_space=pltpu.VMEM)] * count,
        out_specs=[pl.BlockSpec(memory_space=pltpu.VMEM)] * len(spans),
        compiler_params=pltpu.CompilerParams(vmem_limit_bytes=40 * 1024 * 1024),
        cost_estimate=about(2),
    )(here[None], *pieces)


def dp_scatter(total, forward=True, meanwhile=()):
    if lax.axis_size("dp") != 4:
        return lax.psum_scatter(total, "dp", scatter_dimension=0).astype(f32)
    here = lax.axis_index("dp")
    blocks = [lax.dynamic_index_in_dim(total, here ^ k, 0, False) for k in range(4)]
    if not forward:
        own = blocks[0].astype(f32)
        for k in range(1, 4):
            own = own + permuted(blocks[k], "dp", k).astype(f32)
        return own
    half = total.shape[1] // 2
    low, high = [b[:half] for b in blocks], [b[half:] for b in blocks]
    low_in = permuted(jnp.stack([low[1], low[3]]), "dp", 1)
    high_in = permuted(jnp.stack(high[2:]), "dp", 2)
    if meanwhile:
        low_in, high_in = after(low_in, *meanwhile), after(high_in, *meanwhile)
    low_in, high_in = low_in.astype(f32), high_in.astype(f32)
    low_on = (low[2].astype(f32) + low_in[1]).astype(bf16)
    high_on = (high[1].astype(f32) + high_in[1]).astype(bf16)
    low_own = low[0].astype(f32) + low_in[0] + permuted(low_on, "dp", 2).astype(f32)
    high_own = high[0].astype(f32) + high_in[0] + permuted(high_on, "dp", 1).astype(f32)
    return jnp.concatenate([low_own, high_own])


def row_sums(value):
    return other_pairs(value + permuted(value, "seq", 1))


def other_pairs(value):
    total = value
    for by in range(2, lax.axis_size("seq"), 2):
        total = total + permuted(value, "seq", by)
    return total


def segment_of(positions, end_points):
    counted = jnp.sum((end_points[None, :] <= positions[:, None]).astype(jnp.int32), axis=1)
    return jnp.where(positions < 0, -1, counted)


def rope_tables(positions):
    half = ATT_DIM // 2
    freqs = jnp.power(rope_base, -jnp.arange(half, dtype=f32) * (2.0 / ATT_DIM))
    angles = positions.astype(f32)[:, None] * freqs[None, :]
    cosine, sine = jnp.cos(angles), jnp.sin(angles)
    return jnp.concatenate([cosine, cosine], axis=1), jnp.concatenate([sine, sine], axis=1)


def rms_row(values):
    return lax.rsqrt(jnp.mean(values * values, axis=-1, keepdims=True) + epsilon)


def rms_back(grad, values, gain):
    r = rms_row(values)
    scaled = grad * gain
    along = jnp.mean(scaled * values, axis=-1, keepdims=True)
    return scaled * r - values * (r * r * r) * along, jnp.sum(grad * values * r, axis=0)


def dot(left, right):
    return jnp.dot(left, right, preferred_element_type=f32)


def dot_t(left, right):
    return lax.dot_general(left, right, (((1,), (1,)), ((), ())), preferred_element_type=f32)


def cross(left, right):
    return lax.dot_general(left, right, (((0,), (0,)), ((), ())), preferred_element_type=f32)


def halves(columns, pair, lanes):
    left, right = columns[:, 2 * pair : 2 * pair + 1], columns[:, 2 * pair + 1 : 2 * pair + 2]
    return jnp.where(lanes < HEAD_DIM, left, right)


def spread(columns, pairs, lanes):
    return jnp.concatenate([halves(columns, k, lanes) for k in range(pairs)], axis=1)


def counted(pattern, value, dims=(((1,), (0,)), ((), ())), terms=2, first=True):
    pattern = pattern.astype(bf16)
    total, rest = None, value
    for k in range(terms):
        term = rest.astype(bf16)
        pair = (pattern, term) if first else (term, pattern)
        part = lax.dot_general(*pair, dims, preferred_element_type=f32)
        total = part if total is None else total + part
        if k + 1 < terms:
            rest = rest - term.astype(f32)
    return total


def rough(left, right, dims=(((1,), (0,)), ((), ()))):
    return lax.dot_general(
        left.astype(bf16), right.astype(bf16), dims, preferred_element_type=f32
    )


ROWS = (((0,), (0,)), ((), ()))
LAST = (((1,), (1,)), ((), ()))


def block_start(mixed_ref, before_ref, aux_ref, conv_ref, head_ref, ext_ref, width):
    per = mixed_ref.shape[0]
    channels = width + 2 * STATE
    ext_ref[0:8] = before_ref[:, width : width + channels].astype(bf16).astype(f32)
    ext_ref[8 : 8 + per] = mixed_ref[:, width : width + channels].astype(bf16).astype(f32)
    aux = aux_ref[...]
    total = conv_ref[4:5] + ext_ref[8 : 8 + per] * conv_ref[3:4]
    for back in range(1, CONV):
        total = total + ext_ref[8 - back : 8 - back + per] * (
            aux[:, back : back + 1] * conv_ref[3 - back : 4 - back]
        )
    sig = jax.nn.sigmoid(total)
    shifted = mixed_ref[:, width + channels : width + channels + DT_PAD] + head_ref[1:2]
    step = jnp.maximum(shifted, 0.0) + jnp.log1p(jnp.exp(-jnp.abs(shifted)))
    rate = -jnp.exp(head_ref[0:1])
    rows_at = lax.broadcasted_iota(jnp.int32, (per, per), 0)
    cols_at = lax.broadcasted_iota(jnp.int32, (per, per), 1)
    tril = (rows_at >= cols_at).astype(f32)
    cum = counted(tril, step * rate, terms=3)
    return aux, total, sig, shifted, step, rate, tril, cum


def ssd_forward_kernel(
    mixed_ref,
    before_ref,
    aux_ref,
    seg_ref,
    conv_ref,
    head_ref,
    skip_ref,
    y_ref,
    gated_ref,
    enter_ref,
    ext_ref,
    state_ref,
):
    per, width = y_ref.shape
    pairs = width // 128

    @pl.when(pl.program_id(1) == 0)
    def _():
        state_ref[...] = jnp.zeros_like(state_ref)

    aux, total, sig, _, step, _, tril, cum = block_start(
        mixed_ref, before_ref, aux_ref, conv_ref, head_ref, ext_ref, width
    )
    conv = total * sig
    x = conv[:, :width]
    b = conv[:, width : width + STATE].astype(bf16)
    c = conv[:, width + STATE :].astype(bf16)
    lanes = lax.broadcasted_iota(jnp.int32, (per, 128), 1)
    mask = (tril > 0) & (aux[:, 0:1] == seg_ref[0])
    both = rough(c, b, LAST)
    cum_t, step_t = cum.T, step.T
    state = state_ref[...]
    enter_ref[0] = state.astype(bf16)
    carried = rough(c, state)
    grown = jnp.exp(cum) * aux[:, 4:5]
    last = cum[per - 1 : per]
    keep = jnp.exp(last - cum) * aux[:, 5:6] * step
    gate = mixed_ref[:, :width]
    silu_gate = gate * jax.nn.sigmoid(gate)
    scaled = []
    for k in range(pairs):
        at = slice(128 * k, 128 * k + 128)
        x_pair = x[:, at]
        x_low = x_pair.astype(bf16)
        sides = []
        for h in (2 * k, 2 * k + 1):
            gap = jnp.where(mask, cum[:, h : h + 1] - cum_t[h : h + 1], -1e30)
            mixing = both * jnp.exp(gap) * step_t[h : h + 1]
            sides.append(rough(mixing, x_low))
        y = jnp.where(lanes < HEAD_DIM, sides[0], sides[1])
        y = y + carried[:, at] * halves(grown, k, lanes) + skip_ref[:, at] * x_pair
        y_ref[:, at] = y
        gated_ref[:, at] = y * silu_gate[:, at]
        scaled.append(x_pair * halves(keep, k, lanes))
    passed = spread(jnp.exp(last) * aux[0:1, 6:7], pairs, lanes[0:1])
    state_ref[...] = state * passed + rough(b, jnp.concatenate(scaled, axis=1), ROWS)


def ssd_backward_kernel(
    mixed_ref,
    before_ref,
    aux_ref,
    seg_ref,
    conv_ref,
    head_ref,
    skip_ref,
    y_ref,
    enter_ref,
    grad_ref,
    qkv_ref,
    out_ref,
    conv_grad_ref,
    head_grad_ref,
    skip_grad_ref,
    ext_ref,
    next_ref,
    col_ref,
    state_ref,
):
    per, width = y_ref.shape
    pairs = width // 128
    channels = width + 2 * STATE

    @pl.when(pl.program_id(1) == 0)
    def _():
        state_ref[...] = jnp.zeros_like(state_ref)
        next_ref[...] = jnp.zeros_like(next_ref)

    @pl.when((pl.program_id(0) == 0) & (pl.program_id(1) == 0))
    def _():
        conv_grad_ref[...] = jnp.zeros_like(conv_grad_ref)
        head_grad_ref[...] = jnp.zeros_like(head_grad_ref)
        skip_grad_ref[...] = jnp.zeros_like(skip_grad_ref)
        col_ref[...] = jnp.zeros_like(col_ref)

    aux, total, sig, shifted, step, rate, tril, cum = block_start(
        mixed_ref, before_ref, aux_ref, conv_ref, head_ref, ext_ref, width
    )
    conv = total * sig
    x = conv[:, :width]
    b = conv[:, width : width + STATE].astype(bf16)
    c = conv[:, width + STATE :].astype(bf16)
    lanes = lax.broadcasted_iota(jnp.int32, (per, 128), 1)
    mask = (tril > 0) & (aux[:, 0:1] == seg_ref[0])
    both = rough(c, b, LAST)
    cum_t, step_t = cum.T, step.T
    enter = enter_ref[0]
    growth = jnp.exp(cum) * aux[:, 4:5]
    last = cum[per - 1 : per]
    fade = jnp.exp(last - cum) * aux[:, 5:6]
    keep = fade * step
    passed_row = jnp.exp(last) * aux[0:1, 6:7]

    gate = mixed_ref[:, :width]
    gate_sig = jax.nn.sigmoid(gate)
    grad = grad_ref[...]
    dy = grad * gate * gate_sig
    out_ref[:, :width] = (
        grad * y_ref[...] * (gate_sig * (1.0 + gate * (1.0 - gate_sig)))
    ).astype(bf16)

    d_out = state_ref[...]
    wide_growth = spread(growth, pairs, lanes)
    wide_keep = spread(keep, pairs, lanes)
    carried = rough(c, enter)
    dq = dy * wide_growth
    d_c = rough(dq, enter, LAST)
    xk = x * wide_keep
    d_b = rough(xk, d_out, LAST)
    dxk = rough(b, d_out)
    of_head = (
        lax.broadcasted_iota(jnp.int32, (width, 128), 0) // HEAD_DIM
        == lax.broadcasted_iota(jnp.int32, (width, 128), 1)
    ).astype(f32)
    d_growth = counted(of_head, dq * carried, first=False)
    d_keep = counted(of_head, dxk * x, first=False)
    d_passed = jnp.sum(d_out * enter.astype(f32), axis=0, keepdims=True)
    d_passed = counted(of_head, jnp.broadcast_to(d_passed, (16, width)), first=False)[0:1]
    d_x = dxk * wide_keep + dy * skip_ref[...]
    skip_grad_ref[0:1] += jnp.sum(dy * x, axis=0, keepdims=True)
    state_ref[...] = d_out * spread(passed_row, pairs, lanes[0:1]) + rough(c, dq, ROWS)

    d_both = jnp.zeros((per, per), f32)
    row_sums = jnp.zeros((per, 128), f32)
    within = []
    for k in range(pairs):
        at = slice(128 * k, 128 * k + 128)
        x_low = x[:, at].astype(bf16)
        dy_pair = dy[:, at]
        dy_low = dy_pair.astype(bf16)
        sides = []
        for h in (2 * k, 2 * k + 1):
            mine = (lanes >= HEAD_DIM) if h % 2 else (lanes < HEAD_DIM)
            gap = jnp.where(mask, cum[:, h : h + 1] - cum_t[h : h + 1], -1e30)
            level = jnp.exp(gap)
            step_row = step_t[h : h + 1]
            weighted = level * step_row
            sides.append(rough(both * weighted, dy_low, ROWS))
            d_mix = rough(jnp.where(mine, dy_pair, 0.0), x_low, LAST)
            d_both = d_both + d_mix * weighted
            flow = d_mix * both * level
            col_ref[h : h + 1] = jnp.sum(flow, axis=0, keepdims=True)
            row_sum = jnp.sum(flow * step_row, axis=1, keepdims=True)
            row_sums = jnp.where(lanes == h, row_sum, row_sums)
        within.append(jnp.where(lanes < HEAD_DIM, sides[0], sides[1]))
    d_x = d_x + jnp.concatenate(within, axis=1)
    d_c = d_c + rough(d_both, b)
    d_b = d_b + rough(d_both, c, ROWS)
    col_sums = col_ref[...].T
    d_step = col_sums + d_keep * fade
    kept = d_keep * keep
    d_cum = row_sums - col_sums * step + d_growth - kept
    d_last = jnp.sum(kept, axis=0, keepdims=True) + d_passed * passed_row
    at_end = lax.broadcasted_iota(jnp.int32, (per, 128), 0) == per - 1
    d_cum = d_cum + jnp.where(at_end, d_last, 0.0)
    d_decay = counted(tril, d_cum, ROWS)
    d_step = d_step + d_decay * rate
    d_shifted = d_step * jax.nn.sigmoid(shifted)
    head_grad_ref[0:1] += jnp.sum(d_decay * step, axis=0, keepdims=True) * rate
    head_grad_ref[1:2] += jnp.sum(d_shifted, axis=0, keepdims=True)
    out_ref[:, width + channels : width + channels + DT_PAD] = d_shifted.astype(bf16)
    out_ref[:, width + channels + DT_PAD :] = qkv_ref[...]

    d_conv = jnp.concatenate([d_x, d_b, d_c], axis=1)
    d_total = d_conv * (sig * (1.0 + total * (1.0 - sig)))
    conv_grad_ref[4:5] += jnp.sum(d_total, axis=0, keepdims=True)
    conv_grad_ref[3:4] += jnp.sum(d_total * ext_ref[8 : 8 + per], axis=0, keepdims=True)
    for back in range(1, CONV):
        conv_grad_ref[3 - back : 4 - back] += jnp.sum(
            d_total * aux[:, back : back + 1] * ext_ref[8 - back : 8 - back + per],
            axis=0,
            keepdims=True,
        )
    d_in = d_total * conv_ref[3:4]
    for back in range(1, CONV):
        masked = d_total * aux[:, back : back + 1]
        ext_ref[0:per] = masked
        ext_ref[per : per + 8] = next_ref[back - 1]
        d_in = d_in + ext_ref[back : back + per] * conv_ref[3 - back : 4 - back]
        next_ref[back - 1] = masked[0:8]
    out_ref[:, width : width + channels] = d_in.astype(bf16)


def ssd_specs(n, micro, per, width, used, order):
    eighths = per // 8
    return [
        pl.BlockSpec((per, used), lambda m, k: (order(k) * micro + m, 0)),
        pl.BlockSpec(
            (8, used),
            lambda m, k: (
                (jnp.maximum(order(k) - 1, 0) * micro + m) * eighths + eighths - 1,
                0,
            ),
        ),
        pl.BlockSpec((per, 8), lambda m, k: (order(k) * micro + m, 0)),
        pl.BlockSpec((1, 1, per), lambda m, k: (order(k) * micro + m, 0, 0)),
        pl.BlockSpec((8, width + 2 * STATE), lambda m, k: (0, 0)),
        pl.BlockSpec((8, DT_PAD), lambda m, k: (0, 0)),
        pl.BlockSpec((1, width), lambda m, k: (0, 0)),
    ]


def ssd_forward(mixed, aux, seg_rows, conv_rows, head_rows, skip_row, n, micro):
    rows = mixed.shape[0]
    per = rows // (n * micro)
    width = skip_row.shape[1]
    channels = width + 2 * STATE
    used = width + channels + DT_PAD
    specs = ssd_specs(n, micro, per, width, used, lambda k: k)
    by_block = pl.BlockSpec((per, width), lambda m, k: (k * micro + m, 0))
    return pl.pallas_call(
        ssd_forward_kernel,
        grid=(micro, n),
        out_shape=(
            jax.ShapeDtypeStruct((rows, width), f32),
            jax.ShapeDtypeStruct((rows, width), f32),
            jax.ShapeDtypeStruct((n * micro, STATE, width), bf16),
        ),
        in_specs=specs,
        out_specs=(
            by_block,
            by_block,
            pl.BlockSpec((1, STATE, width), lambda m, k: (k * micro + m, 0, 0)),
        ),
        scratch_shapes=[
            pltpu.VMEM((per + 8, channels), f32),
            pltpu.VMEM((STATE, width), f32),
        ],
        compiler_params=pltpu.CompilerParams(vmem_limit_bytes=40 * 1024 * 1024),
        cost_estimate=about(20),
    )(mixed, mixed, aux, seg_rows, conv_rows, head_rows, skip_row)


def ssd_backward(
    mixed, aux, seg_rows, conv_rows, head_rows, skip_row, y, enter, grad, qkv, n, micro
):
    rows = mixed.shape[0]
    per = rows // (n * micro)
    width = skip_row.shape[1]
    channels = width + 2 * STATE
    used = width + channels + DT_PAD

    def order(k):
        return n - 1 - k

    specs = ssd_specs(n, micro, per, width, used, order)
    by_block = pl.BlockSpec((per, width), lambda m, k: (order(k) * micro + m, 0))
    return pl.pallas_call(
        ssd_backward_kernel,
        grid=(micro, n),
        out_shape=(
            jax.ShapeDtypeStruct(mixed.shape, bf16),
            jax.ShapeDtypeStruct((8, channels), f32),
            jax.ShapeDtypeStruct((8, DT_PAD), f32),
            jax.ShapeDtypeStruct((8, width), f32),
        ),
        in_specs=specs
        + [
            by_block,
            pl.BlockSpec((1, STATE, width), lambda m, k: (order(k) * micro + m, 0, 0)),
            by_block,
            pl.BlockSpec((per, qkv.shape[1]), lambda m, k: (order(k) * micro + m, 0)),
        ],
        out_specs=(
            pl.BlockSpec((per, mixed.shape[1]), lambda m, k: (order(k) * micro + m, 0)),
            pl.BlockSpec((8, channels), lambda m, k: (0, 0)),
            pl.BlockSpec((8, DT_PAD), lambda m, k: (0, 0)),
            pl.BlockSpec((8, width), lambda m, k: (0, 0)),
        ),
        scratch_shapes=[
            pltpu.VMEM((per + 8, channels), f32),
            pltpu.VMEM((CONV - 1, 8, channels), f32),
            pltpu.VMEM((128, per), f32),
            pltpu.VMEM((STATE, width), f32),
        ],
        compiler_params=pltpu.CompilerParams(vmem_limit_bytes=40 * 1024 * 1024),
        cost_estimate=about(43),
    )(mixed, mixed, aux, seg_rows, conv_rows, head_rows, skip_row, y, enter, grad, qkv)


def turn(values, cosine, sine):
    half = ATT_DIM // 2
    swapped = jnp.concatenate([-values[:, half:], values[:, :half]], axis=1)
    return values * cosine + swapped * sine


def attention_start(k_ref, v_ref, table_ref, keys_ref, values_ref):
    blocks, per, _ = k_ref.shape
    for b in range(blocks):
        at = slice(b * per, b * per + per)
        keys_ref[at] = turn(k_ref[b], table_ref[b, :, :ATT_DIM], table_ref[b, :, ATT_DIM:]).astype(
            bf16
        )
        values_ref[at] = v_ref[b].astype(bf16)


def attention_probs(q_ref, q_table_ref, q_aux_ref, seg_ref, keys_ref):
    scale = ATT_DIM ** (-0.5)
    table = q_table_ref[0]
    queries = turn(q_ref[0], table[:, :ATT_DIM], table[:, ATT_DIM:]).astype(bf16)
    scores = rough(queries, keys_ref[...], LAST) * scale
    q_aux = q_aux_ref[0]
    positions = lax.broadcasted_iota(jnp.int32, scores.shape, 1)
    seen = (positions <= q_aux[:, 1:2].astype(jnp.int32)) & (q_aux[:, 0:1] == seg_ref[0])
    scores = jnp.where(seen, scores, -1e30)
    raised = jnp.exp(scores - jnp.max(scores, axis=1, keepdims=True))
    return queries, raised / jnp.sum(raised, axis=1, keepdims=True)


def attention_forward_kernel(
    q_ref, k_ref, v_ref, table_ref, q_table_ref, q_aux_ref, seg_ref, out_ref, keys_ref, values_ref
):
    @pl.when(pl.program_id(1) == 0)
    def _():
        attention_start(k_ref, v_ref, table_ref, keys_ref, values_ref)

    _, probs = attention_probs(q_ref, q_table_ref, q_aux_ref, seg_ref, keys_ref)
    out_ref[0] = rough(probs, values_ref[...]).astype(bf16)


def attention_backward_kernel(
    q_ref,
    k_ref,
    v_ref,
    table_ref,
    q_table_ref,
    q_aux_ref,
    seg_ref,
    grad_ref,
    q_grad_ref,
    k_grad_ref,
    v_grad_ref,
    keys_ref,
    values_ref,
    k_sum_ref,
    v_sum_ref,
):
    blocks, per, _ = k_ref.shape

    @pl.when(pl.program_id(1) == 0)
    def _():
        attention_start(k_ref, v_ref, table_ref, keys_ref, values_ref)
        k_sum_ref[...] = jnp.zeros_like(k_sum_ref)
        v_sum_ref[...] = jnp.zeros_like(v_sum_ref)

    scale = ATT_DIM ** (-0.5)
    queries, probs = attention_probs(q_ref, q_table_ref, q_aux_ref, seg_ref, keys_ref)
    grad = grad_ref[0]
    probs_grad = rough(grad, values_ref[...], LAST)
    along = jnp.sum(probs * probs_grad, axis=1, keepdims=True)
    scores_grad = (probs * (probs_grad - along)).astype(bf16)
    table = q_table_ref[0]
    q_grad = rough(scores_grad, keys_ref[...]) * scale
    q_grad_ref[0] = turn(q_grad, table[:, :ATT_DIM], -table[:, ATT_DIM:]).astype(bf16)
    k_sum_ref[...] += rough(scores_grad, queries, ROWS)
    v_sum_ref[...] += rough(probs, grad, ROWS)

    @pl.when(pl.program_id(1) == pl.num_programs(1) - 1)
    def _():
        for b in range(blocks):
            at = slice(b * per, b * per + per)
            k_grad_ref[b] = turn(
                k_sum_ref[at] * scale, table_ref[b, :, :ATT_DIM], -table_ref[b, :, ATT_DIM:]
            ).astype(bf16)
            v_grad_ref[b] = v_sum_ref[at].astype(bf16)


def attention_specs(n, micro, per, q_at, k_at, v_at):
    return [
        pl.BlockSpec((1, per, ATT_DIM), lambda m, k: (k, m, q_at)),
        pl.BlockSpec((n, per, ATT_DIM), lambda m, k: (0, m, k_at)),
        pl.BlockSpec((n, per, ATT_DIM), lambda m, k: (0, m, v_at)),
        pl.BlockSpec((n, per, 2 * ATT_DIM), lambda m, k: (0, 0, 0)),
        pl.BlockSpec((1, per, 2 * ATT_DIM), lambda m, k: (k, 0, 0)),
        pl.BlockSpec((1, per, 8), lambda m, k: (k, m, 0)),
        pl.BlockSpec((1, 1, n * per), lambda m, k: (m, 0, 0)),
    ]


def attention_forward(q, mixed, table, q_table, q_aux, seg, q_at, k_at):
    n, both, _ = mixed.shape
    micro = seg.shape[0]
    per = both // micro
    block = pl.BlockSpec((1, per, ATT_DIM), lambda m, k: (k, m, 0))
    return pl.pallas_call(
        attention_forward_kernel,
        grid=(micro, q_table.shape[0]),
        out_shape=jax.ShapeDtypeStruct((q_table.shape[0], both, ATT_DIM), bf16),
        in_specs=attention_specs(n, micro, per, q_at, k_at, k_at + 1),
        out_specs=block,
        scratch_shapes=[pltpu.VMEM((n * per, ATT_DIM), bf16)] * 2,
        compiler_params=pltpu.CompilerParams(vmem_limit_bytes=40 * 1024 * 1024),
        cost_estimate=about(14),
    )(q, mixed, mixed, table, q_table, q_aux, seg)


def attention_backward(q, mixed, table, q_table, q_aux, seg, grad, q_at, k_at):
    n, both, _ = mixed.shape
    micro = seg.shape[0]
    per = both // micro
    block = pl.BlockSpec((1, per, ATT_DIM), lambda m, k: (k, m, 0))
    whole = pl.BlockSpec((n, per, ATT_DIM), lambda m, k: (0, m, 0))
    return pl.pallas_call(
        attention_backward_kernel,
        grid=(micro, q_table.shape[0]),
        out_shape=(
            jax.ShapeDtypeStruct((q_table.shape[0], both, ATT_DIM), bf16),
            jax.ShapeDtypeStruct((n, both, ATT_DIM), bf16),
            jax.ShapeDtypeStruct((n, both, ATT_DIM), bf16),
        ),
        in_specs=attention_specs(n, micro, per, q_at, k_at, k_at + 1) + [block],
        out_specs=(block, whole, whole),
        scratch_shapes=[pltpu.VMEM((n * per, ATT_DIM), bf16)] * 2
        + [pltpu.VMEM((n * per, ATT_DIM), f32)] * 2,
        compiler_params=pltpu.CompilerParams(vmem_limit_bytes=40 * 1024 * 1024),
        cost_estimate=about(19),
    )(q, mixed, mixed, table, q_table, q_aux, seg, grad)


def ffn_kernel(rows_ref, weight_ref, turned_ref, grad_ref, act_ref, gate_grad_ref, back_ref):
    half = grad_ref.shape[1]
    values = rough(rows_ref[...], weight_ref[...])
    gate, up = values[:, :half], values[:, half:]
    grad = grad_ref[...]
    sig = jax.nn.sigmoid(gate)
    silu = gate * sig
    act_ref[...] = (silu * up).astype(bf16)
    gate_grad_ref[:, :half] = (grad * up * (sig * (1.0 + gate * (1.0 - sig)))).astype(bf16)
    gate_grad_ref[:, half:] = (grad * silu).astype(bf16)
    back_ref[...] = rough(gate_grad_ref[...], turned_ref[...]).astype(bf16)


def ffn_both(rows, weight, turned_weight, act_grad):
    count, depth = rows.shape
    block, wide = 256, weight.shape[1]

    def by_block(columns):
        return pl.BlockSpec((block, columns), lambda k: (k, 0))

    def whole(array):
        return pl.BlockSpec(array.shape, lambda k: (0, 0))

    return pl.pallas_call(
        ffn_kernel,
        grid=(count // block,),
        out_shape=(
            jax.ShapeDtypeStruct((count, wide // 2), bf16),
            jax.ShapeDtypeStruct((count, wide), bf16),
            jax.ShapeDtypeStruct((count, depth), bf16),
        ),
        in_specs=[by_block(depth), whole(weight), whole(turned_weight), by_block(wide // 2)],
        out_specs=(by_block(wide // 2), by_block(wide), by_block(depth)),
        compiler_params=pltpu.CompilerParams(vmem_limit_bytes=48 * 1024 * 1024),
        cost_estimate=about(22),
    )(rows, weight, turned_weight, act_grad)


def local(
    tokens,
    doc_ends,
    input_gain,
    mixer_in,
    conv_weight,
    conv_bias,
    head_params,
    mixer_gain,
    mixer_out,
    attn_qkv,
    attn_out,
    ffn_gain,
    gate_up,
    down_proj,
    out_grad,
):
    n = lax.axis_size("seq")
    nd = lax.axis_size("dp")
    s = lax.axis_index("seq")
    d = lax.axis_index("dp")
    micro, _, per, _ = tokens.shape
    own = micro * per
    length = n * per
    rows = n * own
    owner = mixer_in.shape[0]
    inner = INNER // n
    width = -(-inner // 128) * 128
    heads = HEADS // n
    ffl = FF // n
    parts = n // ATT_HEADS
    group = ATT_HEADS // KV_HEADS
    conv_ch = INNER + 2 * STATE

    def mixed_order(value):
        if value.ndim == 1:
            return jnp.swapaxes(value.reshape(n, nd, owner), 0, 1).reshape(D)
        return regrouped(value, n, nd, owner)

    def plain_order(value):
        if value.ndim == 1:
            return jnp.swapaxes(value.reshape(nd, n, owner), 0, 1).reshape(D)
        return regrouped(value, nd, n, owner)

    def widened(value):
        return jnp.pad(value, [(0, 0)] * (value.ndim - 1) + [(0, width - inner)])

    def from_seq(value):
        return value.reshape(micro, n, per, -1).transpose(1, 0, 2, 3).reshape(rows, -1)

    def gathered(value):
        return lax.all_gather(value, "seq", axis=0, tiled=True)

    def scattered(value, *others):
        total = lax.psum_scatter(value.astype(bf16), "seq", scatter_dimension=0, tiled=True)
        return (after(total, *others) if others else total).astype(f32)

    token_b = mixed_order(tokens.reshape(own, D))
    token_rows = token_b.astype(f32)
    grad_rows = mixed_order(out_grad.reshape(own, D))

    tap_count = conv_weight.shape[1]
    small_own = jnp.concatenate(
        [input_gain, conv_weight.reshape(-1), conv_bias, mixer_gain, ffn_gain]
    )
    small_count = small_own.shape[0]
    small_cols = -(-small_count // owner)
    small_own = jnp.pad(small_own, (0, small_cols * owner - small_count)).reshape(owner, small_cols)

    steps_own = jnp.pad(
        jnp.concatenate(
            [
                mixer_in[:, 2 * INNER + 2 * STATE :].reshape(owner, n, heads).transpose(1, 0, 2),
                jnp.broadcast_to(small_own[None], (n,) + small_own.shape),
            ],
            axis=2,
        ),
        ((0, 0), (0, 0), (0, DT_PAD - heads - small_cols)),
    )
    q_of = [k // parts for k in range(n)]
    kv_of = [ATT_HEADS + q // group for q in q_of]
    sizes = [width, width, 2 * STATE, DT_PAD, ATT_DIM, ATT_DIM, ATT_DIM]
    starts = [sum(sizes[:k]) for k in range(len(sizes) + 1)]
    every = slice(None)
    sent_sizes = [width, width, STATE, DT_PAD, ATT_DIM, ATT_DIM]
    sent_at = [sum(sent_sizes[:k]) for k in range(len(sent_sizes) + 1)]
    moves = []
    for k in range(n):
        odd = k % 2
        for which, source, target, wide in (
            (0, k * inner, sent_at[0], inner),
            (0, INNER + k * inner, sent_at[1], inner),
            (0, 2 * INNER + odd * STATE, sent_at[2], STATE),
            (1, q_of[k] * ATT_DIM, sent_at[4], ATT_DIM),
            (1, (kv_of[k] + odd * KV_HEADS) * ATT_DIM, sent_at[5], ATT_DIM),
        ):
            moves.append(
                (which, (every, slice(source, source + wide)), (k, every, slice(target, target + wide)))
            )
        moves.append((2, (k,), (k, every, slice(sent_at[3], sent_at[4]))))
        if width != inner:
            gap = slice(0, width - inner)
            for target in (sent_at[1], sent_at[2]):
                hole = slice(target - width + inner, target)
                moves.append((3, (every, gap), (k, every, hole)))
    blank = jnp.zeros((owner, 128), bf16)
    packed = assembled(
        (n, owner, sent_at[-1]), bf16, moves, mixer_in, attn_qkv, steps_own, blank
    )
    sent_in = exchanged(packed, "seq")
    positions = jnp.arange(length, dtype=jnp.int32)
    seg = jnp.stack([segment_of(positions, doc_ends[m, 0]) for m in range(micro)])

    blocks = seg.reshape(micro, n, per)
    columns = [seg.astype(f32)]
    for back in range(1, CONV):
        moved = jnp.pad(seg[:, : length - back], ((0, 0), (back, 0)), constant_values=-1)
        columns.append((moved == seg).astype(f32))
    prior = jnp.concatenate(
        [jnp.full((micro, 1), -1, jnp.int32), blocks[:, :-1, per - 1]], axis=1
    )
    last = blocks[:, :, per - 1]
    for flag in (
        blocks == prior[:, :, None],
        blocks == last[:, :, None],
        jnp.broadcast_to((last == prior)[:, :, None], blocks.shape),
        jnp.zeros_like(blocks),
    ):
        columns.append(flag.astype(f32).reshape(micro, length))
    aux = from_seq(jnp.stack(columns, axis=-1))
    seg_blocks = blocks.transpose(1, 0, 2).reshape(n * micro, 1, per).astype(f32)
    cosine, sine = rope_tables(positions)
    table = jnp.concatenate([cosine, sine], axis=1).reshape(n, per, 2 * ATT_DIM)
    part = s % parts

    def taken(value):
        if parts == 1:
            return value
        split = value.reshape(n // parts, parts, *value.shape[1:])
        return lax.dynamic_index_in_dim(split, part, 1, False)

    def put_back(value):
        if parts == 1:
            return value
        here = (jnp.arange(parts) == part).reshape(1, parts, 1, 1)
        return jnp.where(here, value[:, None], 0).reshape(n, *value.shape[1:])

    q_aux = jnp.stack(
        [seg.astype(f32), jnp.broadcast_to(positions.astype(f32), seg.shape)], axis=-1
    )
    q_aux = jnp.pad(from_seq(q_aux), ((0, 0), (0, 6))).reshape(n, own, 8)
    q_aux, q_table = taken(q_aux), taken(table)
    w_half = dp_gather(sent_in)
    small = w_half[:, :, :, sent_at[3] + heads : sent_at[3] + heads + small_cols]
    small = jnp.swapaxes(small, 0, 1).reshape(n * nd, -1)[:, :small_count]
    w_half = w_half.reshape(D, sent_at[-1])
    w_cut = [w_half[:, sent_at[k] : sent_at[k + 1]] for k in range(6)]
    own_side = jnp.concatenate([w_cut[2], w_cut[5]], axis=1)
    other_side = permuted(own_side, "seq", 1)
    odd_place = (s & 1) != 0
    first_side = jnp.where(odd_place, other_side, own_side)
    second_side = jnp.where(odd_place, own_side, other_side)
    w_in = jnp.concatenate(
        [
            w_cut[0],
            w_cut[1],
            first_side[:, :STATE],
            second_side[:, :STATE],
            w_cut[3],
            w_cut[4],
            first_side[:, STATE:],
            second_side[:, STATE:],
        ],
        axis=1,
    )
    w_in = after(w_in, aux, seg_blocks, table, q_aux)
    gu_moves = []
    for k in range(n):
        for half in range(2):
            gu_moves.append(
                (
                    (every, slice(half * FF + k * ffl, half * FF + (k + 1) * ffl)),
                    (k, every, slice(half * ffl, (half + 1) * ffl)),
                )
            )
    gu_own = assembled(
        (n, owner, 2 * ffl), bf16, [(0, flat, cube) for flat, cube in gu_moves], gate_up
    )
    sent_gu = exchanged(after(gu_own, w_in), "seq")
    cuts = [owner, CONV * tap_count, tap_count, mixer_gain.shape[0], owner]
    at = [sum(cuts[:k]) for k in range(len(cuts) + 1)]
    small = small.astype(f32)
    gain_in = mixed_order(small[:, at[0] : at[1]].reshape(-1))
    taps = (
        small[:, at[1] : at[2]].reshape(-1, CONV, tap_count).transpose(1, 0, 2).reshape(CONV, -1)
    )
    shift = small[:, at[2] : at[3]].reshape(-1)
    gain_mix = widened(
        lax.dynamic_slice_in_dim(small[:, at[3] : at[4]].reshape(-1), s * inner, inner)
    )
    gain_ffn = mixed_order(small[:, at[4] : at[5]].reshape(-1))
    conv_rows = jnp.concatenate([taps, shift[None], jnp.zeros((3, conv_ch), f32)])
    conv_rows = jnp.concatenate(
        [
            widened(lax.dynamic_slice_in_dim(conv_rows, s * inner, inner, axis=1)),
            conv_rows[:, INNER:],
        ],
        axis=1,
    )
    head = lax.dynamic_slice_in_dim(head_params, s * heads, heads, axis=1)
    head_rows = jnp.pad(head, ((0, 5), (0, DT_PAD - heads)))
    skip_row = widened(jnp.repeat(head[2], HEAD_DIM)[None])

    token_all = gathered(after(token_b, sent_in))
    token_f32 = token_all.astype(f32)
    normed = (token_f32 * rms_row(token_f32) * gain_in).astype(bf16)
    grads = gathered(after(grad_rows, token_all, w_in))
    mixed = dot(normed, w_in)
    out_own = after(mixed_order(jnp.concatenate([mixer_out, attn_out])), w_in)
    out_cut = mixer_out.shape[0]
    if nd == 4 and out_cut % 16 == 0:
        pieces = [after(permuted(out_own, "dp", k), mixed) for k in range(1, nd)]
        w_mix, w_att = placed_pieces([out_own, *pieces], d, [0, out_cut, out_own.shape[0]])
    else:
        out_parts = dp_gather(out_own, forward=False)
        w_mix = out_parts[:, :out_cut].reshape(-1, D)
        w_att = out_parts[:, out_cut:].reshape(-1, D)
    w_mix = jnp.pad(w_mix, ((0, width - inner), (0, 0)))
    if parts > 1:
        other = permuted(w_att, "seq", 1)
        w_att = jnp.where(
            (s & 1) != 0, jnp.concatenate([other, w_att]), jnp.concatenate([w_att, other])
        )
    w_gu = dp_gather(after(sent_gu, mixed), forward=False).reshape(D, 2 * ffl)
    w_down = dp_gather(after(mixed_order(down_proj), mixed), forward=False).reshape(ffl, D)
    ssd_args = (mixed, aux, seg_blocks, conv_rows, head_rows, skip_row)
    y, gated, enter = ssd_forward(*ssd_args, n, micro)
    squares = row_sums(jnp.sum(gated * gated, axis=1)) / INNER
    r_mix = lax.rsqrt(squares + epsilon)[:, None]
    mixer_b = (gated * r_mix * gain_mix).astype(bf16)

    q_at = starts[4] // ATT_DIM
    mixed_blocks = mixed.reshape(n, own, starts[-1])
    queries, own_q_at = mixed_blocks, q_at
    if parts > 1:
        queries, own_q_at = taken(mixed_blocks[:, :, starts[4] : starts[5]]), 0
    q_aux = after(q_aux, sent_gu, gated)
    att_args = (queries, mixed_blocks, table, q_table, q_aux)
    att_args = att_args + (seg.astype(f32)[:, None],)
    attended_b = put_back(attention_forward(*att_args, own_q_at, q_at + 1)).reshape(rows, ATT_DIM)
    branch_b = jnp.concatenate([mixer_b, attended_b], axis=1)
    w_out = jnp.concatenate([w_mix, w_att])
    branches = dot(branch_b, w_out)
    branches = after(branches.astype(bf16), grads)
    hidden = token_rows + scattered(branches, w_gu, w_down)
    ffn_own = (hidden * rms_row(hidden) * gain_ffn).astype(bf16)
    ffn_in = gathered(ffn_own)

    act_grad = after(dot_t(grads, w_down), branches)
    turned_gu = after(w_gu.T, branches)
    activated_b, gate_grad, ffn_back = ffn_both(ffn_in, w_gu, turned_gu, act_grad)
    gu_total = cross(ffn_in, gate_grad).astype(bf16)
    down_total = cross(activated_b, grads).astype(bf16)
    ffn_in_grad = scattered(ffn_back, gu_total, down_total)

    def over_dp(total, forward, meanwhile=()):
        return dp_scatter(total.reshape(nd, n * owner, -1), forward, meanwhile).astype(bf16)

    def to_owners(part_sum):
        return exchanged(part_sum.reshape(n, owner, -1), "seq")

    gu_part = over_dp(gu_total, False)
    down_grad = dp_scatter(down_total.reshape(nd, -1, D), False)
    hidden_part, ffn_gain_grad = rms_back(ffn_in_grad, hidden, gain_ffn)
    hidden_grad = hidden_part + grad_rows.astype(f32)
    hidden_b = after(gathered(hidden_grad.astype(bf16)), gu_part, down_grad)
    gu_sum = to_owners(gu_part)

    ffn_out = after(dot(activated_b, w_down).astype(bf16), hidden_b)
    ffn_sum = lax.psum_scatter(ffn_out, "seq", scatter_dimension=0, tiled=True)
    layer_out = plain_order((hidden + ffn_sum.astype(f32)).astype(bf16))

    branch_total = cross(branch_b, hidden_b).astype(bf16)
    mix_total, att_total = branch_total[:width], branch_total[width:]
    if parts > 1:
        half = att_total.shape[0] // 2
        low, high = att_total[:half], att_total[half:]
        odd = (s & 1) != 0
        other = permuted(jnp.where(odd, low, high), "seq", 1)
        att_total = (jnp.where(odd, high, low).astype(f32) + other.astype(f32)).astype(bf16)
    out_total = jnp.concatenate(
        [mix_total[:inner].reshape(nd, -1, D), att_total.reshape(nd, -1, D)], axis=1
    )
    if nd == 4:
        out_blocks = [lax.dynamic_index_in_dim(out_total, d ^ k, 0, False) for k in range(nd)]
        out_pieces = [permuted(out_blocks[k], "dp", k) for k in range(1, nd)]
        out_sum = out_blocks[0].astype(f32)
        for piece in out_pieces:
            out_sum = out_sum + piece.astype(f32)
    else:
        out_sum = dp_scatter(out_total, False)
        out_pieces = [out_sum]

    branch_grad = dot_t(hidden_b, w_out)
    mix_grad = branch_grad[:, :width]
    scaled = mix_grad * gain_mix
    along = jnp.sum(scaled * gated, axis=1)
    along = along + permuted(along, "seq", 1)
    att_grad = taken(branch_grad[:, width:].astype(bf16).reshape(n, own, ATT_DIM))
    att_grad = after(att_grad, along)
    q_grad, k_grad, v_grad = attention_backward(*att_args, att_grad, own_q_at, q_at + 1)
    qkv_grad = jnp.concatenate([put_back(q_grad), k_grad, v_grad], axis=2).reshape(rows, -1)

    along = other_pairs(along)[:, None] / INNER
    mix_gain_grad = jnp.sum(mix_grad * gated * r_mix, axis=0)
    gated_grad = scaled * r_mix - gated * (r_mix * r_mix * r_mix) * along
    mixed_grad, conv_g, head_g, skip_g = ssd_backward(
        *ssd_args, y, enter, gated_grad, qkv_grad, n, micro
    )
    mixed_grad = after(mixed_grad, gu_sum, *out_pieces)

    def placed(value, full):
        whole = jnp.zeros(value.shape[:-1] + (full,), f32)
        return lax.dynamic_update_slice_in_dim(
            whole, value, s * value.shape[-1], axis=value.ndim - 1
        )

    def by_owner(value):
        return value.reshape(-1, n * nd, value.shape[-1] // (n * nd)).transpose(1, 0, 2)

    conv_full = jnp.concatenate(
        [placed(conv_g[: CONV + 1, :inner], INNER), conv_g[: CONV + 1, width:]], axis=1
    )
    vectors = [
        by_owner(conv_full),
        by_owner(placed(mix_gain_grad[:inner], INNER)[None]),
        by_owner(plain_order(ffn_gain_grad)[None]),
    ]
    vectors = jnp.concatenate([v.reshape(n * nd, -1) for v in vectors], axis=1)
    vector_count = vectors.shape[1]
    vector_cols = -(-vector_count // owner)
    vectors = jnp.pad(vectors, ((0, 0), (0, vector_cols * owner - vector_count)))
    vectors = vectors.reshape(n, nd, owner, vector_cols).transpose(1, 0, 2, 3)
    vectors = vectors.reshape(D, vector_cols)

    in_back = after(dot_t(mixed_grad, w_in).astype(bf16), ffn_sum)
    mixed_grad = after(mixed_grad, in_back)
    zx_total = cross(normed, mixed_grad[:, : starts[2]]).astype(bf16)
    at_steps, at_heads = starts[3] - starts[2], starts[4] - starts[2]
    spare = starts[-1] - starts[2] - at_steps - heads - vector_cols
    rest_total = cross(normed, mixed_grad[:, starts[2] :])
    rest_total = (
        rest_total + jnp.pad(vectors, ((0, 0), (at_steps + heads, spare)))
    ).astype(bf16)
    zx_part = over_dp(zx_total, True, (rest_total,))
    zx_sum = to_owners(zx_part)
    rest_sum = to_owners(over_dp(rest_total, True, (zx_total,)))
    gu_sum, down_grad = after(gu_sum, rest_total), after(down_grad, rest_total)
    gate_up_grad = assembled(
        (owner, 2 * FF), f32, [(0, cube, flat) for flat, cube in gu_moves], gu_sum
    )
    out_plain = plain_order(out_sum)
    mixer_out_grad = out_plain[: mixer_out.shape[0]]
    attn_out_grad = out_plain[mixer_out.shape[0] :]
    down_grad = plain_order(down_grad)
    normed_sum = lax.psum_scatter(in_back, "seq", scatter_dimension=0, tiled=True)
    normed_sum = after(
        normed_sum, gate_up_grad, mixer_out_grad, attn_out_grad, down_grad, layer_out
    )
    normed_grad = normed_sum.astype(f32)
    head_g = jnp.concatenate(
        [head_g[:2, :heads], skip_g[:1, :inner].reshape(1, heads, HEAD_DIM).sum(axis=2)]
    )
    head_g = after(placed(head_g, HEADS).reshape(-1), normed_sum)
    head_g = summed(head_g, ("dp",))
    head_g = head_g + permuted(head_g, "seq", 1)
    others = [head_g] + [permuted(head_g, "seq", by) for by in range(2, n, 2)]
    head_g = jnp.sum(jnp.stack(others)[jnp.arange(n // 2) ^ (s // 2)], axis=0)
    token_part, _ = rms_back(normed_grad, token_rows, gain_in)
    token_grad = plain_order(token_part + hidden_grad)
    zx_sum = after(zx_sum, token_grad, head_g)

    bc_sum = jnp.sum(rest_sum[:, :, :at_steps].astype(f32), axis=0)
    step_sum = (
        rest_sum[:, :, at_steps : at_steps + heads]
        .transpose(1, 0, 2)
        .reshape(owner, HEADS)
    )
    moves = []
    for k in range(n):
        for half in range(2):
            source = slice(half * width, half * width + inner)
            target = slice(half * INNER + k * inner, half * INNER + (k + 1) * inner)
            moves.append((0, (k, every, source), (every, target)))
    moves.append((1, (every, every), (every, slice(2 * INNER, 2 * INNER + 2 * STATE))))
    moves.append((2, (every, every), (every, slice(2 * INNER + 2 * STATE, PROJ))))
    mixer_in_grad = assembled((owner, PROJ), f32, moves, zx_sum, bc_sum, step_sum)
    head_sum = rest_sum[:, :, at_heads:].astype(f32)
    head_sum = [head_sum[:, :, k * ATT_DIM : (k + 1) * ATT_DIM] for k in range(3)]
    q_sum = head_sum[0].reshape(ATT_HEADS, parts, owner, ATT_DIM).sum(axis=1)
    k_sum = head_sum[1].reshape(KV_HEADS, n // KV_HEADS, owner, ATT_DIM).sum(axis=1)
    v_sum = head_sum[2].reshape(KV_HEADS, n // KV_HEADS, owner, ATT_DIM).sum(axis=1)
    attn_qkv_grad = (
        jnp.concatenate([q_sum, k_sum, v_sum]).transpose(1, 0, 2).reshape(owner, -1)
    )

    vectors = jnp.sum(
        rest_sum[:, :, at_steps + heads : at_steps + heads + vector_cols].astype(f32), axis=0
    ).reshape(-1)[:vector_count]
    ends = [(CONV + 1) * tap_count, (CONV + 1) * tap_count + mixer_gain.shape[0]]
    conv_own = vectors[: ends[0]].reshape(CONV + 1, tap_count)
    in_gain_grad = (
        jnp.sum(mixer_in.astype(f32) * mixer_in_grad, axis=1)
        + jnp.sum(attn_qkv.astype(f32) * attn_qkv_grad, axis=1)
    ) / input_gain.astype(f32)
    return (
        layer_out.reshape(micro, 1, per, D),
        token_grad.reshape(micro, 1, per, D),
        in_gain_grad,
        mixer_in_grad,
        conv_own[:CONV],
        conv_own[CONV],
        head_g.reshape(3, HEADS),
        vectors[ends[0] : ends[1]],
        mixer_out_grad,
        attn_qkv_grad,
        attn_out_grad,
        vectors[ends[1] :],
        gate_up_grad,
        down_grad,
    )


def solution(mesh):
    rows = P(("seq", "dp"), None)
    vector = P(("seq", "dp"))
    activations = P(None, "dp", "seq", None)
    return jax.shard_map(
        local,
        mesh=mesh,
        in_specs=(
            activations,
            P(None, "dp", None),
            vector,
            rows,
            P(None, ("seq", "dp")),
            vector,
            P(),
            vector,
            rows,
            rows,
            rows,
            vector,
            rows,
            rows,
            activations,
        ),
        out_specs=(
            activations,
            activations,
            vector,
            rows,
            P(None, ("seq", "dp")),
            vector,
            P(),
            vector,
            rows,
            rows,
            rows,
            vector,
            rows,
            rows,
        ),
        check_vma=False,
    )
```

```python
import jax
import jax.numpy as jnp
from jax import lax
from jax.experimental import pallas as pl
from jax.experimental.pallas import tpu as pltpu
from jax.sharding import PartitionSpec as P

D = 2048
FF = 4096
HEADS = 48
HEAD_DIM = 64
STATE = 256
ATT_HEADS = 8
KV_HEADS = 2
ATT_DIM = 128
INNER = HEADS * HEAD_DIM
CONV = 4
PROJ = 2 * INNER + 2 * STATE + HEADS
DT_PAD = 128

epsilon = 1e-05
rope_base = 10000.0
f32 = jnp.float32
bf16 = jnp.bfloat16


def after(value, *others):
    def nothing(*refs):
        pass

    return pl.pallas_call(
        nothing,
        out_shape=jax.ShapeDtypeStruct(value.shape, value.dtype),
        in_specs=[pl.BlockSpec(memory_space=pl.ANY)] * (1 + len(others)),
        out_specs=pl.BlockSpec(memory_space=pl.ANY),
        input_output_aliases={0: 0},
    )(value, *others)


def permuted(value, axis, by):
    pairs = [(i, i ^ by) for i in range(lax.axis_size(axis))]
    return lax.ppermute(value, axis, pairs)


def small_gather(value):
    rows = value[None]
    for axis in ("dp", "seq"):
        here = lax.axis_index(axis)
        by = 1
        while by < lax.axis_size(axis):
            other = permuted(rows, axis, by)
            upper = (here & by) != 0
            rows = jnp.where(
                upper, jnp.concatenate([other, rows]), jnp.concatenate([rows, other])
            )
            by *= 2
    return rows


def summed(value, axes):
    for axis in axes:
        by = 1
        while by < lax.axis_size(axis):
            value = value + permuted(value, axis, by)
            by *= 2
    return value


def exchanged(blocks, axis):
    return lax.all_to_all(blocks, axis, 0, 0, tiled=True)


def assembled(shape, kind, moves, *inputs):
    def kernel(*refs):
        out = refs[-1]
        for which, source, target in moves:
            out[target] = refs[which][source].astype(out.dtype)

    return pl.pallas_call(
        kernel,
        out_shape=jax.ShapeDtypeStruct(shape, kind),
        compiler_params=pltpu.CompilerParams(vmem_limit_bytes=40 * 1024 * 1024),
        cost_estimate=about(4),
    )(*inputs)


def about(microseconds):
    return pl.CostEstimate(
        flops=0, bytes_accessed=int(microseconds * 3.6e6), transcendentals=0
    )


def regrouped(value, outer, inner, width):
    rows, total = value.shape
    if width != 64 or outer % 2:
        split = value.reshape(rows, outer, inner, width)
        return jnp.swapaxes(split, 1, 2).reshape(rows, total)

    def kernel(in_ref, out_ref):
        for i in range(inner):
            for o in range(0, outer, 2):
                left = in_ref[:, (o * inner + i) * width : (o * inner + i + 1) * width]
                right = in_ref[:, ((o + 1) * inner + i) * width : ((o + 1) * inner + i + 1) * width]
                at = (i * outer + o) * width
                out_ref[:, at : at + 2 * width] = jnp.concatenate([left, right], axis=1)

    return pl.pallas_call(
        kernel,
        out_shape=jax.ShapeDtypeStruct(value.shape, value.dtype),
        compiler_params=pltpu.CompilerParams(vmem_limit_bytes=40 * 1024 * 1024),
        cost_estimate=about(2),
    )(value)


def dp_gather(value, forward=True):
    if lax.axis_size("dp") != 4:
        return lax.all_gather(value, "dp", axis=0)
    here = lax.axis_index("dp")
    half = value.shape[0] // 2
    one = permuted(value, "dp", 1)
    two = permuted(value, "dp", 2)
    if forward:
        three = jnp.concatenate([permuted(one[:half], "dp", 2), permuted(two[half:], "dp", 1)])
    else:
        three = permuted(value, "dp", 3)
    whole = jnp.zeros((4,) + value.shape, value.dtype)
    for k, piece in enumerate((value, one, two, three)):
        whole = lax.dynamic_update_index_in_dim(whole, piece, here ^ k, 0)
    return whole


def placed_pieces(pieces, here, cuts):
    count, (rows, width) = len(pieces), pieces[0].shape
    spans = list(zip(cuts[:-1], cuts[1:]))

    def kernel(here_ref, *refs):
        for k in range(count):
            owner = here_ref[0] ^ k
            for (low, high), out in zip(spans, refs[count:]):
                out[pl.ds(pl.multiple_of(owner * (high - low), 16), high - low)] = refs[k][low:high]

    return pl.pallas_call(
        kernel,
        out_shape=[
            jax.ShapeDtypeStruct((count * (high - low), width), pieces[0].dtype)
            for low, high in spans
        ],
        in_specs=[pl.BlockSpec(memory_space=pltpu.SMEM)]
        + [pl.BlockSpec(memory_space=pltpu.VMEM)] * count,
        out_specs=[pl.BlockSpec(memory_space=pltpu.VMEM)] * len(spans),
        compiler_params=pltpu.CompilerParams(vmem_limit_bytes=40 * 1024 * 1024),
        cost_estimate=about(2),
    )(here[None], *pieces)


def dp_scatter(total, forward=True, meanwhile=()):
    if lax.axis_size("dp") != 4:
        return lax.psum_scatter(total, "dp", scatter_dimension=0).astype(f32)
    here = lax.axis_index("dp")
    blocks = [lax.dynamic_index_in_dim(total, here ^ k, 0, False) for k in range(4)]
    if not forward:
        own = blocks[0].astype(f32)
        for k in range(1, 4):
            own = own + permuted(blocks[k], "dp", k).astype(f32)
        return own
    half = total.shape[1] // 2
    low, high = [b[:half] for b in blocks], [b[half:] for b in blocks]
    low_in = permuted(jnp.stack([low[1], low[3]]), "dp", 1)
    high_in = permuted(jnp.stack(high[2:]), "dp", 2)
    if meanwhile:
        low_in, high_in = after(low_in, *meanwhile), after(high_in, *meanwhile)
    low_in, high_in = low_in.astype(f32), high_in.astype(f32)
    low_on = (low[2].astype(f32) + low_in[1]).astype(bf16)
    high_on = (high[1].astype(f32) + high_in[1]).astype(bf16)
    low_own = low[0].astype(f32) + low_in[0] + permuted(low_on, "dp", 2).astype(f32)
    high_own = high[0].astype(f32) + high_in[0] + permuted(high_on, "dp", 1).astype(f32)
    return jnp.concatenate([low_own, high_own])


def row_sums(value):
    return other_pairs(value + permuted(value, "seq", 1))


def other_pairs(value):
    total = value
    for by in range(2, lax.axis_size("seq"), 2):
        total = total + permuted(value, "seq", by)
    return total


def segment_of(positions, end_points):
    counted = jnp.sum((end_points[None, :] <= positions[:, None]).astype(jnp.int32), axis=1)
    return jnp.where(positions < 0, -1, counted)


def rope_tables(positions):
    half = ATT_DIM // 2
    freqs = jnp.power(rope_base, -jnp.arange(half, dtype=f32) * (2.0 / ATT_DIM))
    angles = positions.astype(f32)[:, None] * freqs[None, :]
    cosine, sine = jnp.cos(angles), jnp.sin(angles)
    return jnp.concatenate([cosine, cosine], axis=1), jnp.concatenate([sine, sine], axis=1)


def rms_row(values):
    return lax.rsqrt(jnp.mean(values * values, axis=-1, keepdims=True) + epsilon)


def rms_back(grad, values, gain):
    r = rms_row(values)
    scaled = grad * gain
    along = jnp.mean(scaled * values, axis=-1, keepdims=True)
    return scaled * r - values * (r * r * r) * along, jnp.sum(grad * values * r, axis=0)


def dot(left, right):
    return jnp.dot(left, right, preferred_element_type=f32)


def dot_t(left, right):
    return lax.dot_general(left, right, (((1,), (1,)), ((), ())), preferred_element_type=f32)


def cross(left, right):
    return lax.dot_general(left, right, (((0,), (0,)), ((), ())), preferred_element_type=f32)


def halves(columns, pair, lanes):
    left, right = columns[:, 2 * pair : 2 * pair + 1], columns[:, 2 * pair + 1 : 2 * pair + 2]
    return jnp.where(lanes < HEAD_DIM, left, right)


def spread(columns, pairs, lanes):
    return jnp.concatenate([halves(columns, k, lanes) for k in range(pairs)], axis=1)


def counted(pattern, value, dims=(((1,), (0,)), ((), ())), terms=2, first=True):
    pattern = pattern.astype(bf16)
    total, rest = None, value
    for k in range(terms):
        term = rest.astype(bf16)
        pair = (pattern, term) if first else (term, pattern)
        part = lax.dot_general(*pair, dims, preferred_element_type=f32)
        total = part if total is None else total + part
        if k + 1 < terms:
            rest = rest - term.astype(f32)
    return total


def rough(left, right, dims=(((1,), (0,)), ((), ()))):
    return lax.dot_general(
        left.astype(bf16), right.astype(bf16), dims, preferred_element_type=f32
    )


ROWS = (((0,), (0,)), ((), ()))
LAST = (((1,), (1,)), ((), ()))


def block_start(mixed_ref, before_ref, aux_ref, conv_ref, head_ref, ext_ref, width):
    per = mixed_ref.shape[0]
    channels = width + 2 * STATE
    ext_ref[0:8] = before_ref[:, width : width + channels].astype(bf16).astype(f32)
    ext_ref[8 : 8 + per] = mixed_ref[:, width : width + channels].astype(bf16).astype(f32)
    aux = aux_ref[...]
    total = conv_ref[4:5] + ext_ref[8 : 8 + per] * conv_ref[3:4]
    for back in range(1, CONV):
        total = total + ext_ref[8 - back : 8 - back + per] * (
            aux[:, back : back + 1] * conv_ref[3 - back : 4 - back]
        )
    sig = jax.nn.sigmoid(total)
    shifted = mixed_ref[:, width + channels : width + channels + DT_PAD] + head_ref[1:2]
    step = jnp.maximum(shifted, 0.0) + jnp.log1p(jnp.exp(-jnp.abs(shifted)))
    rate = -jnp.exp(head_ref[0:1])
    rows_at = lax.broadcasted_iota(jnp.int32, (per, per), 0)
    cols_at = lax.broadcasted_iota(jnp.int32, (per, per), 1)
    tril = (rows_at >= cols_at).astype(f32)
    cum = counted(tril, step * rate, terms=3)
    return aux, total, sig, shifted, step, rate, tril, cum


def ssd_forward_kernel(
    mixed_ref,
    before_ref,
    aux_ref,
    seg_ref,
    conv_ref,
    head_ref,
    skip_ref,
    y_ref,
    gated_ref,
    enter_ref,
    ext_ref,
    state_ref,
):
    per, width = y_ref.shape
    pairs = width // 128

    @pl.when(pl.program_id(1) == 0)
    def _():
        state_ref[...] = jnp.zeros_like(state_ref)

    aux, total, sig, _, step, _, tril, cum = block_start(
        mixed_ref, before_ref, aux_ref, conv_ref, head_ref, ext_ref, width
    )
    conv = total * sig
    x = conv[:, :width]
    b = conv[:, width : width + STATE].astype(bf16)
    c = conv[:, width + STATE :].astype(bf16)
    lanes = lax.broadcasted_iota(jnp.int32, (per, 128), 1)
    mask = (tril > 0) & (aux[:, 0:1] == seg_ref[0])
    both = rough(c, b, LAST)
    cum_t, step_t = cum.T, step.T
    state = state_ref[...]
    enter_ref[0] = state.astype(bf16)
    carried = rough(c, state)
    grown = jnp.exp(cum) * aux[:, 4:5]
    last = cum[per - 1 : per]
    keep = jnp.exp(last - cum) * aux[:, 5:6] * step
    gate = mixed_ref[:, :width]
    silu_gate = gate * jax.nn.sigmoid(gate)
    scaled = []
    for k in range(pairs):
        at = slice(128 * k, 128 * k + 128)
        x_pair = x[:, at]
        x_low = x_pair.astype(bf16)
        sides = []
        for h in (2 * k, 2 * k + 1):
            gap = jnp.where(mask, cum[:, h : h + 1] - cum_t[h : h + 1], -1e30)
            mixing = both * jnp.exp(gap) * step_t[h : h + 1]
            sides.append(rough(mixing, x_low))
        y = jnp.where(lanes < HEAD_DIM, sides[0], sides[1])
        y = y + carried[:, at] * halves(grown, k, lanes) + skip_ref[:, at] * x_pair
        y_ref[:, at] = y
        gated_ref[:, at] = y * silu_gate[:, at]
        scaled.append(x_pair * halves(keep, k, lanes))
    passed = spread(jnp.exp(last) * aux[0:1, 6:7], pairs, lanes[0:1])
    state_ref[...] = state * passed + rough(b, jnp.concatenate(scaled, axis=1), ROWS)


def ssd_backward_kernel(
    mixed_ref,
    before_ref,
    aux_ref,
    seg_ref,
    conv_ref,
    head_ref,
    skip_ref,
    y_ref,
    enter_ref,
    grad_ref,
    qkv_ref,
    out_ref,
    conv_grad_ref,
    head_grad_ref,
    skip_grad_ref,
    ext_ref,
    next_ref,
    col_ref,
    state_ref,
):
    per, width = y_ref.shape
    pairs = width // 128
    channels = width + 2 * STATE

    @pl.when(pl.program_id(1) == 0)
    def _():
        state_ref[...] = jnp.zeros_like(state_ref)
        next_ref[...] = jnp.zeros_like(next_ref)

    @pl.when((pl.program_id(0) == 0) & (pl.program_id(1) == 0))
    def _():
        conv_grad_ref[...] = jnp.zeros_like(conv_grad_ref)
        head_grad_ref[...] = jnp.zeros_like(head_grad_ref)
        skip_grad_ref[...] = jnp.zeros_like(skip_grad_ref)
        col_ref[...] = jnp.zeros_like(col_ref)

    aux, total, sig, shifted, step, rate, tril, cum = block_start(
        mixed_ref, before_ref, aux_ref, conv_ref, head_ref, ext_ref, width
    )
    conv = total * sig
    x = conv[:, :width]
    b = conv[:, width : width + STATE].astype(bf16)
    c = conv[:, width + STATE :].astype(bf16)
    lanes = lax.broadcasted_iota(jnp.int32, (per, 128), 1)
    mask = (tril > 0) & (aux[:, 0:1] == seg_ref[0])
    both = rough(c, b, LAST)
    cum_t, step_t = cum.T, step.T
    enter = enter_ref[0]
    growth = jnp.exp(cum) * aux[:, 4:5]
    last = cum[per - 1 : per]
    fade = jnp.exp(last - cum) * aux[:, 5:6]
    keep = fade * step
    passed_row = jnp.exp(last) * aux[0:1, 6:7]

    gate = mixed_ref[:, :width]
    gate_sig = jax.nn.sigmoid(gate)
    grad = grad_ref[...]
    dy = grad * gate * gate_sig
    out_ref[:, :width] = (
        grad * y_ref[...] * (gate_sig * (1.0 + gate * (1.0 - gate_sig)))
    ).astype(bf16)

    d_out = state_ref[...]
    wide_growth = spread(growth, pairs, lanes)
    wide_keep = spread(keep, pairs, lanes)
    carried = rough(c, enter)
    dq = dy * wide_growth
    d_c = rough(dq, enter, LAST)
    xk = x * wide_keep
    d_b = rough(xk, d_out, LAST)
    dxk = rough(b, d_out)
    of_head = (
        lax.broadcasted_iota(jnp.int32, (width, 128), 0) // HEAD_DIM
        == lax.broadcasted_iota(jnp.int32, (width, 128), 1)
    ).astype(f32)
    d_growth = counted(of_head, dq * carried, first=False)
    d_keep = counted(of_head, dxk * x, first=False)
    d_passed = jnp.sum(d_out * enter.astype(f32), axis=0, keepdims=True)
    d_passed = counted(of_head, jnp.broadcast_to(d_passed, (16, width)), first=False)[0:1]
    d_x = dxk * wide_keep + dy * skip_ref[...]
    skip_grad_ref[0:1] += jnp.sum(dy * x, axis=0, keepdims=True)
    state_ref[...] = d_out * spread(passed_row, pairs, lanes[0:1]) + rough(c, dq, ROWS)

    d_both = jnp.zeros((per, per), f32)
    row_sums = jnp.zeros((per, 128), f32)
    within = []
    for k in range(pairs):
        at = slice(128 * k, 128 * k + 128)
        x_low = x[:, at].astype(bf16)
        dy_pair = dy[:, at]
        dy_low = dy_pair.astype(bf16)
        sides = []
        for h in (2 * k, 2 * k + 1):
            mine = (lanes >= HEAD_DIM) if h % 2 else (lanes < HEAD_DIM)
            gap = jnp.where(mask, cum[:, h : h + 1] - cum_t[h : h + 1], -1e30)
            level = jnp.exp(gap)
            step_row = step_t[h : h + 1]
            weighted = level * step_row
            sides.append(rough(both * weighted, dy_low, ROWS))
            d_mix = rough(jnp.where(mine, dy_pair, 0.0), x_low, LAST)
            d_both = d_both + d_mix * weighted
            flow = d_mix * both * level
            col_ref[h : h + 1] = jnp.sum(flow, axis=0, keepdims=True)
            row_sum = jnp.sum(flow * step_row, axis=1, keepdims=True)
            row_sums = jnp.where(lanes == h, row_sum, row_sums)
        within.append(jnp.where(lanes < HEAD_DIM, sides[0], sides[1]))
    d_x = d_x + jnp.concatenate(within, axis=1)
    d_c = d_c + rough(d_both, b)
    d_b = d_b + rough(d_both, c, ROWS)
    col_sums = col_ref[...].T
    d_step = col_sums + d_keep * fade
    kept = d_keep * keep
    d_cum = row_sums - col_sums * step + d_growth - kept
    d_last = jnp.sum(kept, axis=0, keepdims=True) + d_passed * passed_row
    at_end = lax.broadcasted_iota(jnp.int32, (per, 128), 0) == per - 1
    d_cum = d_cum + jnp.where(at_end, d_last, 0.0)
    d_decay = counted(tril, d_cum, ROWS)
    d_step = d_step + d_decay * rate
    d_shifted = d_step * jax.nn.sigmoid(shifted)
    head_grad_ref[0:1] += jnp.sum(d_decay * step, axis=0, keepdims=True) * rate
    head_grad_ref[1:2] += jnp.sum(d_shifted, axis=0, keepdims=True)
    out_ref[:, width + channels : width + channels + DT_PAD] = d_shifted.astype(bf16)
    out_ref[:, width + channels + DT_PAD :] = qkv_ref[...]

    d_conv = jnp.concatenate([d_x, d_b, d_c], axis=1)
    d_total = d_conv * (sig * (1.0 + total * (1.0 - sig)))
    conv_grad_ref[4:5] += jnp.sum(d_total, axis=0, keepdims=True)
    conv_grad_ref[3:4] += jnp.sum(d_total * ext_ref[8 : 8 + per], axis=0, keepdims=True)
    for back in range(1, CONV):
        conv_grad_ref[3 - back : 4 - back] += jnp.sum(
            d_total * aux[:, back : back + 1] * ext_ref[8 - back : 8 - back + per],
            axis=0,
            keepdims=True,
        )
    d_in = d_total * conv_ref[3:4]
    for back in range(1, CONV):
        masked = d_total * aux[:, back : back + 1]
        ext_ref[0:per] = masked
        ext_ref[per : per + 8] = next_ref[back - 1]
        d_in = d_in + ext_ref[back : back + per] * conv_ref[3 - back : 4 - back]
        next_ref[back - 1] = masked[0:8]
    out_ref[:, width : width + channels] = d_in.astype(bf16)


def ssd_specs(n, micro, per, width, used, order):
    eighths = per // 8
    return [
        pl.BlockSpec((per, used), lambda m, k: (order(k) * micro + m, 0)),
        pl.BlockSpec(
            (8, used),
            lambda m, k: (
                (jnp.maximum(order(k) - 1, 0) * micro + m) * eighths + eighths - 1,
                0,
            ),
        ),
        pl.BlockSpec((per, 8), lambda m, k: (order(k) * micro + m, 0)),
        pl.BlockSpec((1, 1, per), lambda m, k: (order(k) * micro + m, 0, 0)),
        pl.BlockSpec((8, width + 2 * STATE), lambda m, k: (0, 0)),
        pl.BlockSpec((8, DT_PAD), lambda m, k: (0, 0)),
        pl.BlockSpec((1, width), lambda m, k: (0, 0)),
    ]


def ssd_forward(mixed, aux, seg_rows, conv_rows, head_rows, skip_row, n, micro):
    rows = mixed.shape[0]
    per = rows // (n * micro)
    width = skip_row.shape[1]
    channels = width + 2 * STATE
    used = width + channels + DT_PAD
    specs = ssd_specs(n, micro, per, width, used, lambda k: k)
    by_block = pl.BlockSpec((per, width), lambda m, k: (k * micro + m, 0))
    return pl.pallas_call(
        ssd_forward_kernel,
        grid=(micro, n),
        out_shape=(
            jax.ShapeDtypeStruct((rows, width), f32),
            jax.ShapeDtypeStruct((rows, width), f32),
            jax.ShapeDtypeStruct((n * micro, STATE, width), bf16),
        ),
        in_specs=specs,
        out_specs=(
            by_block,
            by_block,
            pl.BlockSpec((1, STATE, width), lambda m, k: (k * micro + m, 0, 0)),
        ),
        scratch_shapes=[
            pltpu.VMEM((per + 8, channels), f32),
            pltpu.VMEM((STATE, width), f32),
        ],
        compiler_params=pltpu.CompilerParams(vmem_limit_bytes=40 * 1024 * 1024),
        cost_estimate=about(20),
    )(mixed, mixed, aux, seg_rows, conv_rows, head_rows, skip_row)


def ssd_backward(
    mixed, aux, seg_rows, conv_rows, head_rows, skip_row, y, enter, grad, qkv, n, micro
):
    rows = mixed.shape[0]
    per = rows // (n * micro)
    width = skip_row.shape[1]
    channels = width + 2 * STATE
    used = width + channels + DT_PAD

    def order(k):
        return n - 1 - k

    specs = ssd_specs(n, micro, per, width, used, order)
    by_block = pl.BlockSpec((per, width), lambda m, k: (order(k) * micro + m, 0))
    return pl.pallas_call(
        ssd_backward_kernel,
        grid=(micro, n),
        out_shape=(
            jax.ShapeDtypeStruct(mixed.shape, bf16),
            jax.ShapeDtypeStruct((8, channels), f32),
            jax.ShapeDtypeStruct((8, DT_PAD), f32),
            jax.ShapeDtypeStruct((8, width), f32),
        ),
        in_specs=specs
        + [
            by_block,
            pl.BlockSpec((1, STATE, width), lambda m, k: (order(k) * micro + m, 0, 0)),
            by_block,
            pl.BlockSpec((per, qkv.shape[1]), lambda m, k: (order(k) * micro + m, 0)),
        ],
        out_specs=(
            pl.BlockSpec((per, mixed.shape[1]), lambda m, k: (order(k) * micro + m, 0)),
            pl.BlockSpec((8, channels), lambda m, k: (0, 0)),
            pl.BlockSpec((8, DT_PAD), lambda m, k: (0, 0)),
            pl.BlockSpec((8, width), lambda m, k: (0, 0)),
        ),
        scratch_shapes=[
            pltpu.VMEM((per + 8, channels), f32),
            pltpu.VMEM((CONV - 1, 8, channels), f32),
            pltpu.VMEM((128, per), f32),
            pltpu.VMEM((STATE, width), f32),
        ],
        compiler_params=pltpu.CompilerParams(vmem_limit_bytes=40 * 1024 * 1024),
        cost_estimate=about(43),
    )(mixed, mixed, aux, seg_rows, conv_rows, head_rows, skip_row, y, enter, grad, qkv)


def turn(values, cosine, sine):
    half = ATT_DIM // 2
    swapped = jnp.concatenate([-values[:, half:], values[:, :half]], axis=1)
    return values * cosine + swapped * sine


def attention_start(k_ref, v_ref, table_ref, keys_ref, values_ref):
    blocks, per, _ = k_ref.shape
    for b in range(blocks):
        at = slice(b * per, b * per + per)
        keys_ref[at] = turn(k_ref[b], table_ref[b, :, :ATT_DIM], table_ref[b, :, ATT_DIM:]).astype(
            bf16
        )
        values_ref[at] = v_ref[b].astype(bf16)


def attention_probs(q_ref, q_table_ref, q_aux_ref, seg_ref, keys_ref):
    scale = ATT_DIM ** (-0.5)
    table = q_table_ref[0]
    queries = turn(q_ref[0], table[:, :ATT_DIM], table[:, ATT_DIM:]).astype(bf16)
    scores = rough(queries, keys_ref[...], LAST) * scale
    q_aux = q_aux_ref[0]
    positions = lax.broadcasted_iota(jnp.int32, scores.shape, 1)
    seen = (positions <= q_aux[:, 1:2].astype(jnp.int32)) & (q_aux[:, 0:1] == seg_ref[0])
    scores = jnp.where(seen, scores, -1e30)
    raised = jnp.exp(scores - jnp.max(scores, axis=1, keepdims=True))
    return queries, raised / jnp.sum(raised, axis=1, keepdims=True)


def attention_forward_kernel(
    q_ref, k_ref, v_ref, table_ref, q_table_ref, q_aux_ref, seg_ref, out_ref, keys_ref, values_ref
):
    @pl.when(pl.program_id(1) == 0)
    def _():
        attention_start(k_ref, v_ref, table_ref, keys_ref, values_ref)

    _, probs = attention_probs(q_ref, q_table_ref, q_aux_ref, seg_ref, keys_ref)
    out_ref[0] = rough(probs, values_ref[...]).astype(bf16)


def attention_backward_kernel(
    q_ref,
    k_ref,
    v_ref,
    table_ref,
    q_table_ref,
    q_aux_ref,
    seg_ref,
    grad_ref,
    q_grad_ref,
    k_grad_ref,
    v_grad_ref,
    keys_ref,
    values_ref,
    k_sum_ref,
    v_sum_ref,
):
    blocks, per, _ = k_ref.shape

    @pl.when(pl.program_id(1) == 0)
    def _():
        attention_start(k_ref, v_ref, table_ref, keys_ref, values_ref)
        k_sum_ref[...] = jnp.zeros_like(k_sum_ref)
        v_sum_ref[...] = jnp.zeros_like(v_sum_ref)

    scale = ATT_DIM ** (-0.5)
    queries, probs = attention_probs(q_ref, q_table_ref, q_aux_ref, seg_ref, keys_ref)
    grad = grad_ref[0]
    probs_grad = rough(grad, values_ref[...], LAST)
    along = jnp.sum(probs * probs_grad, axis=1, keepdims=True)
    scores_grad = (probs * (probs_grad - along)).astype(bf16)
    table = q_table_ref[0]
    q_grad = rough(scores_grad, keys_ref[...]) * scale
    q_grad_ref[0] = turn(q_grad, table[:, :ATT_DIM], -table[:, ATT_DIM:]).astype(bf16)
    k_sum_ref[...] += rough(scores_grad, queries, ROWS)
    v_sum_ref[...] += rough(probs, grad, ROWS)

    @pl.when(pl.program_id(1) == pl.num_programs(1) - 1)
    def _():
        for b in range(blocks):
            at = slice(b * per, b * per + per)
            k_grad_ref[b] = turn(
                k_sum_ref[at] * scale, table_ref[b, :, :ATT_DIM], -table_ref[b, :, ATT_DIM:]
            ).astype(bf16)
            v_grad_ref[b] = v_sum_ref[at].astype(bf16)


def attention_specs(n, micro, per, q_at, k_at, v_at):
    return [
        pl.BlockSpec((1, per, ATT_DIM), lambda m, k: (k, m, q_at)),
        pl.BlockSpec((n, per, ATT_DIM), lambda m, k: (0, m, k_at)),
        pl.BlockSpec((n, per, ATT_DIM), lambda m, k: (0, m, v_at)),
        pl.BlockSpec((n, per, 2 * ATT_DIM), lambda m, k: (0, 0, 0)),
        pl.BlockSpec((1, per, 2 * ATT_DIM), lambda m, k: (k, 0, 0)),
        pl.BlockSpec((1, per, 8), lambda m, k: (k, m, 0)),
        pl.BlockSpec((1, 1, n * per), lambda m, k: (m, 0, 0)),
    ]


def attention_forward(q, mixed, table, q_table, q_aux, seg, q_at, k_at):
    n, both, _ = mixed.shape
    micro = seg.shape[0]
    per = both // micro
    block = pl.BlockSpec((1, per, ATT_DIM), lambda m, k: (k, m, 0))
    return pl.pallas_call(
        attention_forward_kernel,
        grid=(micro, q_table.shape[0]),
        out_shape=jax.ShapeDtypeStruct((q_table.shape[0], both, ATT_DIM), bf16),
        in_specs=attention_specs(n, micro, per, q_at, k_at, k_at + 1),
        out_specs=block,
        scratch_shapes=[pltpu.VMEM((n * per, ATT_DIM), bf16)] * 2,
        compiler_params=pltpu.CompilerParams(vmem_limit_bytes=40 * 1024 * 1024),
        cost_estimate=about(14),
    )(q, mixed, mixed, table, q_table, q_aux, seg)


def attention_backward(q, mixed, table, q_table, q_aux, seg, grad, q_at, k_at):
    n, both, _ = mixed.shape
    micro = seg.shape[0]
    per = both // micro
    block = pl.BlockSpec((1, per, ATT_DIM), lambda m, k: (k, m, 0))
    whole = pl.BlockSpec((n, per, ATT_DIM), lambda m, k: (0, m, 0))
    return pl.pallas_call(
        attention_backward_kernel,
        grid=(micro, q_table.shape[0]),
        out_shape=(
            jax.ShapeDtypeStruct((q_table.shape[0], both, ATT_DIM), bf16),
            jax.ShapeDtypeStruct((n, both, ATT_DIM), bf16),
            jax.ShapeDtypeStruct((n, both, ATT_DIM), bf16),
        ),
        in_specs=attention_specs(n, micro, per, q_at, k_at, k_at + 1) + [block],
        out_specs=(block, whole, whole),
        scratch_shapes=[pltpu.VMEM((n * per, ATT_DIM), bf16)] * 2
        + [pltpu.VMEM((n * per, ATT_DIM), f32)] * 2,
        compiler_params=pltpu.CompilerParams(vmem_limit_bytes=40 * 1024 * 1024),
        cost_estimate=about(19),
    )(q, mixed, mixed, table, q_table, q_aux, seg, grad)


def ffn_kernel(rows_ref, weight_ref, turned_ref, grad_ref, act_ref, gate_grad_ref, back_ref):
    half = grad_ref.shape[1]
    values = rough(rows_ref[...], weight_ref[...])
    gate, up = values[:, :half], values[:, half:]
    grad = grad_ref[...]
    sig = jax.nn.sigmoid(gate)
    silu = gate * sig
    act_ref[...] = (silu * up).astype(bf16)
    gate_grad_ref[:, :half] = (grad * up * (sig * (1.0 + gate * (1.0 - sig)))).astype(bf16)
    gate_grad_ref[:, half:] = (grad * silu).astype(bf16)
    back_ref[...] = rough(gate_grad_ref[...], turned_ref[...]).astype(bf16)


def ffn_both(rows, weight, turned_weight, act_grad):
    count, depth = rows.shape
    block, wide = 256, weight.shape[1]

    def by_block(columns):
        return pl.BlockSpec((block, columns), lambda k: (k, 0))

    def whole(array):
        return pl.BlockSpec(array.shape, lambda k: (0, 0))

    return pl.pallas_call(
        ffn_kernel,
        grid=(count // block,),
        out_shape=(
            jax.ShapeDtypeStruct((count, wide // 2), bf16),
            jax.ShapeDtypeStruct((count, wide), bf16),
            jax.ShapeDtypeStruct((count, depth), bf16),
        ),
        in_specs=[by_block(depth), whole(weight), whole(turned_weight), by_block(wide // 2)],
        out_specs=(by_block(wide // 2), by_block(wide), by_block(depth)),
        compiler_params=pltpu.CompilerParams(vmem_limit_bytes=48 * 1024 * 1024),
        cost_estimate=about(22),
    )(rows, weight, turned_weight, act_grad)


def local(
    tokens,
    doc_ends,
    input_gain,
    mixer_in,
    conv_weight,
    conv_bias,
    head_params,
    mixer_gain,
    mixer_out,
    attn_qkv,
    attn_out,
    ffn_gain,
    gate_up,
    down_proj,
    out_grad,
):
    n = lax.axis_size("seq")
    nd = lax.axis_size("dp")
    s = lax.axis_index("seq")
    d = lax.axis_index("dp")
    micro, _, per, _ = tokens.shape
    own = micro * per
    length = n * per
    rows = n * own
    owner = mixer_in.shape[0]
    inner = INNER // n
    width = -(-inner // 128) * 128
    heads = HEADS // n
    ffl = FF // n
    parts = n // ATT_HEADS
    group = ATT_HEADS // KV_HEADS
    conv_ch = INNER + 2 * STATE

    def mixed_order(value):
        if value.ndim == 1:
            return jnp.swapaxes(value.reshape(n, nd, owner), 0, 1).reshape(D)
        return regrouped(value, n, nd, owner)

    def plain_order(value):
        if value.ndim == 1:
            return jnp.swapaxes(value.reshape(nd, n, owner), 0, 1).reshape(D)
        return regrouped(value, nd, n, owner)

    def widened(value):
        return jnp.pad(value, [(0, 0)] * (value.ndim - 1) + [(0, width - inner)])

    def from_seq(value):
        return value.reshape(micro, n, per, -1).transpose(1, 0, 2, 3).reshape(rows, -1)

    def gathered(value):
        return lax.all_gather(value, "seq", axis=0, tiled=True)

    def scattered(value, *others):
        total = lax.psum_scatter(value.astype(bf16), "seq", scatter_dimension=0, tiled=True)
        return (after(total, *others) if others else total).astype(f32)

    token_b = mixed_order(tokens.reshape(own, D))
    token_rows = token_b.astype(f32)
    grad_rows = mixed_order(out_grad.reshape(own, D))

    tap_count = conv_weight.shape[1]
    small_own = jnp.concatenate(
        [input_gain, conv_weight.reshape(-1), conv_bias, mixer_gain, ffn_gain]
    )
    small_count = small_own.shape[0]
    small_cols = -(-small_count // owner)
    small_own = jnp.pad(small_own, (0, small_cols * owner - small_count)).reshape(owner, small_cols)

    steps_own = jnp.pad(
        jnp.concatenate(
            [
                mixer_in[:, 2 * INNER + 2 * STATE :].reshape(owner, n, heads).transpose(1, 0, 2),
                jnp.broadcast_to(small_own[None], (n,) + small_own.shape),
            ],
            axis=2,
        ),
        ((0, 0), (0, 0), (0, DT_PAD - heads - small_cols)),
    )
    q_of = [k // parts for k in range(n)]
    kv_of = [ATT_HEADS + q // group for q in q_of]
    sizes = [width, width, 2 * STATE, DT_PAD, ATT_DIM, ATT_DIM, ATT_DIM]
    starts = [sum(sizes[:k]) for k in range(len(sizes) + 1)]
    every = slice(None)
    sent_sizes = [width, width, STATE, DT_PAD, ATT_DIM, ATT_DIM]
    sent_at = [sum(sent_sizes[:k]) for k in range(len(sent_sizes) + 1)]
    moves = []
    for k in range(n):
        odd = k % 2
        for which, source, target, wide in (
            (0, k * inner, sent_at[0], inner),
            (0, INNER + k * inner, sent_at[1], inner),
            (0, 2 * INNER + odd * STATE, sent_at[2], STATE),
            (1, q_of[k] * ATT_DIM, sent_at[4], ATT_DIM),
            (1, (kv_of[k] + odd * KV_HEADS) * ATT_DIM, sent_at[5], ATT_DIM),
        ):
            moves.append(
                (which, (every, slice(source, source + wide)), (k, every, slice(target, target + wide)))
            )
        moves.append((2, (k,), (k, every, slice(sent_at[3], sent_at[4]))))
        if width != inner:
            gap = slice(0, width - inner)
            for target in (sent_at[1], sent_at[2]):
                hole = slice(target - width + inner, target)
                moves.append((3, (every, gap), (k, every, hole)))
    blank = jnp.zeros((owner, 128), bf16)
    packed = assembled(
        (n, owner, sent_at[-1]), bf16, moves, mixer_in, attn_qkv, steps_own, blank
    )
    sent_in = exchanged(packed, "seq")
    positions = jnp.arange(length, dtype=jnp.int32)
    seg = jnp.stack([segment_of(positions, doc_ends[m, 0]) for m in range(micro)])

    blocks = seg.reshape(micro, n, per)
    columns = [seg.astype(f32)]
    for back in range(1, CONV):
        moved = jnp.pad(seg[:, : length - back], ((0, 0), (back, 0)), constant_values=-1)
        columns.append((moved == seg).astype(f32))
    prior = jnp.concatenate(
        [jnp.full((micro, 1), -1, jnp.int32), blocks[:, :-1, per - 1]], axis=1
    )
    last = blocks[:, :, per - 1]
    for flag in (
        blocks == prior[:, :, None],
        blocks == last[:, :, None],
        jnp.broadcast_to((last == prior)[:, :, None], blocks.shape),
        jnp.zeros_like(blocks),
    ):
        columns.append(flag.astype(f32).reshape(micro, length))
    aux = from_seq(jnp.stack(columns, axis=-1))
    seg_blocks = blocks.transpose(1, 0, 2).reshape(n * micro, 1, per).astype(f32)
    cosine, sine = rope_tables(positions)
    table = jnp.concatenate([cosine, sine], axis=1).reshape(n, per, 2 * ATT_DIM)
    part = s % parts

    def taken(value):
        if parts == 1:
            return value
        split = value.reshape(n // parts, parts, *value.shape[1:])
        return lax.dynamic_index_in_dim(split, part, 1, False)

    def put_back(value):
        if parts == 1:
            return value
        here = (jnp.arange(parts) == part).reshape(1, parts, 1, 1)
        return jnp.where(here, value[:, None], 0).reshape(n, *value.shape[1:])

    q_aux = jnp.stack(
        [seg.astype(f32), jnp.broadcast_to(positions.astype(f32), seg.shape)], axis=-1
    )
    q_aux = jnp.pad(from_seq(q_aux), ((0, 0), (0, 6))).reshape(n, own, 8)
    q_aux, q_table = taken(q_aux), taken(table)
    w_half = dp_gather(sent_in)
    small = w_half[:, :, :, sent_at[3] + heads : sent_at[3] + heads + small_cols]
    small = jnp.swapaxes(small, 0, 1).reshape(n * nd, -1)[:, :small_count]
    w_half = w_half.reshape(D, sent_at[-1])
    w_cut = [w_half[:, sent_at[k] : sent_at[k + 1]] for k in range(6)]
    own_side = jnp.concatenate([w_cut[2], w_cut[5]], axis=1)
    other_side = permuted(own_side, "seq", 1)
    odd_place = (s & 1) != 0
    first_side = jnp.where(odd_place, other_side, own_side)
    second_side = jnp.where(odd_place, own_side, other_side)
    w_in = jnp.concatenate(
        [
            w_cut[0],
            w_cut[1],
            first_side[:, :STATE],
            second_side[:, :STATE],
            w_cut[3],
            w_cut[4],
            first_side[:, STATE:],
            second_side[:, STATE:],
        ],
        axis=1,
    )
    w_in = after(w_in, aux, seg_blocks, table, q_aux)
    gu_moves = []
    for k in range(n):
        for half in range(2):
            gu_moves.append(
                (
                    (every, slice(half * FF + k * ffl, half * FF + (k + 1) * ffl)),
                    (k, every, slice(half * ffl, (half + 1) * ffl)),
                )
            )
    gu_own = assembled(
        (n, owner, 2 * ffl), bf16, [(0, flat, cube) for flat, cube in gu_moves], gate_up
    )
    sent_gu = exchanged(after(gu_own, w_in), "seq")
    cuts = [owner, CONV * tap_count, tap_count, mixer_gain.shape[0], owner]
    at = [sum(cuts[:k]) for k in range(len(cuts) + 1)]
    small = small.astype(f32)
    gain_in = mixed_order(small[:, at[0] : at[1]].reshape(-1))
    taps = (
        small[:, at[1] : at[2]].reshape(-1, CONV, tap_count).transpose(1, 0, 2).reshape(CONV, -1)
    )
    shift = small[:, at[2] : at[3]].reshape(-1)
    gain_mix = widened(
        lax.dynamic_slice_in_dim(small[:, at[3] : at[4]].reshape(-1), s * inner, inner)
    )
    gain_ffn = mixed_order(small[:, at[4] : at[5]].reshape(-1))
    conv_rows = jnp.concatenate([taps, shift[None], jnp.zeros((3, conv_ch), f32)])
    conv_rows = jnp.concatenate(
        [
            widened(lax.dynamic_slice_in_dim(conv_rows, s * inner, inner, axis=1)),
            conv_rows[:, INNER:],
        ],
        axis=1,
    )
    head = lax.dynamic_slice_in_dim(head_params, s * heads, heads, axis=1)
    head_rows = jnp.pad(head, ((0, 5), (0, DT_PAD - heads)))
    skip_row = widened(jnp.repeat(head[2], HEAD_DIM)[None])

    token_all = gathered(after(token_b, sent_in))
    token_f32 = token_all.astype(f32)
    normed = (token_f32 * rms_row(token_f32) * gain_in).astype(bf16)
    grads = gathered(after(grad_rows, token_all, w_in))
    mixed = dot(normed, w_in)
    out_own = after(mixed_order(jnp.concatenate([mixer_out, attn_out])), w_in)
    out_cut = mixer_out.shape[0]
    if nd == 4 and out_cut % 16 == 0:
        pieces = [after(permuted(out_own, "dp", k), mixed) for k in range(1, nd)]
        w_mix, w_att = placed_pieces([out_own, *pieces], d, [0, out_cut, out_own.shape[0]])
    else:
        out_parts = dp_gather(out_own, forward=False)
        w_mix = out_parts[:, :out_cut].reshape(-1, D)
        w_att = out_parts[:, out_cut:].reshape(-1, D)
    w_mix = jnp.pad(w_mix, ((0, width - inner), (0, 0)))
    if parts > 1:
        other = permuted(w_att, "seq", 1)
        w_att = jnp.where(
            (s & 1) != 0, jnp.concatenate([other, w_att]), jnp.concatenate([w_att, other])
        )
    w_gu = dp_gather(after(sent_gu, mixed), forward=False).reshape(D, 2 * ffl)
    w_down = dp_gather(after(mixed_order(down_proj), mixed), forward=False).reshape(ffl, D)
    ssd_args = (mixed, aux, seg_blocks, conv_rows, head_rows, skip_row)
    y, gated, enter = ssd_forward(*ssd_args, n, micro)
    squares = row_sums(jnp.sum(gated * gated, axis=1)) / INNER
    r_mix = lax.rsqrt(squares + epsilon)[:, None]
    mixer_b = (gated * r_mix * gain_mix).astype(bf16)

    q_at = starts[4] // ATT_DIM
    mixed_blocks = mixed.reshape(n, own, starts[-1])
    queries, own_q_at = mixed_blocks, q_at
    if parts > 1:
        queries, own_q_at = taken(mixed_blocks[:, :, starts[4] : starts[5]]), 0
    q_aux = after(q_aux, sent_gu, gated)
    att_args = (queries, mixed_blocks, table, q_table, q_aux)
    att_args = att_args + (seg.astype(f32)[:, None],)
    attended_b = put_back(attention_forward(*att_args, own_q_at, q_at + 1)).reshape(rows, ATT_DIM)
    branch_b = jnp.concatenate([mixer_b, attended_b], axis=1)
    w_out = jnp.concatenate([w_mix, w_att])
    branches = dot(branch_b, w_out)
    branches = after(branches.astype(bf16), grads)
    hidden = token_rows + scattered(branches, w_gu, w_down)
    ffn_own = (hidden * rms_row(hidden) * gain_ffn).astype(bf16)
    ffn_in = gathered(ffn_own)

    act_grad = after(dot_t(grads, w_down), branches)
    turned_gu = after(w_gu.T, branches)
    activated_b, gate_grad, ffn_back = ffn_both(ffn_in, w_gu, turned_gu, act_grad)
    gu_total = cross(ffn_in, gate_grad).astype(bf16)
    down_total = cross(activated_b, grads).astype(bf16)
    ffn_in_grad = scattered(ffn_back, gu_total, down_total)

    def over_dp(total, forward, meanwhile=()):
        return dp_scatter(total.reshape(nd, n * owner, -1), forward, meanwhile).astype(bf16)

    def to_owners(part_sum):
        return exchanged(part_sum.reshape(n, owner, -1), "seq")

    gu_part = over_dp(gu_total, False)
    down_grad = dp_scatter(down_total.reshape(nd, -1, D), False)
    hidden_part, ffn_gain_grad = rms_back(ffn_in_grad, hidden, gain_ffn)
    hidden_grad = hidden_part + grad_rows.astype(f32)
    hidden_b = after(gathered(hidden_grad.astype(bf16)), gu_part, down_grad)
    gu_sum = to_owners(gu_part)

    ffn_out = after(dot(activated_b, w_down).astype(bf16), hidden_b)
    ffn_sum = lax.psum_scatter(ffn_out, "seq", scatter_dimension=0, tiled=True)
    layer_out = plain_order((hidden + ffn_sum.astype(f32)).astype(bf16))

    branch_total = cross(branch_b, hidden_b).astype(bf16)
    mix_total, att_total = branch_total[:width], branch_total[width:]
    if parts > 1:
        half = att_total.shape[0] // 2
        low, high = att_total[:half], att_total[half:]
        odd = (s & 1) != 0
        other = permuted(jnp.where(odd, low, high), "seq", 1)
        att_total = (jnp.where(odd, high, low).astype(f32) + other.astype(f32)).astype(bf16)
    out_total = jnp.concatenate(
        [mix_total[:inner].reshape(nd, -1, D), att_total.reshape(nd, -1, D)], axis=1
    )
    if nd == 4:
        out_blocks = [lax.dynamic_index_in_dim(out_total, d ^ k, 0, False) for k in range(nd)]
        out_pieces = [permuted(out_blocks[k], "dp", k) for k in range(1, nd)]
        out_sum = out_blocks[0].astype(f32)
        for piece in out_pieces:
            out_sum = out_sum + piece.astype(f32)
    else:
        out_sum = dp_scatter(out_total, False)
        out_pieces = [out_sum]

    branch_grad = dot_t(hidden_b, w_out)
    mix_grad = branch_grad[:, :width]
    scaled = mix_grad * gain_mix
    along = jnp.sum(scaled * gated, axis=1)
    along = along + permuted(along, "seq", 1)
    att_grad = taken(branch_grad[:, width:].astype(bf16).reshape(n, own, ATT_DIM))
    att_grad = after(att_grad, along)
    q_grad, k_grad, v_grad = attention_backward(*att_args, att_grad, own_q_at, q_at + 1)
    qkv_grad = jnp.concatenate([put_back(q_grad), k_grad, v_grad], axis=2).reshape(rows, -1)

    along = other_pairs(along)[:, None] / INNER
    mix_gain_grad = jnp.sum(mix_grad * gated * r_mix, axis=0)
    gated_grad = scaled * r_mix - gated * (r_mix * r_mix * r_mix) * along
    mixed_grad, conv_g, head_g, skip_g = ssd_backward(
        *ssd_args, y, enter, gated_grad, qkv_grad, n, micro
    )
    mixed_grad = after(mixed_grad, gu_sum, *out_pieces)

    def placed(value, full):
        whole = jnp.zeros(value.shape[:-1] + (full,), f32)
        return lax.dynamic_update_slice_in_dim(
            whole, value, s * value.shape[-1], axis=value.ndim - 1
        )

    def by_owner(value):
        return value.reshape(-1, n * nd, value.shape[-1] // (n * nd)).transpose(1, 0, 2)

    conv_full = jnp.concatenate(
        [placed(conv_g[: CONV + 1, :inner], INNER), conv_g[: CONV + 1, width:]], axis=1
    )
    vectors = [
        by_owner(conv_full),
        by_owner(placed(mix_gain_grad[:inner], INNER)[None]),
        by_owner(plain_order(ffn_gain_grad)[None]),
    ]
    vectors = jnp.concatenate([v.reshape(n * nd, -1) for v in vectors], axis=1)
    vector_count = vectors.shape[1]
    vector_cols = -(-vector_count // owner)
    vectors = jnp.pad(vectors, ((0, 0), (0, vector_cols * owner - vector_count)))
    vectors = vectors.reshape(n, nd, owner, vector_cols).transpose(1, 0, 2, 3)
    vectors = vectors.reshape(D, vector_cols)

    in_back = after(dot_t(mixed_grad, w_in).astype(bf16), ffn_sum)
    mixed_grad = after(mixed_grad, in_back)
    zx_total = cross(normed, mixed_grad[:, : starts[2]]).astype(bf16)
    at_steps, at_heads = starts[3] - starts[2], starts[4] - starts[2]
    spare = starts[-1] - starts[2] - at_steps - heads - vector_cols
    rest_total = cross(normed, mixed_grad[:, starts[2] :])
    rest_total = (
        rest_total + jnp.pad(vectors, ((0, 0), (at_steps + heads, spare)))
    ).astype(bf16)
    zx_part = over_dp(zx_total, True, (rest_total,))
    zx_sum = to_owners(zx_part)
    rest_part = over_dp(rest_total, True, (zx_total,))
    at_kv = at_heads + ATT_DIM
    first_part = jnp.concatenate(
        [rest_part[:, :STATE], rest_part[:, at_kv : at_kv + ATT_DIM]], axis=1
    )
    second_part = jnp.concatenate(
        [rest_part[:, STATE:at_steps], rest_part[:, at_kv + ATT_DIM :]], axis=1
    )
    side = jnp.where(odd_place, second_part, first_part).astype(f32) + permuted(
        jnp.where(odd_place, first_part, second_part), "seq", 1
    ).astype(f32)
    rest_sum = to_owners(
        jnp.concatenate([side.astype(bf16), rest_part[:, at_steps:at_kv]], axis=1)
    )
    gu_sum, down_grad = after(gu_sum, rest_total), after(down_grad, rest_total)
    gate_up_grad = assembled(
        (owner, 2 * FF), f32, [(0, cube, flat) for flat, cube in gu_moves], gu_sum
    )
    out_plain = plain_order(out_sum)
    mixer_out_grad = out_plain[: mixer_out.shape[0]]
    attn_out_grad = out_plain[mixer_out.shape[0] :]
    down_grad = plain_order(down_grad)
    normed_sum = lax.psum_scatter(in_back, "seq", scatter_dimension=0, tiled=True)
    normed_sum = after(
        normed_sum, gate_up_grad, mixer_out_grad, attn_out_grad, down_grad, layer_out
    )
    normed_grad = normed_sum.astype(f32)
    head_g = jnp.concatenate(
        [head_g[:2, :heads], skip_g[:1, :inner].reshape(1, heads, HEAD_DIM).sum(axis=2)]
    )
    head_g = after(placed(head_g, HEADS).reshape(-1), normed_sum)
    head_g = summed(head_g, ("dp",))
    head_g = head_g + permuted(head_g, "seq", 1)
    others = [head_g] + [permuted(head_g, "seq", by) for by in range(2, n, 2)]
    head_g = jnp.sum(jnp.stack(others)[jnp.arange(n // 2) ^ (s // 2)], axis=0)
    token_part, _ = rms_back(normed_grad, token_rows, gain_in)
    token_grad = plain_order(token_part + hidden_grad)
    zx_sum = after(zx_sum, token_grad, head_g)

    at_own = STATE + ATT_DIM
    halves = rest_sum[:, :, :STATE].astype(f32).reshape(n // 2, 2, owner, STATE).sum(axis=0)
    bc_sum = jnp.concatenate([halves[0], halves[1]], axis=1)
    step_sum = rest_sum[:, :, at_own : at_own + heads].transpose(1, 0, 2).reshape(owner, HEADS)
    moves = []
    for k in range(n):
        for half in range(2):
            source = slice(half * width, half * width + inner)
            target = slice(half * INNER + k * inner, half * INNER + (k + 1) * inner)
            moves.append((0, (k, every, source), (every, target)))
    moves.append((1, (every, every), (every, slice(2 * INNER, 2 * INNER + 2 * STATE))))
    moves.append((2, (every, every), (every, slice(2 * INNER + 2 * STATE, PROJ))))
    mixer_in_grad = assembled((owner, PROJ), f32, moves, zx_sum, bc_sum, step_sum)
    q_sum = rest_sum[:, :, at_own + DT_PAD :].astype(f32)
    q_sum = q_sum.reshape(ATT_HEADS, parts, owner, ATT_DIM).sum(axis=1)
    kv_sum = rest_sum[:, :, STATE:at_own].astype(f32)
    kv_sum = kv_sum.reshape(KV_HEADS, n // (2 * KV_HEADS), 2, owner, ATT_DIM).sum(axis=1)
    k_sum, v_sum = kv_sum[:, 0], kv_sum[:, 1]
    attn_qkv_grad = (
        jnp.concatenate([q_sum, k_sum, v_sum]).transpose(1, 0, 2).reshape(owner, -1)
    )

    vectors = jnp.sum(
        rest_sum[:, :, at_own + heads : at_own + heads + vector_cols].astype(f32), axis=0
    ).reshape(-1)[:vector_count]
    ends = [(CONV + 1) * tap_count, (CONV + 1) * tap_count + mixer_gain.shape[0]]
    conv_own = vectors[: ends[0]].reshape(CONV + 1, tap_count)
    in_gain_grad = (
        jnp.sum(mixer_in.astype(f32) * mixer_in_grad, axis=1)
        + jnp.sum(attn_qkv.astype(f32) * attn_qkv_grad, axis=1)
    ) / input_gain.astype(f32)
    return (
        layer_out.reshape(micro, 1, per, D),
        token_grad.reshape(micro, 1, per, D),
        in_gain_grad,
        mixer_in_grad,
        conv_own[:CONV],
        conv_own[CONV],
        head_g.reshape(3, HEADS),
        vectors[ends[0] : ends[1]],
        mixer_out_grad,
        attn_qkv_grad,
        attn_out_grad,
        vectors[ends[1] :],
        gate_up_grad,
        down_grad,
    )


def solution(mesh):
    rows = P(("seq", "dp"), None)
    vector = P(("seq", "dp"))
    activations = P(None, "dp", "seq", None)
    return jax.shard_map(
        local,
        mesh=mesh,
        in_specs=(
            activations,
            P(None, "dp", None),
            vector,
            rows,
            P(None, ("seq", "dp")),
            vector,
            P(),
            vector,
            rows,
            rows,
            rows,
            vector,
            rows,
            rows,
            activations,
        ),
        out_specs=(
            activations,
            activations,
            vector,
            rows,
            P(None, ("seq", "dp")),
            vector,
            P(),
            vector,
            rows,
            rows,
            rows,
            vector,
            rows,
            rows,
        ),
        check_vma=False,
    )
```
